32 devices in a mesh: loop: 4 (over y, x), trans: 8 (over z, core).
Axes of the slice: x: 2, y: 2, z: 4, core: 2. Of those that a mesh axis runs over, the one named last changes fastest.
Arguments:
- block_now: float32 [8, 3, 64, 4, 1024], P(None, None, None, 'loop', 'trans')
- block_prev: float32 [8, 3, 64, 4, 1024], P(None, None, None, 'loop', 'trans'), may hold values from -6 to 6
- coupling_prev: float32 [8, 8], replicated, may hold values from -3 to 3
- material: int32 [64, 4, 1024], P(None, 'loop', 'trans'), may hold values from 0 to 3
- permittivity: float32 [4], replicated, may hold values from 1 to 12
Outputs:
- block_next: float32 [8, 3, 64, 4, 1024], P(None, None, None, 'loop', 'trans')
- alpha_block: float32 [8, 8], replicated
- beta_block: float32 [8, 8], replicated
The draws below stay inside these ranges and needn't reach their ends.
All inputs are finite; a program needn't handle non-finite values.
Results may differ from the reference program's by a relative error of at most 0.0003.
Values sent between devices are 32-bit elements; how exact they have to be, the bound alone decides.
No kernel may reach another device: no remote copies, remote signals or barrier semaphores. Data moves between devices by JAX's collectives and lax.ppermute only.
A program may use at most 64 MiB of HBM per device.

```python
import math
import jax
import jax.numpy as jnp
from jax import lax

BLOCK = 8
LEVELS = 4
NZ = 64
NP = 4
NT = 1024


def draw_block_now(key, part):
    shape = (BLOCK, 3, NZ, NP, NT)
    trans_pos = jnp.arange(NT, dtype=jnp.float32)
    ramp = 1.0 + 2.0 * trans_pos / max(NT - 1, 1)
    base = jax.random.truncated_normal(key, -5.0, 5.0, shape, jnp.float32)
    return (base * ramp).astype(jnp.float32)


def touch_ends(result, key, least, high):
    spot = [jax.random.randint(jax.random.fold_in(key, axis), (), 0, length) for axis, length in enumerate(result.shape)]
    widest = result.shape.index(max(result.shape))
    next_to = spot[:widest] + [(spot[widest] + 1) % result.shape[widest]] + spot[widest + 1:]
    return result.at[tuple(spot)].set(least).at[tuple(next_to)].set(high)


def shard_levels(rng, extent, shards, low, top_value):
    def one(position, shards_of):
        steps = jax.random.uniform(jax.random.fold_in(jax.random.fold_in(rng, 6), position), (shards_of,), jnp.float32, low / len(shards), top_value / len(shards))
        return jnp.repeat(jnp.exp(steps), extent[position] // shards_of).reshape((-1,) + (1,) * (len(extent) - position - 1))

    factor_of = one(*shards[0])
    for cut in shards[1:]:
        factor_of = factor_of * one(*cut)
    return factor_of


def bell_draw(stream_key, extent, width, most, split=(), held_as=jnp.bfloat16):
    values = jax.random.normal(stream_key, extent, jnp.float32) * width
    if len(split) > 0:
        values = shard_levels(stream_key, extent, split, -0.22, 0.18) * values
    return jnp.clip(values, min=-most, max=most).astype(held_as)


def setup_inputs(seed: int = 0) -> dict:
    streams_of = jax.random.split(jax.random.key(seed), 6)
    block_now = draw_block_now(jax.random.fold_in(streams_of[5], 71), 0)
    block_prev = bell_draw(streams_of[1], (BLOCK, 3, NZ, NP, NT), 1.0, 6.0, ((3, 4), (4, 8)), jnp.float32)
    coupling_prev = bell_draw(streams_of[2], (BLOCK, BLOCK), 0.5, 3.0, (), jnp.float32)
    material = touch_ends(jax.random.randint(streams_of[3], (NZ, NP, NT), 0, LEVELS), jax.random.fold_in(streams_of[3], 1), 0, LEVELS - 1).astype(jnp.int32)
    permittivity = jnp.clip(jnp.exp(jax.random.uniform(streams_of[4], (LEVELS,), jnp.float32, math.log(1.0), math.log(12.0))), 1.0, 12.0)
    return {"block_now": block_now, "block_prev": block_prev, "coupling_prev": coupling_prev, "material": material, "permittivity": permittivity}


def cell_scale(material, permittivity):
    levels = jnp.arange(permittivity.shape[0], dtype=jnp.int32)
    inverse = 1.0 / jnp.sqrt(permittivity)
    match = (material[None] == levels[:, None, None, None]).astype(permittivity.dtype)
    return lax.optimization_barrier(jnp.sum(match * inverse[:, None, None, None], axis=0))

def cut_axis(field, axis, start, stop):
    return lax.slice_in_dim(field, start, field.shape[axis] + stop, axis=axis)

def ahead(field, axis):
    diff = cut_axis(field, axis, 1, 0) - cut_axis(field, axis, 0, -1)
    for other in (1, 2, 3):
        if other != axis:
            diff = cut_axis(diff, other, 0, -1)
    return diff

def behind(field, axis):
    diff = cut_axis(field, axis, 1, 0) - cut_axis(field, axis, 0, -1)
    for other in (1, 2, 3):
        if other != axis:
            diff = cut_axis(diff, other, 1, 0)
    return diff

def curl_ahead(field):
    comp_z, comp_p, comp_t = (field[:, 0], field[:, 1], field[:, 2])
    out_z = ahead(comp_t, 2) - ahead(comp_p, 3)
    out_p = ahead(comp_z, 3) - ahead(comp_t, 1)
    out_t = ahead(comp_p, 1) - ahead(comp_z, 2)
    return jnp.stack([out_z, out_p, out_t], axis=1)

def curl_behind(field):
    comp_z, comp_p, comp_t = (field[:, 0], field[:, 1], field[:, 2])
    out_z = behind(comp_t, 2) - behind(comp_p, 3)
    out_p = behind(comp_z, 3) - behind(comp_t, 1)
    out_t = behind(comp_p, 1) - behind(comp_z, 2)
    return jnp.stack([out_z, out_p, out_t], axis=1)

def reference(block_now, block_prev, coupling_prev, material, permittivity):
    hp = lax.Precision.HIGHEST
    scale = cell_scale(material, permittivity)

    def apply_one(vector):
        field = (vector * scale[None])[None]
        padded = jnp.pad(field, ((0, 0), (0, 0), (1, 1), (0, 0), (1, 1)))
        padded = jnp.concatenate([padded[:, :, :, -1:], padded, padded[:, :, :, :1]], axis=3)
        curl_h = curl_ahead(padded)
        return (curl_behind(curl_h) * scale[None, None])[0]
    image = lax.map(apply_one, block_now)
    work = image - jnp.einsum('kcxyz,bk->bcxyz', block_prev, coupling_prev, precision=hp)
    count = 3.0 * block_now.shape[2] * block_now.shape[3] * block_now.shape[4]
    alpha_block = jnp.einsum('jcxyz,bcxyz->jb', block_now, work, precision=hp) / count
    resid = work - jnp.einsum('jcxyz,jb->bcxyz', block_now, alpha_block, precision=hp)
    gram = jnp.einsum('jcxyz,bcxyz->jb', resid, resid, precision=hp) / count
    lower = jnp.linalg.cholesky(gram)
    eye = jnp.eye(lower.shape[0], dtype=lower.dtype)
    lower_inv = jax.scipy.linalg.solve_triangular(lower, eye, lower=True)
    block_next = jnp.einsum('jcxyz,bj->bcxyz', resid, lower_inv, precision=hp)
    return (block_next, alpha_block, lower.T)
```

```python
import jax
import jax.numpy as jnp
from jax import lax
from jax.experimental import pallas as pl
from jax.experimental.pallas import tpu as pltpu
from jax.sharding import PartitionSpec as P

VM = pltpu.VMEM
SM = pltpu.SMEM


def lane_ids(shape):
    return lax.broadcasted_iota(jnp.int32, shape, len(shape) - 1)


def row_ids(shape):
    return lax.broadcasted_iota(jnp.int32, shape, len(shape) - 2)


def roll_by(x, shift, axis):
    return pltpu.roll(x, shift % x.shape[axis], axis)


def cell_scale(mat, eps_ref):
    eps = jnp.full(mat.shape, eps_ref[0], jnp.float32)
    for level in range(1, eps_ref.shape[0]):
        eps = jnp.where(mat == level, eps_ref[level], eps)
    return 1.0 / jnp.sqrt(eps)


def z_next(x):
    n = x.shape[0]
    return jnp.where(row_ids(x.shape) == n - 1, 0.0, roll_by(x, -1, 0))


def z_prev(x):
    return jnp.where(row_ids(x.shape) == 0, 0.0, roll_by(x, 1, 0))


def pack_kernel(eps_ref, v_ref, mat_ref, fwd_ref, bwd_ref, right_ref, left_ref, scale_ref):
    nb = v_ref.shape[0]
    scale = cell_scale(mat_ref[...], eps_ref)
    scale_ref[...] = scale
    lane = lane_ids(scale.shape)
    last = scale.shape[1] - 1
    right = jnp.zeros_like(scale)
    left = jnp.zeros_like(scale)
    for b in range(nb):
        uz = v_ref[b, 0] * scale
        up = v_ref[b, 1] * scale
        ut = v_ref[b, 2] * scale
        bwd_ref[b, 0] = uz
        bwd_ref[b, 1] = ut
        fwd_ref[b, 0] = uz + (z_next(up) - up)
        fwd_ref[b, 1] = ut + (jnp.where(lane == last, 0.0, roll_by(up, -1, 1)) - up)
        for c, u in enumerate((uz, up, ut)):
            spot = 3 * b + c
            right = jnp.where(lane == spot, roll_by(u, spot + 1, 1), right)
            left = jnp.where(lane == spot, roll_by(u, spot, 1), left)
    right_ref[...] = right
    left_ref[...] = left


def gram_sums(v_ref, w_ref, acc_ref, pairs, base, group):
    steps = v_ref.shape[1] // 8
    for first in range(0, len(pairs), group):
        part = pairs[first : first + group]

        def body(r, accs):
            rows = pl.ds(pl.multiple_of(r * 8, 8), 8)
            vs = {j: v_ref[j, rows, :] for j in sorted({p[0] for p in part})}
            ws = {b: w_ref[b, rows, :] for b in sorted({p[1] for p in part})}
            return tuple(acc + vs[j] * ws[b] for acc, (j, b) in zip(accs, part))

        zero = jnp.zeros((8, v_ref.shape[2]), jnp.float32)
        accs = lax.fori_loop(0, steps, body, tuple(zero for _ in part))
        for i, acc in enumerate(accs):
            acc_ref[base + first + i] = acc


def local_kernel(eps_ref, coup_ref, v_ref, scale_ref, q_ref, fr_ref, fl_ref, cr_ref, cl_ref, l_ref, acc_ref):
    nb = v_ref.shape[0]
    nz = scale_ref.shape[0]

    def body(b, carry):
        scale = scale_ref[...]
        lane = lane_ids(scale.shape)
        last = scale.shape[1] - 1
        uz = v_ref[b, pl.ds(0, nz), :] * scale
        up = v_ref[b, pl.ds(nz, nz), :] * scale
        ut = v_ref[b, pl.ds(2 * nz, nz), :] * scale

        def at_first(edge, c):
            return pltpu.roll(edge[...], (edge.shape[1] - (3 * b + c)) % edge.shape[1], 1)

        def at_last(edge, c):
            return pltpu.roll(edge[...], edge.shape[1] - 1 - (3 * b + c), 1)

        def prev(u, c):
            return jnp.where(lane == 0, at_first(fr_ref, c), roll_by(u, 1, 1))

        def nxt(u, c):
            return jnp.where(lane == last, at_last(fl_ref, c), roll_by(u, -1, 1))

        dt_ut = ut - prev(ut, 2)
        up_next = nxt(up, 1)
        uz_next = nxt(uz, 0)
        im_z = (z_next(up) - up) + (z_next(dt_ut) - dt_ut) + 4.0 * uz - uz_next - prev(uz, 0)
        corner_r = jnp.where(lane == 0, at_first(cr_ref, 2), 0.0)
        im_p = (
            4.0 * up - z_next(up) - z_prev(up) - up_next - prev(up, 1)
            - (uz - z_prev(uz)) - dt_ut - corner_r
        )
        corner_l = jnp.where(lane == last, at_last(cl_ref, 1), 0.0)
        im_t = (
            (uz_next - z_prev(uz_next)) - (uz - z_prev(uz)) + (up_next - up)
            + 4.0 * ut - z_next(ut) - z_prev(ut) - corner_l
        )
        for c, im in enumerate((im_z, im_p, im_t)):
            rows = pl.ds(c * nz, nz)
            out = im * scale
            for k in range(nb):
                out = out - coup_ref[b, k] * q_ref[k, rows, :]
            l_ref[b, rows, :] = out
        return carry

    lax.fori_loop(0, nb, body, 0)
    pairs = [(j, b) for b in range(nb) for j in range(nb) if j <= b]
    gram_sums(v_ref, v_ref, acc_ref, pairs, 0, 36)


def sum_kernel(v_ref, scale_ref, l_ref, acc0_ref, fwd_ref, bwd_ref, w_ref, pay_ref, acc_ref):
    nb = v_ref.shape[0]
    nz = scale_ref.shape[0]

    def body(b, carry):
        scale = scale_ref[...]
        lane = lane_ids(scale.shape)
        za = fwd_ref[b, 0]
        tb = fwd_ref[b, 1]
        uz = bwd_ref[b, 0]
        ut = bwd_ref[b, 1]
        up_prev = jnp.where(lane == 0, 0.0, roll_by(ut, 1, 1))
        w_ref[b, pl.ds(0, nz), :] = l_ref[b, pl.ds(0, nz), :] - scale * (za + uz)
        div = (uz - z_prev(uz)) + (ut - up_prev)
        w_ref[b, pl.ds(nz, nz), :] = l_ref[b, pl.ds(nz, nz), :] + scale * div
        w_ref[b, pl.ds(2 * nz, nz), :] = l_ref[b, pl.ds(2 * nz, nz), :] - scale * (tb + ut)
        return carry

    lax.fori_loop(0, nb, body, 0)
    full = [(j, b) for half in (0, 1) for b in range(nb) for j in range(half * nb // 2, (half + 1) * nb // 2)]
    tri = [(j, b) for b in range(nb) for j in range(nb) if j <= b]
    gram_sums(v_ref, w_ref, acc_ref, full, 0, nb * nb // 2)
    gram_sums(w_ref, w_ref, acc_ref, tri, len(full), len(tri))
    lane = lane_ids((8, v_ref.shape[2]))
    row = row_ids((8, v_ref.shape[2]))
    place = {}
    for i, (j, b) in enumerate(full):
        place.setdefault(("new", i), []).extend([(j, b), (b, 3 * nb + j)])
    for i, (j, b) in enumerate(tri):
        place.setdefault(("new", len(full) + i), []).extend({(j, nb + b), (b, nb + j)})
        place.setdefault(("old", i), []).extend({(j, 2 * nb + b), (b, 2 * nb + j)})
    pay = jnp.zeros((8, v_ref.shape[2]), jnp.float32)
    for (which, i), spots in place.items():
        acc = acc_ref[i] if which == "new" else acc0_ref[i]
        total = jnp.sum(jnp.sum(acc, axis=0, keepdims=True), axis=1, keepdims=True)
        hit = (row == spots[0][0]) & (lane == spots[0][1])
        for spot in spots[1:]:
            hit = hit | ((row == spot[0]) & (lane == spot[1]))
        pay = jnp.where(hit, total, pay)
    pay_ref[...] = pay


def lane_at(x, k):
    return jnp.broadcast_to(x[:, k : k + 1], x.shape)


def row_at(x, k):
    return jnp.broadcast_to(x[k : k + 1, :], x.shape)


def last_kernel(count, pay_ref, v_ref, w_ref, out_ref, alpha_ref, beta_ref, coef_ref):
    nb = v_ref.shape[0]
    pay = pay_ref[...]
    lane = lane_ids(pay.shape)
    row = row_ids(pay.shape)
    proj = pay
    alpha = proj / count
    alpha_t = roll_by(pay, -3 * nb, 1) / count
    ww = roll_by(pay, -nb, 1)
    vv = roll_by(pay, -2 * nb, 1)
    cross = jnp.zeros_like(pay)
    half = jnp.zeros_like(pay)
    for j in range(nb):
        cross = cross + lane_at(alpha_t, j) * row_at(proj, j)
        half = half + lane_at(vv, j) * row_at(alpha, j)
    quad = jnp.zeros_like(pay)
    for k in range(nb):
        quad = quad + lane_at(alpha_t, k) * row_at(half, k)
    gram = ((ww - cross) + (quad - cross)) / count
    mat = jnp.where(lane < nb, gram, jnp.where(lane - nb == row, 1.0, 0.0))
    fact = jnp.zeros_like(pay)
    for k in range(nb):
        line = row_at(mat, k)
        root = 1.0 / jnp.sqrt(lane_at(line, k))
        line = line * root
        fact = jnp.where(row == k, line, fact)
        if k < nb - 1:
            mat = mat - (lane_at(mat, k) * root) * line
    inv = roll_by(fact, -nb, 1)
    alpha_ref[...] = alpha[:, :nb]
    beta_ref[...] = jnp.where(lane >= row, fact, 0.0)[:, :nb]
    mix = jnp.zeros_like(pay)
    for j in range(nb):
        mix = mix + lane_at(inv, j) * row_at(alpha_t, j)
    for j in range(nb):
        coef_ref[j] = lane_at(inv, j)
        coef_ref[nb + j] = -lane_at(mix, j)
    step = 16

    def body(r, carry):
        rows = pl.ds(pl.multiple_of(r * step, step), step)
        xs = [w_ref[j, rows, :] for j in range(nb)] + [v_ref[j, rows, :] for j in range(nb)]
        for b in range(nb):
            acc = coef_ref[0, pl.ds(b, 1), :] * xs[0]
            for j in range(1, 2 * nb):
                acc = acc + coef_ref[j, pl.ds(b, 1), :] * xs[j]
            out_ref[b, rows, :] = acc
        return carry

    lax.fori_loop(0, v_ref.shape[1] // step, body, 0)


def shift(x, loop_by, trans_by):
    loops, trans = lax.axis_size("loop"), lax.axis_size("trans")
    pairs = []
    for i in range(loops):
        for t in range(trans):
            if 0 <= t + trans_by < trans:
                pairs.append((i * trans + t, ((i + loop_by) % loops) * trans + t + trans_by))
    return lax.ppermute(x, ("loop", "trans"), pairs)


def all_sum(x):
    sizes = {axis: lax.axis_size(axis) for axis in ("trans", "loop")}
    for axis, size in sizes.items():
        if size & (size - 1):
            x = lax.psum(x, axis)
            continue
        bit = 1
        while bit < size:
            x = x + lax.ppermute(x, axis, [(i, i ^ bit) for i in range(size)])
            bit *= 2
    return x


def local(block_now, block_prev, coupling_prev, material, permittivity):
    nb, nc, nz, _, nt = block_now.shape
    f32 = jnp.float32
    count = float(nc * nz * nt * lax.axis_size("loop") * lax.axis_size("trans"))
    v4 = block_now.reshape(nb, nc, nz, nt)
    v = block_now.reshape(nb, nc * nz, nt)
    q = block_prev.reshape(nb, nc * nz, nt)
    mat = material.reshape(nz, nt)
    vm, sm = pl.BlockSpec(memory_space=VM), pl.BlockSpec(memory_space=SM)
    params = pltpu.CompilerParams(vmem_limit_bytes=32 * 2**20)
    halo = jax.ShapeDtypeStruct((nb, 2, nz, nt), f32)
    plane = jax.ShapeDtypeStruct((nz, nt), f32)
    field = jax.ShapeDtypeStruct((nb, nc * nz, nt), f32)
    fwd, bwd, right, left, scale = pl.pallas_call(
        pack_kernel,
        out_shape=(halo, halo, plane, plane, plane),
        in_specs=[sm, vm, vm],
        out_specs=(vm,) * 5,
        compiler_params=params,
        name="pack",
    )(permittivity, v4, mat)
    fwd = shift(fwd, 1, 0)
    bwd = shift(bwd, -1, 0)
    from_left = shift(right, 0, 1)
    from_right = shift(left, 0, -1)
    corner_r = shift(right, -1, 1)
    corner_l = shift(left, 1, -1)
    npair = nb * (nb + 1) // 2
    inner, acc0 = pl.pallas_call(
        local_kernel,
        out_shape=(field, jax.ShapeDtypeStruct((npair, 8, nt), f32)),
        in_specs=[sm, sm] + [vm] * 7,
        out_specs=(vm, vm),
        compiler_params=params,
        cost_estimate=pl.CostEstimate(flops=10**7, bytes_accessed=3 * 10**6, transcendentals=0),
        name="inner",
    )(permittivity, coupling_prev, v, scale, q, from_left, from_right, corner_r, corner_l)
    w, pay = pl.pallas_call(
        sum_kernel,
        out_shape=(field, jax.ShapeDtypeStruct((8, nt), f32)),
        in_specs=[vm] * 6,
        out_specs=(vm, vm),
        scratch_shapes=[VM((nb * nb + npair, 8, nt), f32)],
        compiler_params=params,
        name="products",
    )(v, scale, inner, acc0, fwd, bwd)
    pay = all_sum(pay)
    small = jax.ShapeDtypeStruct((nb, nb), f32)
    out, alpha, beta = pl.pallas_call(
        lambda *refs: last_kernel(count, *refs),
        out_shape=(field, small, small),
        in_specs=[vm] * 3,
        out_specs=(vm,) * 3,
        scratch_shapes=[VM((2 * nb, 8, nt), f32)],
        compiler_params=params,
        name="combine",
    )(pay, v, w)
    return out.reshape(block_now.shape), alpha, beta


def solution(mesh):
    in_specs = (
        P(None, None, None, "loop", "trans"),
        P(None, None, None, "loop", "trans"),
        P(),
        P(None, "loop", "trans"),
        P(),
    )
    out_specs = (P(None, None, None, "loop", "trans"), P(), P())
    return jax.shard_map(local, mesh=mesh, in_specs=in_specs, out_specs=out_specs, check_vma=False)
```

```python
import jax
import jax.numpy as jnp
from jax import lax
from jax.experimental import pallas as pl
from jax.experimental.pallas import tpu as pltpu
from jax.sharding import PartitionSpec as P

VM = pltpu.VMEM
SM = pltpu.SMEM


def lane_ids(shape):
    return lax.broadcasted_iota(jnp.int32, shape, len(shape) - 1)


def row_ids(shape):
    return lax.broadcasted_iota(jnp.int32, shape, len(shape) - 2)


def roll_by(x, shift, axis):
    return pltpu.roll(x, shift % x.shape[axis], axis)


def cell_scale(mat, eps_ref):
    eps = jnp.full(mat.shape, eps_ref[0], jnp.float32)
    for level in range(1, eps_ref.shape[0]):
        eps = jnp.where(mat == level, eps_ref[level], eps)
    return 1.0 / jnp.sqrt(eps)


def z_next(x):
    n = x.shape[0]
    return jnp.where(row_ids(x.shape) == n - 1, 0.0, roll_by(x, -1, 0))


def z_prev(x):
    return jnp.where(row_ids(x.shape) == 0, 0.0, roll_by(x, 1, 0))


def packed(v_ref, b, scale, fwd_ref, bwd_ref, at):
    nz = scale.shape[0]
    lane = lane_ids(scale.shape)
    last = scale.shape[1] - 1
    uz = v_ref[b, pl.ds(0, nz), :] * scale
    up = v_ref[b, pl.ds(nz, nz), :] * scale
    ut = v_ref[b, pl.ds(2 * nz, nz), :] * scale
    bwd_ref[at] = uz
    bwd_ref[at + 1] = ut
    fwd_ref[at] = uz + (z_next(up) - up)
    fwd_ref[at + 1] = ut + (jnp.where(lane == last, 0.0, roll_by(up, -1, 1)) - up)


def first_kernel(v_hbm, mat_hbm, eps_hbm, fwd_ref, bwd_ref, scale_ref, v_ref, mat_ref, eps_ref, sems):
    count = v_ref.shape[0]
    copies = [
        pltpu.make_async_copy(eps_hbm, eps_ref, sems.at[0]),
        pltpu.make_async_copy(mat_hbm, mat_ref, sems.at[1]),
    ]
    for b in range(count):
        copies.append(pltpu.make_async_copy(v_hbm.at[b], v_ref.at[b], sems.at[2 + b]))
    for copy in copies:
        copy.start()
    copies[0].wait()
    copies[1].wait()
    scale = cell_scale(mat_ref[...], eps_ref)
    scale_ref[...] = scale
    for b in range(count):
        copies[2 + b].wait()
        packed(v_ref, b, scale, fwd_ref, bwd_ref, 2 * b)


def edge_kernel(v_ref, scale_ref, right_ref, left_ref):
    scale = scale_ref[...]
    nz = scale.shape[0]
    lane = lane_ids(scale.shape)
    right = jnp.zeros_like(scale)
    left = jnp.zeros_like(scale)
    for b in range(v_ref.shape[0]):
        for c in range(3):
            u = v_ref[b, pl.ds(c * nz, nz), :] * scale
            spot = 3 * b + c
            right = jnp.where(lane == spot, roll_by(u, spot + 1, 1), right)
            left = jnp.where(lane == spot, roll_by(u, spot, 1), left)
    right_ref[...] = right
    left_ref[...] = left


def corner_kernel(begin, end, v_ref, scale_ref, fr_ref, fl_ref, fwd_ref, bwd_ref):
    scale = scale_ref[...]
    for b in range(begin, end):
        packed(v_ref, b, scale, fwd_ref, bwd_ref, 2 * (b - begin))
    fwd_ref[2 * (end - begin)] = fl_ref[...]
    bwd_ref[2 * (end - begin)] = fr_ref[...]


def more_kernel(begin, end, v_ref, scale_ref, fwd_a_ref, bwd_a_ref, fwd_ref, bwd_ref):
    scale = scale_ref[...]
    for b in range(begin, end):
        packed(v_ref, b, scale, fwd_ref, bwd_ref, 2 * (b - begin))


def gram_sums(pairs, lefts, rights, steps, group):
    out = []
    for first in range(0, len(pairs), group):
        part = pairs[first : first + group]

        def body(r, accs):
            rows = pl.ds(pl.multiple_of(r * 8, 8), 8)
            load = lambda side, i: side[i][0][side[i][1], rows, :]
            ls = {j: load(lefts, j) for j in sorted({p[0] for p in part})}
            if lefts is rights:
                rs = {b: ls[b] if b in ls else load(rights, b) for b in sorted({p[1] for p in part})}
            else:
                rs = {b: load(rights, b) for b in sorted({p[1] for p in part})}
            return tuple(acc + ls[j] * rs[b] for acc, (j, b) in zip(accs, part))

        zero = jnp.zeros((8, lefts[0][0].shape[2]), jnp.float32)
        out.extend(lax.fori_loop(0, steps, body, tuple(zero for _ in part)))
    return out


def put(rows, acc, spots):
    total = jnp.sum(jnp.sum(acc, axis=0, keepdims=True), axis=1, keepdims=True)
    lane = lane_ids(rows[0].shape)
    rows = list(rows)
    for row in {s[0] for s in spots}:
        hit = None
        for spot in spots:
            if spot[0] == row:
                here = lane == spot[1]
                hit = here if hit is None else hit | here
        rows[row] = jnp.where(hit, total, rows[row])
    return rows


def inner_kernel(coup_ref, v_ref, scale_ref, q_ref, fr_ref, fl_ref, l_ref, pay_ref):
    nb = v_ref.shape[0]
    nz = scale_ref.shape[0]

    def body(b, carry):
        scale = scale_ref[...]
        lane = lane_ids(scale.shape)
        last = scale.shape[1] - 1
        uz = v_ref[b, pl.ds(0, nz), :] * scale
        up = v_ref[b, pl.ds(nz, nz), :] * scale
        ut = v_ref[b, pl.ds(2 * nz, nz), :] * scale

        def prev(u, c):
            edge = pltpu.roll(fr_ref[...], (last + 1 - (3 * b + c)) % (last + 1), 1)
            return jnp.where(lane == 0, edge, roll_by(u, 1, 1))

        def nxt(u, c):
            edge = pltpu.roll(fl_ref[...], last - (3 * b + c), 1)
            return jnp.where(lane == last, edge, roll_by(u, -1, 1))

        dt_ut = ut - prev(ut, 2)
        up_next = nxt(up, 1)
        uz_next = nxt(uz, 0)
        im_z = (z_next(up) - up) + (z_next(dt_ut) - dt_ut) + 4.0 * uz - uz_next - prev(uz, 0)
        im_p = 4.0 * up - z_next(up) - z_prev(up) - up_next - prev(up, 1) - (uz - z_prev(uz)) - dt_ut
        im_t = (
            (uz_next - z_prev(uz_next)) - (uz - z_prev(uz)) + (up_next - up)
            + 4.0 * ut - z_next(ut) - z_prev(ut)
        )
        for c, im in enumerate((im_z, im_p, im_t)):
            rows = pl.ds(c * nz, nz)
            out = im * scale
            for k in range(nb):
                out = out - coup_ref[b, k] * q_ref[k, rows, :]
            l_ref[b, rows, :] = out
        return carry

    lax.fori_loop(0, nb, body, 0)
    pairs = [(j, b) for b in range(nb) for j in range(b + 1)]
    side = [(v_ref, j) for j in range(nb)]
    row = jnp.zeros((1, v_ref.shape[2]), jnp.float32)
    rows = [row, row]
    for (j, b), acc in zip(pairs, gram_sums(pairs, side, side, v_ref.shape[1] // 8, 36)):
        rows = put(rows, acc, {(1, nb * j + b), (1, nb * b + j)})
    pay_ref[0:1, :] = rows[0]
    pay_ref[1:2, :] = rows[1]


def sum_kernel(cuts, begin, v_ref, scale_ref, l_ref, pay_in_ref, *refs):
    nb = v_ref.shape[0]
    nz, nt = scale_ref.shape
    end = cuts[-1][1]
    halos = refs[: 2 * len(cuts) + 2]
    corner_f, corner_b = halos[-2:]
    rest = refs[2 * len(cuts) + 2 :]
    old, (w_ref, pay_ref) = rest[:-2], rest[-2:]
    scale = scale_ref[...]
    lane = lane_ids(scale.shape)
    plane_f, plane_b = corner_f.shape[0] - 1, corner_b.shape[0] - 1
    for i, (low, high) in enumerate(cuts):
        fwd_ref, bwd_ref = halos[2 * i : 2 * i + 2]

        def body(m, carry):
            b = low + m
            za = fwd_ref[2 * m]
            tb = fwd_ref[2 * m + 1]
            uz = bwd_ref[2 * m]
            ut = bwd_ref[2 * m + 1]
            edge_b = pltpu.roll(corner_b[plane_b], (nt - (3 * b + 2)) % nt, 1)
            edge_f = pltpu.roll(corner_f[plane_f], nt - 1 - (3 * b + 1), 1)
            ut_prev = jnp.where(lane == 0, edge_b, roll_by(ut, 1, 1))
            tb = tb + jnp.where(lane == nt - 1, edge_f, 0.0)
            to = b - begin
            w_ref[to, pl.ds(0, nz), :] = l_ref[b, pl.ds(0, nz), :] - scale * (za + uz)
            div = (uz - z_prev(uz)) + (ut - ut_prev)
            w_ref[to, pl.ds(nz, nz), :] = l_ref[b, pl.ds(nz, nz), :] + scale * div
            w_ref[to, pl.ds(2 * nz, nz), :] = l_ref[b, pl.ds(2 * nz, nz), :] - scale * (tb + ut)
            return carry

        lax.fori_loop(0, high - low, body, 0)
    steps = v_ref.shape[1] // 8
    vs = [(v_ref, j) for j in range(nb)]
    ws = [(old[0], b) for b in range(begin)] + [(w_ref, b - begin) for b in range(begin, end)]
    rows = [pay_in_ref[0:1, :], pay_in_ref[1:2, :]]
    for j0 in range(0, nb, nb // 2):
        pairs = [(j, b) for b in range(begin, end) for j in range(j0, j0 + nb // 2)]
        for (j, b), acc in zip(pairs, gram_sums(pairs, vs, ws, steps, 32)):
            rows = put(rows, acc, {(0, nb * j + b), (1, nb * nb + nb * b + j)})
    pairs = [(j, b) for b in range(begin, end) for j in range(b + 1)]
    for (j, b), acc in zip(pairs, gram_sums(pairs, ws, ws, steps, 36)):
        rows = put(rows, acc, {(0, nb * nb + nb * j + b), (0, nb * nb + nb * b + j)})
    pay_ref[0:1, :] = rows[0]
    pay_ref[1:2, :] = rows[1]


def lane_at(x, k):
    return jnp.broadcast_to(x[:, k : k + 1], x.shape)


def row_at(x, k):
    return jnp.broadcast_to(x[k : k + 1, :], x.shape)


def matrix_of(line, offset, nb):
    x = jnp.broadcast_to(line, (8, line.shape[1]))
    row = row_ids(x.shape)
    out = roll_by(x, -offset, 1)
    for i in range(1, nb):
        out = jnp.where(row == i, roll_by(x, -offset - nb * i, 1), out)
    return out


def last_kernel(count, pay_ref, v_ref, *refs):
    w_refs = refs[:-6]
    out_hbm, alpha_ref, beta_ref, coef_ref, out_ref, sems = refs[-6:]
    nb = v_ref.shape[0]
    total = jnp.sum(pay_ref[...], axis=0)
    proj = matrix_of(total[0:1], 0, nb)
    ww = matrix_of(total[0:1], nb * nb, nb)
    vv = matrix_of(total[1:2], 0, nb)
    alpha = proj / count
    alpha_t = matrix_of(total[1:2], nb * nb, nb) / count
    lane = lane_ids(proj.shape)
    row = row_ids(proj.shape)
    cross = jnp.zeros_like(proj)
    half = jnp.zeros_like(proj)
    for j in range(nb):
        cross = cross + lane_at(alpha_t, j) * row_at(proj, j)
        half = half + lane_at(vv, j) * row_at(alpha, j)
    quad = jnp.zeros_like(proj)
    for k in range(nb):
        quad = quad + lane_at(alpha_t, k) * row_at(half, k)
    gram = ((ww - cross) + (quad - cross)) / count
    mat = jnp.where(lane < nb, gram, jnp.where(lane - nb == row, 1.0, 0.0))
    fact = jnp.zeros_like(proj)
    for k in range(nb):
        line = row_at(mat, k)
        root = 1.0 / jnp.sqrt(lane_at(line, k))
        line = line * root
        fact = jnp.where(row == k, line, fact)
        if k < nb - 1:
            mat = mat - (lane_at(mat, k) * root) * line
    inv = roll_by(fact, -nb, 1)
    alpha_ref[...] = alpha[:, :nb]
    beta_ref[...] = jnp.where(lane >= row, fact, 0.0)[:, :nb]
    mix = jnp.zeros_like(proj)
    for j in range(nb):
        mix = mix + lane_at(inv, j) * row_at(alpha_t, j)
    for j in range(nb):
        coef_ref[j] = lane_at(inv, j)
        coef_ref[nb + j] = -lane_at(mix, j)
    step = 16
    ws = [(w, i) for w in w_refs for i in range(w.shape[0])]
    pieces = sems.shape[0]
    length = v_ref.shape[1] // pieces
    copies = []
    for piece in range(pieces):
        base = piece * length

        def body(r, carry):
            rows = pl.ds(pl.multiple_of(base + r * step, step), step)
            xs = [ref[i, rows, :] for ref, i in ws] + [v_ref[j, rows, :] for j in range(nb)]
            for b in range(nb):
                acc = coef_ref[0, pl.ds(b, 1), :] * xs[0]
                for j in range(1, 2 * nb):
                    acc = acc + coef_ref[j, pl.ds(b, 1), :] * xs[j]
                out_ref[b, rows, :] = acc
            return carry

        lax.fori_loop(0, length // step, body, 0)
        part = pl.ds(base, length)
        copy = pltpu.make_async_copy(out_ref.at[:, part, :], out_hbm.at[:, part, :], sems.at[piece])
        copy.start()
        copies.append(copy)
    for copy in copies:
        copy.wait()


def shift(x, loop_by, trans_by):
    if trans_by:
        count = lax.axis_size("trans")
        return lax.ppermute(x, "trans", [(t, t + trans_by) for t in range(count) if 0 <= t + trans_by < count])
    count = lax.axis_size("loop")
    return lax.ppermute(x, "loop", [(i, (i + loop_by) % count) for i in range(count)])


def local(block_now, block_prev, coupling_prev, material, permittivity):
    nb, nc, nz, _, nt = block_now.shape
    f32 = jnp.float32
    devices = lax.axis_size("loop") * lax.axis_size("trans")
    count = float(nc * nz * nt * devices)
    v = block_now.reshape(nb, nc * nz, nt)
    q = block_prev.reshape(nb, nc * nz, nt)
    mat = material.reshape(nz, nt)
    vm, sm = pl.BlockSpec(memory_space=VM), pl.BlockSpec(memory_space=SM)
    hbm = pl.BlockSpec(memory_space=pltpu.HBM)
    params = pltpu.CompilerParams(vmem_limit_bytes=32 * 2**20)
    wide = pltpu.CompilerParams(vmem_limit_bytes=int(62 * 2**20))
    free = pl.CostEstimate(flops=0, bytes_accessed=0, transcendentals=0)
    plane = jax.ShapeDtypeStruct((nz, nt), f32)
    pay_shape = jax.ShapeDtypeStruct((2, nt), f32)
    cut_a, cut_b, cut_c = (0, nb // 2), (nb // 2, nb * 3 // 4), (nb * 3 // 4, nb)

    def planes(n):
        return jax.ShapeDtypeStruct((n, nz, nt), f32)

    def works(n):
        return jax.ShapeDtypeStruct((n, nc * nz, nt), f32)

    size_a, size_b, size_c = (2 * (c[1] - c[0]) for c in (cut_a, cut_b, cut_c))
    fwd_a, bwd_a, scale = pl.pallas_call(
        first_kernel,
        out_shape=(planes(size_a), planes(size_a), plane),
        in_specs=[hbm] * 3,
        out_specs=(vm,) * 3,
        scratch_shapes=[
            VM((cut_a[1], nc * nz, nt), f32),
            VM((nz, nt), jnp.int32),
            SM(permittivity.shape, f32),
            pltpu.SemaphoreType.DMA((2 + cut_a[1],)),
        ],
        compiler_params=wide,
        cost_estimate=free,
        name="first",
    )(v, mat, permittivity)
    fwd_a, bwd_a = shift(fwd_a, 1, 0), shift(bwd_a, -1, 0)
    right, left = pl.pallas_call(
        edge_kernel,
        out_shape=(plane, plane),
        in_specs=[vm, vm],
        out_specs=(vm, vm),
        compiler_params=params,
        cost_estimate=free,
        name="edges",
    )(v, scale)
    from_left, from_right = shift(right, 0, 1), shift(left, 0, -1)
    fwd_b, bwd_b = pl.pallas_call(
        lambda *refs: corner_kernel(*cut_b, *refs),
        out_shape=(planes(size_b + 1), planes(size_b + 1)),
        in_specs=[vm] * 4,
        out_specs=(vm, vm),
        compiler_params=params,
        cost_estimate=free,
        name="pack_b",
    )(v, scale, from_left, from_right)
    fwd_b, bwd_b = shift(fwd_b, 1, 0), shift(bwd_b, -1, 0)
    fwd_c, bwd_c = pl.pallas_call(
        lambda *refs: more_kernel(*cut_c, *refs),
        out_shape=(planes(size_c), planes(size_c)),
        in_specs=[vm, vm, hbm, hbm],
        out_specs=(vm, vm),
        compiler_params=params,
        cost_estimate=free,
        name="pack_c",
    )(v, scale, fwd_a, bwd_a)
    fwd_c, bwd_c = shift(fwd_c, 1, 0), shift(bwd_c, -1, 0)
    inner, pay = pl.pallas_call(
        inner_kernel,
        out_shape=(works(nb), pay_shape),
        in_specs=[sm] + [vm] * 5,
        out_specs=(vm, vm),
        compiler_params=params,
        cost_estimate=free,
        name="inner",
    )(coupling_prev, v, scale, q, from_left, from_right)
    w_ab, pay = pl.pallas_call(
        lambda *refs: sum_kernel((cut_a, cut_b), 0, *refs),
        out_shape=(works(cut_b[1]), pay_shape),
        in_specs=[vm] * 10,
        out_specs=(vm, vm),
        compiler_params=params,
        cost_estimate=free,
        name="products",
    )(v, scale, inner, pay, fwd_a, bwd_a, fwd_b, bwd_b, fwd_b, bwd_b)
    w_c, pay = pl.pallas_call(
        lambda *refs: sum_kernel((cut_c,), cut_c[0], *refs),
        out_shape=(works(cut_c[1] - cut_c[0]), pay_shape),
        in_specs=[vm] * 9,
        out_specs=(vm, vm),
        compiler_params=params,
        cost_estimate=free,
        name="products_last",
    )(v, scale, inner, pay, fwd_c, bwd_c, fwd_b, bwd_b, w_ab)
    pay = jnp.broadcast_to(pay[None], (devices, 2, nt))
    pay = lax.all_to_all(pay, ("loop", "trans"), 0, 0)
    small = jax.ShapeDtypeStruct((nb, nb), f32)
    out, alpha, beta = pl.pallas_call(
        lambda *refs: last_kernel(count, *refs),
        out_shape=(works(nb), small, small),
        in_specs=[vm] * 4,
        out_specs=(hbm, vm, vm),
        scratch_shapes=[VM((2 * nb, 8, nt), f32), VM((nb, nc * nz, nt), f32), pltpu.SemaphoreType.DMA((4,))],
        compiler_params=params,
        cost_estimate=free,
        name="combine",
    )(pay, v, w_ab, w_c)
    return out.reshape(block_now.shape), alpha, beta


def solution(mesh):
    in_specs = (
        P(None, None, None, "loop", "trans"),
        P(None, None, None, "loop", "trans"),
        P(),
        P(None, "loop", "trans"),
        P(),
    )
    out_specs = (P(None, None, None, "loop", "trans"), P(), P())
    return jax.shard_map(local, mesh=mesh, in_specs=in_specs, out_specs=out_specs, check_vma=False)
```

```python
import jax
import jax.numpy as jnp
from jax import lax
from jax.experimental import pallas as pl
from jax.experimental.pallas import tpu as pltpu
from jax.sharding import PartitionSpec as P

VM = pltpu.VMEM
SM = pltpu.SMEM


def lane_ids(shape):
    return lax.broadcasted_iota(jnp.int32, shape, len(shape) - 1)


def row_ids(shape):
    return lax.broadcasted_iota(jnp.int32, shape, len(shape) - 2)


def roll_by(x, shift, axis):
    return pltpu.roll(x, shift % x.shape[axis], axis)


def cell_scale(mat, eps_ref):
    eps = jnp.full(mat.shape, eps_ref[0], jnp.float32)
    for level in range(1, eps_ref.shape[0]):
        eps = jnp.where(mat == level, eps_ref[level], eps)
    return 1.0 / jnp.sqrt(eps)


def z_next(x):
    n = x.shape[0]
    return jnp.where(row_ids(x.shape) == n - 1, 0.0, roll_by(x, -1, 0))


def z_prev(x):
    return jnp.where(row_ids(x.shape) == 0, 0.0, roll_by(x, 1, 0))


def packed(v_ref, b, scale, fwd_ref, bwd_ref, at):
    nz = scale.shape[0]
    lane = lane_ids(scale.shape)
    last = scale.shape[1] - 1
    uz = v_ref[b, pl.ds(0, nz), :] * scale
    up = v_ref[b, pl.ds(nz, nz), :] * scale
    ut = v_ref[b, pl.ds(2 * nz, nz), :] * scale
    one, two = pl.ds(at * nz, nz), pl.ds((at + 1) * nz, nz)
    bwd_ref[one, :] = uz
    bwd_ref[two, :] = ut
    fwd_ref[one, :] = uz + (z_next(up) - up)
    fwd_ref[two, :] = ut + (jnp.where(lane == last, 0.0, roll_by(up, -1, 1)) - up)


def first_kernel(v_hbm, mat_hbm, eps_hbm, fwd_ref, bwd_ref, scale_ref, v_ref, mat_ref, eps_ref, sems):
    count = v_ref.shape[0]
    copies = [
        pltpu.make_async_copy(eps_hbm, eps_ref, sems.at[0]),
        pltpu.make_async_copy(mat_hbm, mat_ref, sems.at[1]),
    ]
    for b in range(count):
        copies.append(pltpu.make_async_copy(v_hbm.at[b], v_ref.at[b], sems.at[2 + b]))
    for copy in copies:
        copy.start()
    copies[0].wait()
    copies[1].wait()
    scale = cell_scale(mat_ref[...], eps_ref)
    scale_ref[...] = scale
    for b in range(count):
        copies[2 + b].wait()
        packed(v_ref, b, scale, fwd_ref, bwd_ref, 2 * b)


def edge_kernel(v_ref, scale_ref, right_ref, left_ref):
    scale = scale_ref[...]
    nz = scale.shape[0]
    lane = lane_ids(scale.shape)
    right = jnp.zeros_like(scale)
    left = jnp.zeros_like(scale)
    for b in range(v_ref.shape[0]):
        for c in range(3):
            u = v_ref[b, pl.ds(c * nz, nz), :] * scale
            spot = v_ref.shape[0] * c + b
            right = jnp.where(lane == spot, roll_by(u, spot + 1, 1), right)
            left = jnp.where(lane == spot, roll_by(u, spot, 1), left)
    right_ref[...] = right
    left_ref[...] = left


def turned(x):
    pad = jnp.zeros((x.shape[1] - x.shape[0], x.shape[1]), x.dtype)
    return jnp.concatenate([x, pad], axis=0).T


def corner_kernel(begin, end, v_ref, scale_ref, fr_ref, fl_ref, fwd_ref, bwd_ref):
    scale = scale_ref[...]
    for b in range(begin, end):
        packed(v_ref, b, scale, fwd_ref, bwd_ref, 2 * (b - begin))
    nb = v_ref.shape[0]
    rows = pl.ds(2 * (end - begin) * scale.shape[0], nb)
    fwd_ref[rows, :] = turned(fl_ref[...])[nb : 2 * nb, :]
    bwd_ref[rows, :] = turned(fr_ref[...])[2 * nb : 3 * nb, :]


def more_kernel(begin, end, v_ref, scale_ref, fwd_a_ref, bwd_a_ref, fwd_ref, bwd_ref):
    scale = scale_ref[...]
    for b in range(begin, end):
        packed(v_ref, b, scale, fwd_ref, bwd_ref, 2 * (b - begin))


def merge(a, b, dist):
    low = (row_ids(a.shape) & dist) == 0
    other = jnp.where(low, b, a)
    swapped = roll_by(other, dist, 0)
    if 2 * dist != a.shape[0]:
        swapped = jnp.where(low, roll_by(other, -dist, 0), swapped)
    return jnp.where(low, a, b) + swapped


def add_products(pairs, steps, group, pays, unroll=1):
    shape = pays[0].shape
    lane, row = lane_ids(shape), row_ids(shape)
    zero = jnp.zeros(shape, jnp.float32)
    for first in range(0, len(pairs), group):
        part = pairs[first : first + group]

        def body(r, accs):
            rows = pl.ds(pl.multiple_of(r * 8, 8), 8)
            got = {}
            for left, j, right, b, _ in part:
                for ref, i in ((left, j), (right, b)):
                    if (id(ref), i) not in got:
                        got[(id(ref), i)] = ref[i, rows, :]
            return tuple(
                acc + got[(id(left), j)] * got[(id(right), b)]
                for acc, (left, j, right, b, _) in zip(accs, part)
            )

        accs = list(lax.fori_loop(0, steps, body, tuple(zero for _ in part), unroll=unroll))
        for at in range(0, len(part), 8):
            eight = accs[at : at + 8]
            eight = eight + [zero] * (8 - len(eight))
            four = [merge(eight[i], eight[i + 4], 4) for i in range(4)]
            two = [merge(four[i], four[i + 2], 2) for i in range(2)]
            sums = jnp.sum(merge(two[0], two[1], 1), axis=1, keepdims=True)
            for line in range(len(pays)):
                hit = None
                for i, pair in enumerate(part[at : at + 8]):
                    for spot in sorted(pair[4]):
                        if spot[0] == line:
                            here = (row == i) & (lane == spot[1])
                            hit = here if hit is None else hit | here
                if hit is not None:
                    pays[line] = pays[line] + jnp.where(hit, sums, 0.0)
    return pays


def store_pays(pay_ref, pays, before=None):
    for line, pay in enumerate(pays):
        total = jnp.sum(pay, axis=0, keepdims=True)
        if before is not None:
            total = total + before[line : line + 1, :]
        pay_ref[line : line + 1, :] = total


def inner_kernel(coup_ref, v_ref, scale_ref, q_ref, fr_ref, fl_ref, l_ref, pay_ref):
    nb = v_ref.shape[0]
    nz = scale_ref.shape[0]

    def body(b, carry):
        scale = scale_ref[...]
        lane = lane_ids(scale.shape)
        last = scale.shape[1] - 1
        uz = v_ref[b, pl.ds(0, nz), :] * scale
        up = v_ref[b, pl.ds(nz, nz), :] * scale
        ut = v_ref[b, pl.ds(2 * nz, nz), :] * scale

        def prev(u, c):
            edge = pltpu.roll(fr_ref[...], (last + 1 - (nb * c + b)) % (last + 1), 1)
            return jnp.where(lane == 0, edge, roll_by(u, 1, 1))

        def nxt(u, c):
            edge = pltpu.roll(fl_ref[...], last - (nb * c + b), 1)
            return jnp.where(lane == last, edge, roll_by(u, -1, 1))

        dt_ut = ut - prev(ut, 2)
        up_next = nxt(up, 1)
        uz_next = nxt(uz, 0)
        im_z = (z_next(up) - up) + (z_next(dt_ut) - dt_ut) + 4.0 * uz - uz_next - prev(uz, 0)
        im_p = 4.0 * up - z_next(up) - z_prev(up) - up_next - prev(up, 1) - (uz - z_prev(uz)) - dt_ut
        im_t = (
            (uz_next - z_prev(uz_next)) - (uz - z_prev(uz)) + (up_next - up)
            + 4.0 * ut - z_next(ut) - z_prev(ut)
        )
        for c, im in enumerate((im_z, im_p, im_t)):
            rows = pl.ds(c * nz, nz)
            out = im * scale
            for k in range(nb):
                out = out - coup_ref[b, k] * q_ref[k, rows, :]
            l_ref[b, rows, :] = out
        return carry

    lax.fori_loop(0, nb, body, 0)
    zero = jnp.zeros((8, v_ref.shape[2]), jnp.float32)
    pairs = [(v_ref, j, v_ref, b, {(1, nb * j + b), (1, nb * b + j)}) for b in range(nb) for j in range(b + 1)]
    store_pays(pay_ref, add_products(pairs, v_ref.shape[1] // 8, 36, [zero, zero]))


def sum_kernel(cuts, begin, v_ref, scale_ref, l_ref, pay_in_ref, *refs):
    nb = v_ref.shape[0]
    nz, nt = scale_ref.shape
    end = cuts[-1][1]
    halos = refs[: 2 * len(cuts) + 2]
    corner_f, corner_b = halos[-2:]
    rest = refs[2 * len(cuts) + 2 :]
    old, (w_ref, pay_ref) = rest[:-2], rest[-2:]
    scale = scale_ref[...]
    lane = lane_ids(scale.shape)
    columns_f = turned(corner_f[pl.ds(corner_f.shape[0] - nb, nb), :])[:nz, :]
    columns_b = turned(corner_b[pl.ds(corner_b.shape[0] - nb, nb), :])[:nz, :]
    for i, (low, high) in enumerate(cuts):
        fwd_ref, bwd_ref = halos[2 * i : 2 * i + 2]

        for m in range(high - low):
            b = low + m
            one, two = pl.ds(2 * m * nz, nz), pl.ds((2 * m + 1) * nz, nz)
            za, tb = fwd_ref[one, :], fwd_ref[two, :]
            uz, ut = bwd_ref[one, :], bwd_ref[two, :]
            edge_b = roll_by(columns_b, -b, 1)
            edge_f = roll_by(columns_f, nt - 1 - b, 1)
            ut_prev = jnp.where(lane == 0, edge_b, roll_by(ut, 1, 1))
            tb = tb + jnp.where(lane == nt - 1, edge_f, 0.0)
            to = b - begin
            w_ref[to, pl.ds(0, nz), :] = l_ref[b, pl.ds(0, nz), :] - scale * (za + uz)
            div = (uz - z_prev(uz)) + (ut - ut_prev)
            w_ref[to, pl.ds(nz, nz), :] = l_ref[b, pl.ds(nz, nz), :] + scale * div
            w_ref[to, pl.ds(2 * nz, nz), :] = l_ref[b, pl.ds(2 * nz, nz), :] - scale * (tb + ut)

    ws = [(old[0], b) for b in range(begin)] + [(w_ref, b - begin) for b in range(begin, end)]
    pairs = []
    for b in range(begin, end):
        pairs += [(v_ref, j, *ws[b], {(0, nb * j + b), (1, nb * nb + nb * b + j)}) for j in range(nb)]
        pairs += [(*ws[j], *ws[b], {(0, nb * nb + nb * j + b), (0, nb * nb + nb * b + j)}) for j in range(b + 1)]
    zero = jnp.zeros((8, nt), jnp.float32)
    store_pays(pay_ref, add_products(pairs, v_ref.shape[1] // 8, 36, [zero, zero]), pay_in_ref)


def lane_at(x, k):
    return jnp.broadcast_to(x[:, k : k + 1], x.shape)


def row_at(x, k):
    return jnp.broadcast_to(x[k : k + 1, :], x.shape)


def matrix_of(line, offset, nb):
    x = jnp.broadcast_to(line, (8, line.shape[1]))
    row = row_ids(x.shape)
    out = roll_by(x, -offset, 1)
    for i in range(1, nb):
        out = jnp.where(row == i, roll_by(x, -offset - nb * i, 1), out)
    return out


def last_kernel(count, pay_ref, v_ref, *refs):
    w_refs = refs[:-6]
    out_hbm, alpha_ref, beta_ref, coef_ref, out_ref, sems = refs[-6:]
    nb = v_ref.shape[0]
    total = jnp.sum(pay_ref[...], axis=0)
    proj = matrix_of(total[0:1], 0, nb)
    ww = matrix_of(total[0:1], nb * nb, nb)
    vv = matrix_of(total[1:2], 0, nb)
    alpha = proj / count
    alpha_t = matrix_of(total[1:2], nb * nb, nb) / count
    lane = lane_ids(proj.shape)
    row = row_ids(proj.shape)
    cross = jnp.zeros_like(proj)
    half = jnp.zeros_like(proj)
    for j in range(nb):
        cross = cross + lane_at(alpha_t, j) * row_at(proj, j)
        half = half + lane_at(vv, j) * row_at(alpha, j)
    quad = jnp.zeros_like(proj)
    for k in range(nb):
        quad = quad + lane_at(alpha_t, k) * row_at(half, k)
    gram = ((ww - cross) + (quad - cross)) / count
    ws = [(w, i) for w in w_refs for i in range(w.shape[0])]
    for j in range(nb):
        coef_ref[j] = lane_at(alpha_t, j)
    blocks = v_ref.shape[1] // 8
    mat = jnp.where(lane < nb, gram, jnp.where(lane - nb == row, 1.0, 0.0))
    fact = jnp.zeros_like(proj)
    for k in range(nb):
        line = row_at(mat, k)
        root = lane_at(line, k)
        root = 1.0 / jnp.sqrt(root)
        line = line * root
        fact = jnp.where(row == k, line, fact)
        if k < nb - 1:
            mat = mat - (lane_at(mat, k) * root) * line
        for r in range(k * blocks // nb, (k + 1) * blocks // nb):
            rows = pl.ds(8 * r, 8)
            vs = [v_ref[j, rows, :] for j in range(nb)]
            for b, (w_ref, i) in enumerate(ws):
                acc = w_ref[i, rows, :]
                for j in range(nb):
                    acc = acc - coef_ref[j, pl.ds(b, 1), :] * vs[j]
                out_ref[b, rows, :] = acc
    inv = roll_by(fact, -nb, 1)
    alpha_ref[...] = alpha[:, :nb]
    beta_ref[...] = jnp.where(lane >= row, fact, 0.0)[:, :nb]
    for j in range(nb):
        coef_ref[nb + j] = lane_at(inv, j)
    step = 16
    pieces = sems.shape[0]
    length = v_ref.shape[1] // pieces
    copies = []
    for piece in range(pieces):
        base = piece * length

        def body(r, carry):
            rows = pl.ds(pl.multiple_of(base + r * step, step), step)
            xs = [out_ref[j, rows, :] for j in range(nb)]
            for b in range(nb):
                acc = coef_ref[nb, pl.ds(b, 1), :] * xs[0]
                for j in range(1, b + 1):
                    acc = acc + coef_ref[nb + j, pl.ds(b, 1), :] * xs[j]
                out_ref[b, rows, :] = acc
            return carry

        lax.fori_loop(0, length // step, body, 0)
        part = pl.ds(base, length)
        copy = pltpu.make_async_copy(out_ref.at[:, part, :], out_hbm.at[:, part, :], sems.at[piece])
        copy.start()
        copies.append(copy)
    for copy in copies:
        copy.wait()


def shift(x, loop_by, trans_by):
    if trans_by:
        count = lax.axis_size("trans")
        return lax.ppermute(x, "trans", [(t, t + trans_by) for t in range(count) if 0 <= t + trans_by < count])
    count = lax.axis_size("loop")
    return lax.ppermute(x, "loop", [(i, (i + loop_by) % count) for i in range(count)])


def local(block_now, block_prev, coupling_prev, material, permittivity):
    nb, nc, nz, _, nt = block_now.shape
    f32 = jnp.float32
    devices = lax.axis_size("loop") * lax.axis_size("trans")
    count = float(nc * nz * nt * devices)
    v = block_now.reshape(nb, nc * nz, nt)
    q = block_prev.reshape(nb, nc * nz, nt)
    mat = material.reshape(nz, nt)
    vm, sm = pl.BlockSpec(memory_space=VM), pl.BlockSpec(memory_space=SM)
    hbm = pl.BlockSpec(memory_space=pltpu.HBM)
    params = pltpu.CompilerParams(vmem_limit_bytes=32 * 2**20)
    wide = pltpu.CompilerParams(vmem_limit_bytes=int(62 * 2**20))
    free = pl.CostEstimate(flops=0, bytes_accessed=0, transcendentals=0)
    plane = jax.ShapeDtypeStruct((nz, nt), f32)
    pay_shape = jax.ShapeDtypeStruct((2, nt), f32)
    cut_a, cut_b, cut_c = (0, nb // 2), (nb // 2, nb * 3 // 4), (nb * 3 // 4, nb)

    def planes(n, more=0):
        return jax.ShapeDtypeStruct((n * nz + more, nt), f32)

    def works(n):
        return jax.ShapeDtypeStruct((n, nc * nz, nt), f32)

    size_a, size_b, size_c = (2 * (c[1] - c[0]) for c in (cut_a, cut_b, cut_c))
    fwd_a, bwd_a, scale = pl.pallas_call(
        first_kernel,
        out_shape=(planes(size_a), planes(size_a), plane),
        in_specs=[hbm] * 3,
        out_specs=(vm,) * 3,
        scratch_shapes=[
            VM((cut_a[1], nc * nz, nt), f32),
            VM((nz, nt), jnp.int32),
            SM(permittivity.shape, f32),
            pltpu.SemaphoreType.DMA((2 + cut_a[1],)),
        ],
        compiler_params=wide,
        cost_estimate=free,
        name="first",
    )(v, mat, permittivity)
    fwd_a, bwd_a = shift(fwd_a, 1, 0), shift(bwd_a, -1, 0)
    right, left = pl.pallas_call(
        edge_kernel,
        out_shape=(plane, plane),
        in_specs=[vm, vm],
        out_specs=(vm, vm),
        compiler_params=params,
        cost_estimate=free,
        name="edges",
    )(v, scale)
    from_left, from_right = shift(right, 0, 1), shift(left, 0, -1)
    fwd_b, bwd_b = pl.pallas_call(
        lambda *refs: corner_kernel(*cut_b, *refs),
        out_shape=(planes(size_b, nb), planes(size_b, nb)),
        in_specs=[vm] * 4,
        out_specs=(vm, vm),
        compiler_params=params,
        cost_estimate=free,
        name="pack_b",
    )(v, scale, from_left, from_right)
    fwd_b, bwd_b = shift(fwd_b, 1, 0), shift(bwd_b, -1, 0)
    fwd_c, bwd_c = pl.pallas_call(
        lambda *refs: more_kernel(*cut_c, *refs),
        out_shape=(planes(size_c), planes(size_c)),
        in_specs=[vm, vm, hbm, hbm],
        out_specs=(vm, vm),
        compiler_params=params,
        cost_estimate=free,
        name="pack_c",
    )(v, scale, fwd_a, bwd_a)
    fwd_c, bwd_c = shift(fwd_c, 1, 0), shift(bwd_c, -1, 0)
    inner, pay = pl.pallas_call(
        inner_kernel,
        out_shape=(works(nb), pay_shape),
        in_specs=[sm] + [vm] * 5,
        out_specs=(vm, vm),
        compiler_params=params,
        cost_estimate=free,
        name="inner",
    )(coupling_prev, v, scale, q, from_left, from_right)
    w_ab, pay = pl.pallas_call(
        lambda *refs: sum_kernel((cut_a, cut_b), 0, *refs),
        out_shape=(works(cut_b[1]), pay_shape),
        in_specs=[vm] * 10,
        out_specs=(vm, vm),
        compiler_params=params,
        cost_estimate=free,
        name="products",
    )(v, scale, inner, pay, fwd_a, bwd_a, fwd_b, bwd_b, fwd_b, bwd_b)
    w_c, pay = pl.pallas_call(
        lambda *refs: sum_kernel((cut_c,), cut_c[0], *refs),
        out_shape=(works(cut_c[1] - cut_c[0]), pay_shape),
        in_specs=[vm] * 9,
        out_specs=(vm, vm),
        compiler_params=params,
        cost_estimate=free,
        name="products_last",
    )(v, scale, inner, pay, fwd_c, bwd_c, fwd_b, bwd_b, w_ab)
    pay = jnp.broadcast_to(pay[None], (devices, 2, nt))
    pay = lax.all_to_all(pay, ("loop", "trans"), 0, 0)
    small = jax.ShapeDtypeStruct((nb, nb), f32)
    out, alpha, beta = pl.pallas_call(
        lambda *refs: last_kernel(count, *refs),
        out_shape=(works(nb), small, small),
        in_specs=[vm] * 4,
        out_specs=(hbm, vm, vm),
        scratch_shapes=[VM((2 * nb, 8, nt), f32), VM((nb, nc * nz, nt), f32), pltpu.SemaphoreType.DMA((4,))],
        compiler_params=params,
        cost_estimate=free,
        name="combine",
    )(pay, v, w_ab, w_c)
    return out.reshape(block_now.shape), alpha, beta


def solution(mesh):
    in_specs = (
        P(None, None, None, "loop", "trans"),
        P(None, None, None, "loop", "trans"),
        P(),
        P(None, "loop", "trans"),
        P(),
    )
    out_specs = (P(None, None, None, "loop", "trans"), P(), P())
    return jax.shard_map(local, mesh=mesh, in_specs=in_specs, out_specs=out_specs, check_vma=False)
```

```python
import jax
import jax.numpy as jnp
from jax import lax
from jax.experimental import pallas as pl
from jax.experimental.pallas import tpu as pltpu
from jax.sharding import PartitionSpec as P

VM = pltpu.VMEM
SM = pltpu.SMEM


def lane_ids(shape):
    return lax.broadcasted_iota(jnp.int32, shape, len(shape) - 1)


def row_ids(shape):
    return lax.broadcasted_iota(jnp.int32, shape, len(shape) - 2)


def roll_by(x, shift, axis):
    return pltpu.roll(x, shift % x.shape[axis], axis)


def cell_scale(mat, eps_ref):
    eps = jnp.full(mat.shape, eps_ref[0], jnp.float32)
    for level in range(1, eps_ref.shape[0]):
        eps = jnp.where(mat == level, eps_ref[level], eps)
    return 1.0 / jnp.sqrt(eps)


def z_next(x):
    n = x.shape[0]
    return jnp.where(row_ids(x.shape) == n - 1, 0.0, roll_by(x, -1, 0))


def z_prev(x):
    return jnp.where(row_ids(x.shape) == 0, 0.0, roll_by(x, 1, 0))


def packed(v_ref, b, scale, fwd_ref, bwd_ref, at):
    nz = scale.shape[0]
    lane = lane_ids(scale.shape)
    last = scale.shape[1] - 1
    uz = v_ref[b, pl.ds(0, nz), :] * scale
    up = v_ref[b, pl.ds(nz, nz), :] * scale
    ut = v_ref[b, pl.ds(2 * nz, nz), :] * scale
    one, two = pl.ds(at * nz, nz), pl.ds((at + 1) * nz, nz)
    bwd_ref[one, :] = uz
    bwd_ref[two, :] = ut
    fwd_ref[one, :] = uz + (z_next(up) - up)
    fwd_ref[two, :] = ut + (jnp.where(lane == last, 0.0, roll_by(up, -1, 1)) - up)


def first_kernel(v_hbm, mat_hbm, eps_hbm, fwd_ref, bwd_ref, scale_ref, v_ref, mat_ref, eps_ref, sems):
    count = v_ref.shape[0]
    copies = [
        pltpu.make_async_copy(eps_hbm, eps_ref, sems.at[0]),
        pltpu.make_async_copy(mat_hbm, mat_ref, sems.at[1]),
    ]
    for b in range(count):
        copies.append(pltpu.make_async_copy(v_hbm.at[b], v_ref.at[b], sems.at[2 + b]))
    for copy in copies:
        copy.start()
    copies[0].wait()
    copies[1].wait()
    scale = cell_scale(mat_ref[...], eps_ref)
    scale_ref[...] = scale
    for b in range(count):
        copies[2 + b].wait()
        packed(v_ref, b, scale, fwd_ref, bwd_ref, 2 * b)


def edge_kernel(v_ref, scale_ref, right_ref, left_ref):
    scale = scale_ref[...]
    nz = scale.shape[0]
    lane = lane_ids(scale.shape)
    right = jnp.zeros_like(scale)
    left = jnp.zeros_like(scale)
    for b in range(v_ref.shape[0]):
        for c in range(3):
            u = v_ref[b, pl.ds(c * nz, nz), :] * scale
            spot = v_ref.shape[0] * c + b
            right = jnp.where(lane == spot, roll_by(u, spot + 1, 1), right)
            left = jnp.where(lane == spot, roll_by(u, spot, 1), left)
    right_ref[...] = right
    left_ref[...] = left


def turned(x):
    pad = jnp.zeros((x.shape[1] - x.shape[0], x.shape[1]), x.dtype)
    return jnp.concatenate([x, pad], axis=0).T


def corner_kernel(begin, end, v_ref, scale_ref, fr_ref, fl_ref, fwd_ref, bwd_ref):
    scale = scale_ref[...]
    for b in range(begin, end):
        packed(v_ref, b, scale, fwd_ref, bwd_ref, 2 * (b - begin))
    nb = v_ref.shape[0]
    rows = pl.ds(2 * (end - begin) * scale.shape[0], nb)
    fwd_ref[rows, :] = turned(fl_ref[...])[nb : 2 * nb, :]
    bwd_ref[rows, :] = turned(fr_ref[...])[2 * nb : 3 * nb, :]


def more_kernel(begin, end, v_ref, scale_ref, fwd_a_ref, bwd_a_ref, fwd_ref, bwd_ref):
    scale = scale_ref[...]
    for b in range(begin, end):
        packed(v_ref, b, scale, fwd_ref, bwd_ref, 2 * (b - begin))


def merge(a, b, dist):
    low = (row_ids(a.shape) & dist) == 0
    other = jnp.where(low, b, a)
    swapped = roll_by(other, dist, 0)
    if 2 * dist != a.shape[0]:
        swapped = jnp.where(low, roll_by(other, -dist, 0), swapped)
    return jnp.where(low, a, b) + swapped


def add_products(pairs, steps, group, pays, unroll=1):
    shape = pays[0].shape
    lane, row = lane_ids(shape), row_ids(shape)
    zero = jnp.zeros(shape, jnp.float32)
    for first in range(0, len(pairs), group):
        part = pairs[first : first + group]

        def body(r, accs):
            rows = pl.ds(pl.multiple_of(r * 8, 8), 8)
            got = {}
            for left, j, right, b, _ in part:
                for ref, i in ((left, j), (right, b)):
                    if (id(ref), i) not in got:
                        got[(id(ref), i)] = ref[i, rows, :]
            return tuple(
                acc + got[(id(left), j)] * got[(id(right), b)]
                for acc, (left, j, right, b, _) in zip(accs, part)
            )

        accs = list(lax.fori_loop(0, steps, body, tuple(zero for _ in part), unroll=unroll))
        for at in range(0, len(part), 8):
            eight = accs[at : at + 8]
            eight = eight + [zero] * (8 - len(eight))
            four = [merge(eight[i], eight[i + 4], 4) for i in range(4)]
            two = [merge(four[i], four[i + 2], 2) for i in range(2)]
            sums = jnp.sum(merge(two[0], two[1], 1), axis=1, keepdims=True)
            for line in range(len(pays)):
                hit = None
                for i, pair in enumerate(part[at : at + 8]):
                    for spot in sorted(pair[4]):
                        if spot[0] == line:
                            here = (row == i) & (lane == spot[1])
                            hit = here if hit is None else hit | here
                if hit is not None:
                    pays[line] = pays[line] + jnp.where(hit, sums, 0.0)
    return pays


def store_pays(pay_ref, pays, before=None):
    for line, pay in enumerate(pays):
        total = jnp.sum(pay, axis=0, keepdims=True)
        if before is not None:
            total = total + before[line : line + 1, :]
        pay_ref[line : line + 1, :] = total


def inner_kernel(coup_ref, v_ref, scale_ref, q_ref, fr_ref, fl_ref, l_ref, pay_ref):
    nb = v_ref.shape[0]
    nz = scale_ref.shape[0]

    def body(b, carry):
        scale = scale_ref[...]
        lane = lane_ids(scale.shape)
        last = scale.shape[1] - 1
        uz = v_ref[b, pl.ds(0, nz), :] * scale
        up = v_ref[b, pl.ds(nz, nz), :] * scale
        ut = v_ref[b, pl.ds(2 * nz, nz), :] * scale

        def prev(u, c):
            edge = pltpu.roll(fr_ref[...], (last + 1 - (nb * c + b)) % (last + 1), 1)
            return jnp.where(lane == 0, edge, roll_by(u, 1, 1))

        def nxt(u, c):
            edge = pltpu.roll(fl_ref[...], last - (nb * c + b), 1)
            return jnp.where(lane == last, edge, roll_by(u, -1, 1))

        dt_ut = ut - prev(ut, 2)
        up_next = nxt(up, 1)
        uz_next = nxt(uz, 0)
        im_z = (z_next(up) - up) + (z_next(dt_ut) - dt_ut) + 4.0 * uz - uz_next - prev(uz, 0)
        im_p = 4.0 * up - z_next(up) - z_prev(up) - up_next - prev(up, 1) - (uz - z_prev(uz)) - dt_ut
        im_t = (
            (uz_next - z_prev(uz_next)) - (uz - z_prev(uz)) + (up_next - up)
            + 4.0 * ut - z_next(ut) - z_prev(ut)
        )
        for c, im in enumerate((im_z, im_p, im_t)):
            rows = pl.ds(c * nz, nz)
            out = im * scale
            for k in range(nb):
                out = out - coup_ref[b, k] * q_ref[k, rows, :]
            l_ref[b, rows, :] = out
        return carry

    lax.fori_loop(0, nb, body, 0)
    zero = jnp.zeros((8, v_ref.shape[2]), jnp.float32)
    pairs = [(v_ref, j, v_ref, b, {(1, nb * j + b), (1, nb * b + j)}) for b in range(nb) for j in range(b + 1)]
    store_pays(pay_ref, add_products(pairs, v_ref.shape[1] // 8, 36, [zero, zero]))


def sum_kernel(cuts, begin, v_ref, scale_ref, l_ref, pay_in_ref, *refs):
    nb = v_ref.shape[0]
    nz, nt = scale_ref.shape
    end = cuts[-1][1]
    halos = refs[: 2 * len(cuts)]
    corners = refs[2 * len(cuts) : 2 * len(cuts) + 2]
    if begin == 0:
        w_ref, pay_ref, columns_f_ref, columns_b_ref = refs[-4:]
        for corner, columns_ref in zip(corners, (columns_f_ref, columns_b_ref)):
            columns_ref[...] = turned(corner[pl.ds(corner.shape[0] - nb, nb), :])[:nz, :]
    else:
        columns_f_ref, columns_b_ref = corners
        old, w_ref, pay_ref = refs[-3:]
    columns_f, columns_b = columns_f_ref[...], columns_b_ref[...]
    scale = scale_ref[...]
    lane = lane_ids(scale.shape)
    for i, (low, high) in enumerate(cuts):
        fwd_ref, bwd_ref = halos[2 * i : 2 * i + 2]

        for m in range(high - low):
            b = low + m
            one, two = pl.ds(2 * m * nz, nz), pl.ds((2 * m + 1) * nz, nz)
            za, tb = fwd_ref[one, :], fwd_ref[two, :]
            uz, ut = bwd_ref[one, :], bwd_ref[two, :]
            edge_b = roll_by(columns_b, -b, 1)
            edge_f = roll_by(columns_f, nt - 1 - b, 1)
            ut_prev = jnp.where(lane == 0, edge_b, roll_by(ut, 1, 1))
            tb = tb + jnp.where(lane == nt - 1, edge_f, 0.0)
            to = b - begin
            w_ref[to, pl.ds(0, nz), :] = l_ref[b, pl.ds(0, nz), :] - scale * (za + uz)
            div = (uz - z_prev(uz)) + (ut - ut_prev)
            w_ref[to, pl.ds(nz, nz), :] = l_ref[b, pl.ds(nz, nz), :] + scale * div
            w_ref[to, pl.ds(2 * nz, nz), :] = l_ref[b, pl.ds(2 * nz, nz), :] - scale * (tb + ut)

    ws = [(old, b) for b in range(begin)] + [(w_ref, b - begin) for b in range(begin, end)]
    pairs = []
    for b in range(begin, end):
        pairs += [(v_ref, j, *ws[b], {(0, nb * j + b), (1, nb * nb + nb * b + j)}) for j in range(nb)]
        pairs += [(*ws[j], *ws[b], {(0, nb * nb + nb * j + b), (0, nb * nb + nb * b + j)}) for j in range(b + 1)]
    zero = jnp.zeros((8, nt), jnp.float32)
    store_pays(pay_ref, add_products(pairs, v_ref.shape[1] // 8, 36, [zero, zero]), pay_in_ref)


def lane_at(x, k):
    return jnp.broadcast_to(x[:, k : k + 1], x.shape)


def row_at(x, k):
    return jnp.broadcast_to(x[k : k + 1, :], x.shape)


def matrix_of(line, offset, nb):
    x = jnp.broadcast_to(line, (8, line.shape[1]))
    row = row_ids(x.shape)
    out = roll_by(x, -offset, 1)
    for i in range(1, nb):
        out = jnp.where(row == i, roll_by(x, -offset - nb * i, 1), out)
    return out


def last_kernel(count, pay_ref, v_ref, *refs):
    w_refs = refs[:-8]
    out_hbm, alpha_hbm, beta_hbm, coef_ref, out_ref, alpha_ref, beta_ref, sems = refs[-8:]
    nb = v_ref.shape[0]
    total = jnp.sum(pay_ref[...], axis=0)
    proj = matrix_of(total[0:1], 0, nb)
    ww = matrix_of(total[0:1], nb * nb, nb)
    vv = matrix_of(total[1:2], 0, nb)
    alpha = proj / count
    alpha_t = matrix_of(total[1:2], nb * nb, nb) / count
    alpha_ref[...] = alpha[:, :nb]
    copies = [pltpu.make_async_copy(alpha_ref, alpha_hbm, sems.at[0])]
    copies[0].start()
    lane = lane_ids(proj.shape)
    row = row_ids(proj.shape)
    cross = jnp.zeros_like(proj)
    half = jnp.zeros_like(proj)
    for j in range(nb):
        coef_ref[j] = lane_at(alpha_t, j)
        cross = cross + lane_at(alpha_t, j) * row_at(proj, j)
        half = half + lane_at(vv, j) * row_at(alpha, j)
    quad = jnp.zeros_like(proj)
    for k in range(nb):
        quad = quad + lane_at(alpha_t, k) * row_at(half, k)
    gram = ((ww - cross) + (quad - cross)) / count
    ws = [(w, i) for w in w_refs for i in range(w.shape[0])]
    blocks = v_ref.shape[1] // 8
    mat = {}
    for i in range(nb):
        line = row_at(gram, i)
        for j in range(i + 1):
            mat[i, j] = lane_at(line, j)
    low, inv = {}, {}
    beta = jnp.zeros_like(proj)
    for k in range(nb):
        root = lax.rsqrt(mat[k, k])
        low[k, k] = mat[k, k] * root
        for i in range(k + 1, nb):
            low[i, k] = mat[i, k] * root
        for i in range(k + 1, nb):
            for j in range(k + 1, i + 1):
                mat[i, j] = mat[i, j] - low[i, k] * low[j, k]
        for i in range(k, nb):
            beta = jnp.where((row == k) & (lane == i), low[i, k], beta)
        inv[k, k] = root
        for j in range(k):
            acc = low[k, j] * inv[j, j]
            for q in range(j + 1, k):
                acc = acc + low[k, q] * inv[q, j]
            inv[k, j] = -(root * acc)
        for j in range(k + 1):
            coef_ref[nb + k * (k + 1) // 2 + j] = inv[k, j]
        for r in range(k * blocks // nb, (k + 1) * blocks // nb):
            rows = pl.ds(8 * r, 8)
            vs = [v_ref[j, rows, :] for j in range(nb)]
            for b, (w_ref, i) in enumerate(ws):
                acc = w_ref[i, rows, :]
                for j in range(nb):
                    acc = acc - coef_ref[j, pl.ds(b, 1), :] * vs[j]
                out_ref[b, rows, :] = acc
    beta_ref[...] = beta[:, :nb]
    copies.append(pltpu.make_async_copy(beta_ref, beta_hbm, sems.at[1]))
    copies[1].start()
    step = 16
    pieces = sems.shape[0] - 2
    length = v_ref.shape[1] // pieces
    for piece in range(pieces):
        base = piece * length

        def body(r, carry):
            rows = pl.ds(pl.multiple_of(base + r * step, step), step)
            xs = [out_ref[j, rows, :] for j in range(nb)]
            for b in range(nb):
                at = nb + b * (b + 1) // 2
                acc = coef_ref[at, pl.ds(0, 1), :] * xs[0]
                for j in range(1, b + 1):
                    acc = acc + coef_ref[at + j, pl.ds(0, 1), :] * xs[j]
                out_ref[b, rows, :] = acc
            return carry

        lax.fori_loop(0, length // step, body, 0)
        part = pl.ds(base, length)
        copy = pltpu.make_async_copy(out_ref.at[:, part, :], out_hbm.at[:, part, :], sems.at[2 + piece])
        copy.start()
        copies.append(copy)
    for copy in copies:
        copy.wait()


def shift(x, loop_by, trans_by):
    if trans_by:
        count = lax.axis_size("trans")
        return lax.ppermute(x, "trans", [(t, t + trans_by) for t in range(count) if 0 <= t + trans_by < count])
    count = lax.axis_size("loop")
    return lax.ppermute(x, "loop", [(i, (i + loop_by) % count) for i in range(count)])


def local(block_now, block_prev, coupling_prev, material, permittivity):
    nb, nc, nz, _, nt = block_now.shape
    f32 = jnp.float32
    devices = lax.axis_size("loop") * lax.axis_size("trans")
    count = float(nc * nz * nt * devices)
    v = block_now.reshape(nb, nc * nz, nt)
    q = block_prev.reshape(nb, nc * nz, nt)
    mat = material.reshape(nz, nt)
    vm, sm = pl.BlockSpec(memory_space=VM), pl.BlockSpec(memory_space=SM)
    hbm = pl.BlockSpec(memory_space=pltpu.HBM)
    params = pltpu.CompilerParams(vmem_limit_bytes=32 * 2**20)
    wide = pltpu.CompilerParams(vmem_limit_bytes=int(62 * 2**20))
    free = pl.CostEstimate(flops=0, bytes_accessed=0, transcendentals=0)
    plane = jax.ShapeDtypeStruct((nz, nt), f32)
    pay_shape = jax.ShapeDtypeStruct((2, nt), f32)
    cut_a, cut_b, cut_c = (0, nb // 2), (nb // 2, nb - 1), (nb - 1, nb)

    def planes(n, more=0):
        return jax.ShapeDtypeStruct((n * nz + more, nt), f32)

    def works(n):
        return jax.ShapeDtypeStruct((n, nc * nz, nt), f32)

    size_a, size_b, size_c = (2 * (c[1] - c[0]) for c in (cut_a, cut_b, cut_c))
    fwd_a, bwd_a, scale = pl.pallas_call(
        first_kernel,
        out_shape=(planes(size_a), planes(size_a), plane),
        in_specs=[hbm] * 3,
        out_specs=(vm,) * 3,
        scratch_shapes=[
            VM((cut_a[1], nc * nz, nt), f32),
            VM((nz, nt), jnp.int32),
            SM(permittivity.shape, f32),
            pltpu.SemaphoreType.DMA((2 + cut_a[1],)),
        ],
        compiler_params=wide,
        cost_estimate=free,
        name="first",
    )(v, mat, permittivity)
    fwd_a, bwd_a = shift(fwd_a, 1, 0), shift(bwd_a, -1, 0)
    right, left = pl.pallas_call(
        edge_kernel,
        out_shape=(plane, plane),
        in_specs=[vm, vm],
        out_specs=(vm, vm),
        compiler_params=params,
        cost_estimate=free,
        name="edges",
    )(v, scale)
    from_left, from_right = shift(right, 0, 1), shift(left, 0, -1)
    fwd_b, bwd_b = pl.pallas_call(
        lambda *refs: corner_kernel(*cut_b, *refs),
        out_shape=(planes(size_b, nb), planes(size_b, nb)),
        in_specs=[vm] * 4,
        out_specs=(vm, vm),
        compiler_params=params,
        cost_estimate=free,
        name="pack_b",
    )(v, scale, from_left, from_right)
    fwd_b, bwd_b = shift(fwd_b, 1, 0), shift(bwd_b, -1, 0)
    fwd_c, bwd_c = pl.pallas_call(
        lambda *refs: more_kernel(*cut_c, *refs),
        out_shape=(planes(size_c), planes(size_c)),
        in_specs=[vm, vm, hbm, hbm],
        out_specs=(vm, vm),
        compiler_params=params,
        cost_estimate=free,
        name="pack_c",
    )(v, scale, fwd_a, bwd_a)
    fwd_c, bwd_c = shift(fwd_c, 1, 0), shift(bwd_c, -1, 0)
    inner, pay = pl.pallas_call(
        inner_kernel,
        out_shape=(works(nb), pay_shape),
        in_specs=[sm] + [vm] * 5,
        out_specs=(vm, vm),
        compiler_params=params,
        cost_estimate=free,
        name="inner",
    )(coupling_prev, v, scale, q, from_left, from_right)
    w_ab, pay, columns_f, columns_b = pl.pallas_call(
        lambda *refs: sum_kernel((cut_a, cut_b), 0, *refs),
        out_shape=(works(cut_b[1]), pay_shape, plane, plane),
        in_specs=[vm] * 10,
        out_specs=(vm,) * 4,
        compiler_params=params,
        cost_estimate=free,
        name="products",
    )(v, scale, inner, pay, fwd_a, bwd_a, fwd_b, bwd_b, fwd_b, bwd_b)
    w_c, pay = pl.pallas_call(
        lambda *refs: sum_kernel((cut_c,), cut_c[0], *refs),
        out_shape=(works(cut_c[1] - cut_c[0]), pay_shape),
        in_specs=[vm] * 9,
        out_specs=(vm, vm),
        compiler_params=params,
        cost_estimate=free,
        name="products_last",
    )(v, scale, inner, pay, fwd_c, bwd_c, columns_f, columns_b, w_ab)
    pay = jnp.broadcast_to(pay[None], (devices, 2, nt))
    pay = lax.all_to_all(pay, ("loop", "trans"), 0, 0)
    small = jax.ShapeDtypeStruct((nb, nb), f32)
    out, alpha, beta = pl.pallas_call(
        lambda *refs: last_kernel(count, *refs),
        out_shape=(works(nb), small, small),
        in_specs=[vm] * 4,
        out_specs=(hbm,) * 3,
        scratch_shapes=[
            VM((nb + nb * (nb + 1) // 2, 8, nt), f32),
            VM((nb, nc * nz, nt), f32),
            VM((nb, nb), f32),
            VM((nb, nb), f32),
            pltpu.SemaphoreType.DMA((6,)),
        ],
        compiler_params=params,
        cost_estimate=free,
        name="combine",
    )(pay, v, w_ab, w_c)
    return out.reshape(block_now.shape), alpha, beta


def solution(mesh):
    in_specs = (
        P(None, None, None, "loop", "trans"),
        P(None, None, None, "loop", "trans"),
        P(),
        P(None, "loop", "trans"),
        P(),
    )
    out_specs = (P(None, None, None, "loop", "trans"), P(), P())
    return jax.shard_map(local, mesh=mesh, in_specs=in_specs, out_specs=out_specs, check_vma=False)
```

```python
import jax
import jax.numpy as jnp
from jax import lax
from jax.experimental import pallas as pl
from jax.experimental.pallas import tpu as pltpu
from jax.sharding import PartitionSpec as P

VM = pltpu.VMEM
SM = pltpu.SMEM


def lane_ids(shape):
    return lax.broadcasted_iota(jnp.int32, shape, len(shape) - 1)


def row_ids(shape):
    return lax.broadcasted_iota(jnp.int32, shape, len(shape) - 2)


def roll_by(x, shift, axis):
    return pltpu.roll(x, shift % x.shape[axis], axis)


def cell_scale(mat, eps_ref):
    eps = jnp.full(mat.shape, eps_ref[0], jnp.float32)
    for level in range(1, eps_ref.shape[0]):
        eps = jnp.where(mat == level, eps_ref[level], eps)
    return 1.0 / jnp.sqrt(eps)


def z_next(x):
    n = x.shape[0]
    return jnp.where(row_ids(x.shape) == n - 1, 0.0, roll_by(x, -1, 0))


def z_prev(x):
    return jnp.where(row_ids(x.shape) == 0, 0.0, roll_by(x, 1, 0))


def packed(v_ref, b, scale, fwd_ref, bwd_ref, at):
    nz = scale.shape[0]
    lane = lane_ids(scale.shape)
    last = scale.shape[1] - 1
    uz = v_ref[b, pl.ds(0, nz), :] * scale
    up = v_ref[b, pl.ds(nz, nz), :] * scale
    ut = v_ref[b, pl.ds(2 * nz, nz), :] * scale
    one, two = pl.ds(at * nz, nz), pl.ds((at + 1) * nz, nz)
    bwd_ref[one, :] = uz
    bwd_ref[two, :] = ut
    fwd_ref[one, :] = uz + (z_next(up) - up)
    fwd_ref[two, :] = ut + (jnp.where(lane == last, 0.0, roll_by(up, -1, 1)) - up)


def first_kernel(v_hbm, mat_hbm, eps_hbm, fwd_ref, bwd_ref, scale_ref, v_ref, mat_ref, eps_ref, sems):
    count = v_ref.shape[0]
    copies = [
        pltpu.make_async_copy(eps_hbm, eps_ref, sems.at[0]),
        pltpu.make_async_copy(mat_hbm, mat_ref, sems.at[1]),
    ]
    for b in range(count):
        copies.append(pltpu.make_async_copy(v_hbm.at[b], v_ref.at[b], sems.at[2 + b]))
    for copy in copies:
        copy.start()
    copies[0].wait()
    copies[1].wait()
    scale = cell_scale(mat_ref[...], eps_ref)
    scale_ref[...] = scale
    for b in range(count):
        copies[2 + b].wait()
        packed(v_ref, b, scale, fwd_ref, bwd_ref, 2 * b)


def edge_kernel(v_ref, scale_ref, right_ref, left_ref):
    scale = scale_ref[...]
    nz = scale.shape[0]
    lane = lane_ids(scale.shape)
    right = jnp.zeros_like(scale)
    left = jnp.zeros_like(scale)
    for b in range(v_ref.shape[0]):
        for c in range(3):
            u = v_ref[b, pl.ds(c * nz, nz), :] * scale
            spot = v_ref.shape[0] * c + b
            right = jnp.where(lane == spot, roll_by(u, spot + 1, 1), right)
            left = jnp.where(lane == spot, roll_by(u, spot, 1), left)
    right_ref[...] = right
    left_ref[...] = left


def turned(x):
    pad = jnp.zeros((x.shape[1] - x.shape[0], x.shape[1]), x.dtype)
    return jnp.concatenate([x, pad], axis=0).T


def corner_kernel(begin, end, v_ref, scale_ref, fr_ref, fl_ref, fwd_ref, bwd_ref):
    scale = scale_ref[...]
    for b in range(begin, end):
        packed(v_ref, b, scale, fwd_ref, bwd_ref, 2 * (b - begin))
    nb = v_ref.shape[0]
    rows = pl.ds(2 * (end - begin) * scale.shape[0], nb)
    fwd_ref[rows, :] = turned(fl_ref[...])[nb : 2 * nb, :]
    bwd_ref[rows, :] = turned(fr_ref[...])[2 * nb : 3 * nb, :]


def more_kernel(begin, end, v_ref, scale_ref, fwd_a_ref, bwd_a_ref, fwd_ref, bwd_ref):
    scale = scale_ref[...]
    for b in range(begin, end):
        packed(v_ref, b, scale, fwd_ref, bwd_ref, 2 * (b - begin))


def merge(a, b, dist):
    low = (row_ids(a.shape) & dist) == 0
    other = jnp.where(low, b, a)
    swapped = roll_by(other, dist, 0)
    if 2 * dist != a.shape[0]:
        swapped = jnp.where(low, roll_by(other, -dist, 0), swapped)
    return jnp.where(low, a, b) + swapped


def add_products(pairs, steps, group, pays, unroll=8):
    shape = pays[0].shape
    lane, row = lane_ids(shape), row_ids(shape)
    zero = jnp.zeros(shape, jnp.float32)
    for first in range(0, len(pairs), group):
        part = pairs[first : first + group]

        def body(r, accs):
            rows = pl.ds(pl.multiple_of(r * 8, 8), 8)
            got = {}
            for left, j, right, b, _ in part:
                for ref, i in ((left, j), (right, b)):
                    if (id(ref), i) not in got:
                        got[(id(ref), i)] = ref[i, rows, :]
            return tuple(
                acc + got[(id(left), j)] * got[(id(right), b)]
                for acc, (left, j, right, b, _) in zip(accs, part)
            )

        accs = list(lax.fori_loop(0, steps, body, tuple(zero for _ in part), unroll=unroll))
        for at in range(0, len(part), 8):
            eight = accs[at : at + 8]
            eight = eight + [zero] * (8 - len(eight))
            four = [merge(eight[i], eight[i + 4], 4) for i in range(4)]
            two = [merge(four[i], four[i + 2], 2) for i in range(2)]
            sums = jnp.sum(merge(two[0], two[1], 1), axis=1, keepdims=True)
            for line in range(len(pays)):
                hit = None
                for i, pair in enumerate(part[at : at + 8]):
                    for spot in sorted(pair[4]):
                        if spot[0] == line:
                            here = (row == i) & (lane == spot[1])
                            hit = here if hit is None else hit | here
                if hit is not None:
                    pays[line] = pays[line] + jnp.where(hit, sums, 0.0)
    return pays


def store_pays(pay_ref, pays, before=None):
    for line, pay in enumerate(pays):
        total = jnp.sum(pay, axis=0, keepdims=True)
        if before is not None:
            total = total + before[line : line + 1, :]
        pay_ref[line : line + 1, :] = total


def inner_kernel(coup_ref, v_ref, scale_ref, q_ref, fr_ref, fl_ref, l_ref, pay_ref):
    nb = v_ref.shape[0]
    nz = scale_ref.shape[0]

    def body(b, carry):
        scale = scale_ref[...]
        lane = lane_ids(scale.shape)
        last = scale.shape[1] - 1
        uz = v_ref[b, pl.ds(0, nz), :] * scale
        up = v_ref[b, pl.ds(nz, nz), :] * scale
        ut = v_ref[b, pl.ds(2 * nz, nz), :] * scale

        def prev(u, c):
            edge = pltpu.roll(fr_ref[...], (last + 1 - (nb * c + b)) % (last + 1), 1)
            return jnp.where(lane == 0, edge, roll_by(u, 1, 1))

        def nxt(u, c):
            edge = pltpu.roll(fl_ref[...], last - (nb * c + b), 1)
            return jnp.where(lane == last, edge, roll_by(u, -1, 1))

        dt_ut = ut - prev(ut, 2)
        up_next = nxt(up, 1)
        uz_next = nxt(uz, 0)
        im_z = (z_next(up) - up) + (z_next(dt_ut) - dt_ut) + 4.0 * uz - uz_next - prev(uz, 0)
        im_p = 4.0 * up - z_next(up) - z_prev(up) - up_next - prev(up, 1) - (uz - z_prev(uz)) - dt_ut
        im_t = (
            (uz_next - z_prev(uz_next)) - (uz - z_prev(uz)) + (up_next - up)
            + 4.0 * ut - z_next(ut) - z_prev(ut)
        )
        for c, im in enumerate((im_z, im_p, im_t)):
            rows = pl.ds(c * nz, nz)
            out = im * scale
            for k in range(nb):
                out = out - coup_ref[b, k] * q_ref[k, rows, :]
            l_ref[b, rows, :] = out
        return carry

    lax.fori_loop(0, nb, body, 0)
    zero = jnp.zeros((8, v_ref.shape[2]), jnp.float32)
    pairs = [(v_ref, j, v_ref, b, {(1, nb * j + b), (1, nb * b + j)}) for b in range(nb) for j in range(b + 1)]
    store_pays(pay_ref, add_products(pairs, v_ref.shape[1] // 8, 36, [zero, zero]))


def sum_kernel(cuts, begin, v_ref, scale_ref, l_ref, pay_in_ref, *refs):
    nb = v_ref.shape[0]
    nz, nt = scale_ref.shape
    end = cuts[-1][1]
    halos = refs[: 2 * len(cuts)]
    corners = refs[2 * len(cuts) : 2 * len(cuts) + 2]
    if begin == 0:
        w_ref, pay_ref, columns_f_ref, columns_b_ref = refs[-4:]
        for corner, columns_ref in zip(corners, (columns_f_ref, columns_b_ref)):
            columns_ref[...] = turned(corner[pl.ds(corner.shape[0] - nb, nb), :])[:nz, :]
    else:
        columns_f_ref, columns_b_ref = corners
        old, w_ref, pay_ref = refs[-3:]
    columns_f, columns_b = columns_f_ref[...], columns_b_ref[...]
    scale = scale_ref[...]
    lane = lane_ids(scale.shape)
    for i, (low, high) in enumerate(cuts):
        fwd_ref, bwd_ref = halos[2 * i : 2 * i + 2]

        for m in range(high - low):
            b = low + m
            one, two = pl.ds(2 * m * nz, nz), pl.ds((2 * m + 1) * nz, nz)
            za, tb = fwd_ref[one, :], fwd_ref[two, :]
            uz, ut = bwd_ref[one, :], bwd_ref[two, :]
            edge_b = roll_by(columns_b, -b, 1)
            edge_f = roll_by(columns_f, nt - 1 - b, 1)
            ut_prev = jnp.where(lane == 0, edge_b, roll_by(ut, 1, 1))
            tb = tb + jnp.where(lane == nt - 1, edge_f, 0.0)
            to = b - begin
            w_ref[to, pl.ds(0, nz), :] = l_ref[b, pl.ds(0, nz), :] - scale * (za + uz)
            div = (uz - z_prev(uz)) + (ut - ut_prev)
            w_ref[to, pl.ds(nz, nz), :] = l_ref[b, pl.ds(nz, nz), :] + scale * div
            w_ref[to, pl.ds(2 * nz, nz), :] = l_ref[b, pl.ds(2 * nz, nz), :] - scale * (tb + ut)

    ws = [(old, b) for b in range(begin)] + [(w_ref, b - begin) for b in range(begin, end)]
    pairs = []
    for b in range(begin, end):
        pairs += [(v_ref, j, *ws[b], {(0, nb * j + b), (1, nb * nb + nb * b + j)}) for j in range(nb)]
        pairs += [(*ws[j], *ws[b], {(0, nb * nb + nb * j + b), (0, nb * nb + nb * b + j)}) for j in range(b + 1)]
    zero = jnp.zeros((8, nt), jnp.float32)
    store_pays(pay_ref, add_products(pairs, v_ref.shape[1] // 8, 42, [zero, zero]), pay_in_ref)


def lane_at(x, k):
    return jnp.broadcast_to(x[:, k : k + 1], x.shape)


def row_at(x, k):
    return jnp.broadcast_to(x[k : k + 1, :], x.shape)


def matrix_of(line, offset, nb):
    x = jnp.broadcast_to(line, (8, line.shape[1]))
    row = row_ids(x.shape)
    out = roll_by(x, -offset, 1)
    for i in range(1, nb):
        out = jnp.where(row == i, roll_by(x, -offset - nb * i, 1), out)
    return out


def last_kernel(count, pay_ref, v_ref, *refs):
    w_refs = refs[:-8]
    out_hbm, alpha_hbm, beta_hbm, coef_ref, out_ref, alpha_ref, beta_ref, sems = refs[-8:]
    nb = v_ref.shape[0]
    total = jnp.sum(pay_ref[...], axis=0)
    proj = matrix_of(total[0:1], 0, nb)
    ww = matrix_of(total[0:1], nb * nb, nb)
    vv = matrix_of(total[1:2], 0, nb)
    alpha = proj / count
    alpha_t = matrix_of(total[1:2], nb * nb, nb) / count
    alpha_ref[...] = alpha[:, :nb]
    copies = [pltpu.make_async_copy(alpha_ref, alpha_hbm, sems.at[0])]
    copies[0].start()
    lane = lane_ids(proj.shape)
    row = row_ids(proj.shape)
    cross = jnp.zeros_like(proj)
    half = jnp.zeros_like(proj)
    for j in range(nb):
        coef_ref[j] = lane_at(alpha_t, j)
        cross = cross + lane_at(alpha_t, j) * row_at(proj, j)
        half = half + lane_at(vv, j) * row_at(alpha, j)
    quad = jnp.zeros_like(proj)
    for k in range(nb):
        quad = quad + lane_at(alpha_t, k) * row_at(half, k)
    gram = ((ww - cross) + (quad - cross)) / count
    ws = [(w, i) for w in w_refs for i in range(w.shape[0])]
    blocks = v_ref.shape[1] // 8
    mat = {}
    for i in range(nb):
        line = row_at(gram, i)
        for j in range(i + 1):
            mat[i, j] = lane_at(line, j)
    low, inv = {}, {}
    beta = jnp.zeros_like(proj)
    for k in range(nb):
        root = lax.rsqrt(mat[k, k])
        low[k, k] = mat[k, k] * root
        for i in range(k + 1, nb):
            low[i, k] = mat[i, k] * root
        for i in range(k + 1, nb):
            for j in range(k + 1, i + 1):
                mat[i, j] = mat[i, j] - low[i, k] * low[j, k]
        for i in range(k, nb):
            beta = jnp.where((row == k) & (lane == i), low[i, k], beta)
        inv[k, k] = root
        for j in range(k):
            acc = low[k, j] * inv[j, j]
            for q in range(j + 1, k):
                acc = acc + low[k, q] * inv[q, j]
            inv[k, j] = -(root * acc)
        for j in range(k + 1):
            coef_ref[nb + k * (k + 1) // 2 + j] = inv[k, j]
        for r in range(k * blocks // nb, (k + 1) * blocks // nb):
            rows = pl.ds(8 * r, 8)
            vs = [v_ref[j, rows, :] for j in range(nb)]
            for b, (w_ref, i) in enumerate(ws):
                acc = w_ref[i, rows, :]
                for j in range(nb):
                    acc = acc - coef_ref[j, pl.ds(b, 1), :] * vs[j]
                out_ref[b, rows, :] = acc
    beta_ref[...] = beta[:, :nb]
    copies.append(pltpu.make_async_copy(beta_ref, beta_hbm, sems.at[1]))
    copies[1].start()
    step = 16
    pieces = sems.shape[0] - 2
    length = v_ref.shape[1] // pieces
    for piece in range(pieces):
        base = piece * length

        def body(r, carry):
            rows = pl.ds(pl.multiple_of(base + r * step, step), step)
            xs = [out_ref[j, rows, :] for j in range(nb)]
            for b in range(nb):
                at = nb + b * (b + 1) // 2
                acc = coef_ref[at, pl.ds(0, 1), :] * xs[0]
                for j in range(1, b + 1):
                    acc = acc + coef_ref[at + j, pl.ds(0, 1), :] * xs[j]
                out_ref[b, rows, :] = acc
            return carry

        lax.fori_loop(0, length // step, body, 0)
        part = pl.ds(base, length)
        copy = pltpu.make_async_copy(out_ref.at[:, part, :], out_hbm.at[:, part, :], sems.at[2 + piece])
        copy.start()
        copies.append(copy)
    for copy in copies:
        copy.wait()


def shift(x, loop_by, trans_by):
    if trans_by:
        count = lax.axis_size("trans")
        return lax.ppermute(x, "trans", [(t, t + trans_by) for t in range(count) if 0 <= t + trans_by < count])
    count = lax.axis_size("loop")
    return lax.ppermute(x, "loop", [(i, (i + loop_by) % count) for i in range(count)])


def local(block_now, block_prev, coupling_prev, material, permittivity):
    nb, nc, nz, _, nt = block_now.shape
    f32 = jnp.float32
    devices = lax.axis_size("loop") * lax.axis_size("trans")
    count = float(nc * nz * nt * devices)
    v = block_now.reshape(nb, nc * nz, nt)
    q = block_prev.reshape(nb, nc * nz, nt)
    mat = material.reshape(nz, nt)
    vm, sm = pl.BlockSpec(memory_space=VM), pl.BlockSpec(memory_space=SM)
    hbm = pl.BlockSpec(memory_space=pltpu.HBM)
    params = pltpu.CompilerParams(vmem_limit_bytes=32 * 2**20)
    free = pl.CostEstimate(flops=0, bytes_accessed=0, transcendentals=0)
    plane = jax.ShapeDtypeStruct((nz, nt), f32)
    pay_shape = jax.ShapeDtypeStruct((2, nt), f32)
    cut_a, cut_b, cut_c = (0, nb // 2), (nb // 2, nb - 1), (nb - 1, nb)

    def planes(n, more=0):
        return jax.ShapeDtypeStruct((n * nz + more, nt), f32)

    def works(n):
        return jax.ShapeDtypeStruct((n, nc * nz, nt), f32)

    size_a, size_b, size_c = (2 * (c[1] - c[0]) for c in (cut_a, cut_b, cut_c))
    fwd_a, bwd_a, scale = pl.pallas_call(
        first_kernel,
        out_shape=(planes(size_a), planes(size_a), plane),
        in_specs=[hbm] * 3,
        out_specs=(vm,) * 3,
        scratch_shapes=[
            VM((cut_a[1], nc * nz, nt), f32),
            VM((nz, nt), jnp.int32),
            SM(permittivity.shape, f32),
            pltpu.SemaphoreType.DMA((2 + cut_a[1],)),
        ],
        compiler_params=params,
        cost_estimate=free,
        name="first",
    )(*(pltpu.with_memory_space_constraint(x, pltpu.HBM) for x in (v, mat, permittivity)))
    fwd_a, bwd_a = shift(fwd_a, 1, 0), shift(bwd_a, -1, 0)
    right, left = pl.pallas_call(
        edge_kernel,
        out_shape=(plane, plane),
        in_specs=[vm, vm],
        out_specs=(vm, vm),
        compiler_params=params,
        cost_estimate=free,
        name="edges",
    )(v, scale)
    from_left, from_right = shift(right, 0, 1), shift(left, 0, -1)
    fwd_b, bwd_b = pl.pallas_call(
        lambda *refs: corner_kernel(*cut_b, *refs),
        out_shape=(planes(size_b, nb), planes(size_b, nb)),
        in_specs=[vm] * 4,
        out_specs=(vm, vm),
        compiler_params=params,
        cost_estimate=free,
        name="pack_b",
    )(v, scale, from_left, from_right)
    fwd_b, bwd_b = shift(fwd_b, 1, 0), shift(bwd_b, -1, 0)
    fwd_c, bwd_c = pl.pallas_call(
        lambda *refs: more_kernel(*cut_c, *refs),
        out_shape=(planes(size_c), planes(size_c)),
        in_specs=[vm, vm, hbm, hbm],
        out_specs=(vm, vm),
        compiler_params=params,
        cost_estimate=free,
        name="pack_c",
    )(v, scale, fwd_a, bwd_a)
    fwd_c, bwd_c = shift(fwd_c, 1, 0), shift(bwd_c, -1, 0)
    inner, pay = pl.pallas_call(
        inner_kernel,
        out_shape=(works(nb), pay_shape),
        in_specs=[sm] + [vm] * 5,
        out_specs=(vm, vm),
        compiler_params=params,
        cost_estimate=free,
        name="inner",
    )(coupling_prev, v, scale, q, from_left, from_right)
    w_ab, pay, columns_f, columns_b = pl.pallas_call(
        lambda *refs: sum_kernel((cut_a, cut_b), 0, *refs),
        out_shape=(works(cut_b[1]), pay_shape, plane, plane),
        in_specs=[vm] * 10,
        out_specs=(vm,) * 4,
        compiler_params=params,
        cost_estimate=free,
        name="products",
    )(v, scale, inner, pay, fwd_a, bwd_a, fwd_b, bwd_b, fwd_b, bwd_b)
    w_c, pay = pl.pallas_call(
        lambda *refs: sum_kernel((cut_c,), cut_c[0], *refs),
        out_shape=(works(cut_c[1] - cut_c[0]), pay_shape),
        in_specs=[vm] * 9,
        out_specs=(vm, vm),
        compiler_params=params,
        cost_estimate=free,
        name="products_last",
    )(v, scale, inner, pay, fwd_c, bwd_c, columns_f, columns_b, w_ab)
    pay = jnp.broadcast_to(pay[None], (devices, 2, nt))
    pay = lax.all_to_all(pay, ("loop", "trans"), 0, 0)
    small = jax.ShapeDtypeStruct((nb, nb), f32)
    out, alpha, beta = pl.pallas_call(
        lambda *refs: last_kernel(count, *refs),
        out_shape=(works(nb), small, small),
        in_specs=[vm] * 4,
        out_specs=(hbm,) * 3,
        scratch_shapes=[
            VM((nb + nb * (nb + 1) // 2, 8, nt), f32),
            VM((nb, nc * nz, nt), f32),
            VM((nb, nb), f32),
            VM((nb, nb), f32),
            pltpu.SemaphoreType.DMA((6,)),
        ],
        compiler_params=params,
        cost_estimate=free,
        name="combine",
    )(pay, v, w_ab, w_c)
    return out.reshape(block_now.shape), alpha, beta


def solution(mesh):
    in_specs = (
        P(None, None, None, "loop", "trans"),
        P(None, None, None, "loop", "trans"),
        P(),
        P(None, "loop", "trans"),
        P(),
    )
    out_specs = (P(None, None, None, "loop", "trans"), P(), P())
    return jax.shard_map(local, mesh=mesh, in_specs=in_specs, out_specs=out_specs, check_vma=False)
```

```python
import jax
import jax.numpy as jnp
from jax import lax
from jax.experimental import pallas as pl
from jax.experimental.pallas import tpu as pltpu
from jax.sharding import PartitionSpec as P

VM = pltpu.VMEM
SM = pltpu.SMEM


def lane_ids(shape):
    return lax.broadcasted_iota(jnp.int32, shape, len(shape) - 1)


def row_ids(shape):
    return lax.broadcasted_iota(jnp.int32, shape, len(shape) - 2)


def roll_by(x, shift, axis):
    return pltpu.roll(x, shift % x.shape[axis], axis)


def cell_scale(mat, eps_ref):
    eps = jnp.full(mat.shape, eps_ref[0], jnp.float32)
    for level in range(1, eps_ref.shape[0]):
        eps = jnp.where(mat == level, eps_ref[level], eps)
    return 1.0 / jnp.sqrt(eps)


def z_next(x):
    n = x.shape[0]
    return jnp.where(row_ids(x.shape) == n - 1, 0.0, roll_by(x, -1, 0))


def z_prev(x):
    return jnp.where(row_ids(x.shape) == 0, 0.0, roll_by(x, 1, 0))


def packed(v_ref, b, scale, fwd_ref, bwd_ref, at):
    nz = scale.shape[0]
    uz = v_ref[b, pl.ds(0, nz), :] * scale
    up = v_ref[b, pl.ds(nz, nz), :] * scale
    ut = v_ref[b, pl.ds(2 * nz, nz), :] * scale
    one, two = pl.ds(at * nz, nz), pl.ds((at + 1) * nz, nz)
    bwd_ref[one, :] = uz
    bwd_ref[two, :] = ut
    fwd_ref[one, :], fwd_ref[two, :] = forward_pair(uz, up, ut)


def first_kernel(cuts, v_hbm, mat_hbm, eps_hbm, *refs):
    outs, (scale_ref, v_ref, mat_ref, eps_ref, sems) = refs[: len(cuts)], refs[len(cuts) :]
    copies = [
        pltpu.make_async_copy(eps_hbm, eps_ref, sems.at[0]),
        pltpu.make_async_copy(mat_hbm, mat_ref, sems.at[1]),
    ]
    for b in range(v_ref.shape[0]):
        copies.append(pltpu.make_async_copy(v_hbm.at[b], v_ref.at[b], sems.at[2 + b]))
    for copy in copies:
        copy.start()
    copies[0].wait()
    copies[1].wait()
    scale = cell_scale(mat_ref[...], eps_ref)
    scale_ref[...] = scale
    nz = scale.shape[0]
    for (begin, end), out_ref in zip(cuts, outs):
        for b in range(begin, end):
            copies[2 + b].wait()
            for c in range(3):
                rows = pl.ds((3 * (b - begin) + c) * nz, nz)
                out_ref[rows, :] = v_ref[b, pl.ds(c * nz, nz), :] * scale


def edge_kernel(v_ref, scale_ref, right_ref, left_ref):
    scale = scale_ref[...]
    nz = scale.shape[0]
    lane = lane_ids(scale.shape)
    right = jnp.zeros_like(scale)
    left = jnp.zeros_like(scale)
    for b in range(v_ref.shape[0]):
        for c in range(3):
            u = v_ref[b, pl.ds(c * nz, nz), :] * scale
            spot = v_ref.shape[0] * c + b
            right = jnp.where(lane == spot, roll_by(u, spot + 1, 1), right)
            left = jnp.where(lane == spot, roll_by(u, spot, 1), left)
    right_ref[...] = right
    left_ref[...] = left


def turned(x):
    pad = jnp.zeros((x.shape[1] - x.shape[0], x.shape[1]), x.dtype)
    return jnp.concatenate([x, pad], axis=0).T


def forward_pair(uz, up, ut):
    lane = lane_ids(up.shape)
    up_next = jnp.where(lane == up.shape[1] - 1, 0.0, roll_by(up, -1, 1))
    return uz + (z_next(up) - up), ut + (up_next - up)


def odd_loop():
    return lax.rem(lax.axis_index("loop"), 2) == 1


def relay_kernel(nz, x_ref, *refs):
    y_ref = refs[-1]
    odd = odd_loop()
    count = x_ref.shape[0] // (3 * nz)

    def comps(m):
        return [x_ref[pl.ds((3 * m + c) * nz, nz), :] for c in range(3)]

    def store(m, pair):
        y_ref[pl.ds(2 * m * nz, nz), :] = pair[0]
        y_ref[pl.ds((2 * m + 1) * nz, nz), :] = pair[1]

    @pl.when(odd)
    def _():
        for m in range(count):
            store(m, comps(m)[::2])

    @pl.when(jnp.logical_not(odd))
    def _():
        for m in range(count):
            store(m, forward_pair(*comps(m)))


def direct_kernel(begin, end, v_ref, scale_ref, fr_ref, fl_ref, fwd_ref, bwd_ref):
    nb = v_ref.shape[0]
    scale = scale_ref[...]
    for b in range(begin, end):
        packed(v_ref, b, scale, fwd_ref, bwd_ref, 2 * (b - begin))
    rows = pl.ds(2 * (end - begin) * scale.shape[0], nb)
    fwd_ref[rows, :] = turned(fl_ref[...])[nb : 2 * nb, :]
    bwd_ref[rows, :] = turned(fr_ref[...])[2 * nb : 3 * nb, :]


def column_rows(block, count, nz, nt):
    lane = lane_ids((nz, nt))
    first = last = jnp.zeros((nz, nt), jnp.float32)
    for b in range(count):
        first = jnp.where(lane == b, roll_by(block(b, 1), b, 1), first)
        last = jnp.where(lane == b, roll_by(block(b, 2), b + 1, 1), last)
    return side_by_side(turned(first)[:8, :], turned(last)[:8, :], nz)


def side_by_side(first, last, nz):
    return first + roll_by(last, nz, 1)


def merge(a, b, dist):
    low = (row_ids(a.shape) & dist) == 0
    other = jnp.where(low, b, a)
    swapped = roll_by(other, dist, 0)
    if 2 * dist != a.shape[0]:
        swapped = jnp.where(low, roll_by(other, -dist, 0), swapped)
    return jnp.where(low, a, b) + swapped


def add_products(pairs, steps, group, pays, unroll=8):
    shape = pays[0].shape
    lane, row = lane_ids(shape), row_ids(shape)
    zero = jnp.zeros(shape, jnp.float32)
    for first in range(0, len(pairs), group):
        part = pairs[first : first + group]

        def body(r, accs):
            rows = pl.ds(pl.multiple_of(r * 8, 8), 8)
            got = {}
            for left, j, right, b, _ in part:
                for ref, i in ((left, j), (right, b)):
                    if (id(ref), i) not in got:
                        got[(id(ref), i)] = ref[i, rows, :]
            return tuple(
                acc + got[(id(left), j)] * got[(id(right), b)]
                for acc, (left, j, right, b, _) in zip(accs, part)
            )

        accs = list(lax.fori_loop(0, steps, body, tuple(zero for _ in part), unroll=unroll))
        for at in range(0, len(part), 8):
            eight = accs[at : at + 8]
            eight = eight + [zero] * (8 - len(eight))
            four = [merge(eight[i], eight[i + 4], 4) for i in range(4)]
            two = [merge(four[i], four[i + 2], 2) for i in range(2)]
            sums = jnp.sum(merge(two[0], two[1], 1), axis=1, keepdims=True)
            for line in range(len(pays)):
                hit = None
                for i, pair in enumerate(part[at : at + 8]):
                    for spot in sorted(pair[4]):
                        if spot[0] == line:
                            here = (row == i) & (lane == spot[1])
                            hit = here if hit is None else hit | here
                if hit is not None:
                    pays[line] = pays[line] + jnp.where(hit, sums, 0.0)
    return pays


def store_pays(pay_ref, pays, before=None):
    for line, pay in enumerate(pays):
        total = jnp.sum(pay, axis=0, keepdims=True)
        if before is not None:
            total = total + before[line : line + 1, :]
        pay_ref[line : line + 1, :] = total


def inner_kernel(coup_ref, v_ref, scale_ref, q_ref, fr_ref, fl_ref, l_ref, pay_ref):
    nb = v_ref.shape[0]
    nz = scale_ref.shape[0]

    def body(b, carry):
        scale = scale_ref[...]
        lane = lane_ids(scale.shape)
        last = scale.shape[1] - 1
        uz = v_ref[b, pl.ds(0, nz), :] * scale
        up = v_ref[b, pl.ds(nz, nz), :] * scale
        ut = v_ref[b, pl.ds(2 * nz, nz), :] * scale

        def prev(u, c):
            edge = pltpu.roll(fr_ref[...], (last + 1 - (nb * c + b)) % (last + 1), 1)
            return jnp.where(lane == 0, edge, roll_by(u, 1, 1))

        def nxt(u, c):
            edge = pltpu.roll(fl_ref[...], last - (nb * c + b), 1)
            return jnp.where(lane == last, edge, roll_by(u, -1, 1))

        dt_ut = ut - prev(ut, 2)
        up_next = nxt(up, 1)
        uz_next = nxt(uz, 0)
        im_z = (z_next(up) - up) + (z_next(dt_ut) - dt_ut) + 4.0 * uz - uz_next - prev(uz, 0)
        im_p = 4.0 * up - z_next(up) - z_prev(up) - up_next - prev(up, 1) - (uz - z_prev(uz)) - dt_ut
        im_t = (
            (uz_next - z_prev(uz_next)) - (uz - z_prev(uz)) + (up_next - up)
            + 4.0 * ut - z_next(ut) - z_prev(ut)
        )
        for c, im in enumerate((im_z, im_p, im_t)):
            rows = pl.ds(c * nz, nz)
            out = im * scale
            for k in range(nb):
                out = out - coup_ref[b, k] * q_ref[k, rows, :]
            l_ref[b, rows, :] = out
        return carry

    lax.fori_loop(0, nb, body, 0)
    zero = jnp.zeros((8, v_ref.shape[2]), jnp.float32)
    pairs = [(v_ref, j, v_ref, b, {(1, nb * j + b), (1, nb * b + j)}) for b in range(nb) for j in range(b + 1)]
    store_pays(pay_ref, add_products(pairs, v_ref.shape[1] // 8, 36, [zero, zero]))


def works_of(b, pairs, l_ref, scale, w_ref, to, columns=None):
    nz, nt = scale.shape
    lane = lane_ids(scale.shape)
    za, tb, uz, ut = pairs
    ut_prev = roll_by(ut, 1, 1)
    if columns is None:
        ut_prev = jnp.where(lane == 0, 0.0, ut_prev)
    else:
        edge_f, edge_b = columns[0], columns[1]
        ut_prev = jnp.where(lane == 0, roll_by(edge_b, -b, 1), ut_prev)
        tb = tb + jnp.where(lane == nt - 1, roll_by(edge_f, nt - 1 - b, 1), 0.0)
    w_ref[to, pl.ds(0, nz), :] = l_ref[b, pl.ds(0, nz), :] - scale * (za + uz)
    div = (uz - z_prev(uz)) + (ut - ut_prev)
    w_ref[to, pl.ds(nz, nz), :] = l_ref[b, pl.ds(nz, nz), :] + scale * div
    w_ref[to, pl.ds(2 * nz, nz), :] = l_ref[b, pl.ds(2 * nz, nz), :] - scale * (tb + ut)


def product_pairs(v_ref, ws, begin, end):
    nb = v_ref.shape[0]
    pairs = []
    for b in range(begin, end):
        pairs += [(v_ref, j, *ws[b], {(0, nb * j + b), (1, nb * nb + nb * b + j)}) for j in range(nb)]
        pairs += [(*ws[j], *ws[b], {(0, nb * nb + nb * j + b), (0, nb * nb + nb * b + j)}) for j in range(b + 1)]
    return pairs


def relayed_kernel(cuts, v_ref, scale_ref, l_ref, pay_in_ref, *refs):
    halos, (w_ref, pay_ref, cols_ref) = refs[:-3], refs[-3:]
    nb = v_ref.shape[0]
    nz, nt = scale_ref.shape
    end = cuts[-1][1]
    scale = scale_ref[...]
    odd = odd_loop()
    for i, (low, high) in enumerate(cuts):
        x_ref, y_ref = halos[2 * i : 2 * i + 2]
        for m in range(high - low):
            xz, xp, xt = (x_ref[pl.ds((3 * m + c) * nz, nz), :] for c in range(3))
            y0, y1 = (y_ref[pl.ds((2 * m + c) * nz, nz), :] for c in range(2))
            f0, f1 = forward_pair(xz, xp, xt)
            pairs = (
                jnp.where(odd, f0, y0), jnp.where(odd, f1, y1), jnp.where(odd, y0, xz), jnp.where(odd, y1, xt)
            )
            works_of(low + m, pairs, l_ref, scale, w_ref, low + m)
    zero = jnp.zeros((8, nt), jnp.float32)
    pairs = product_pairs(v_ref, [(w_ref, b) for b in range(end)], 0, end)
    store_pays(pay_ref, add_products(pairs, v_ref.shape[1] // 8, 42, [zero, zero]), pay_in_ref)
    cols_ref[0:8, :] = column_rows(lambda b, c: v_ref[b, pl.ds(c * nz, nz), :], nb, nz, nt)
    cols_ref[8:16, :] = column_rows(lambda b, c: w_ref[b, pl.ds(c * nz, nz), :], end, nz, nt)
    turned_scale = turned(scale)
    scale_row = side_by_side(turned_scale[0:1, :], turned_scale[nt - 1 : nt, :], nz)
    cols_ref[16:24, :] = jnp.broadcast_to(scale_row, (8, nt))


def direct_sum_kernel(begin, end, v_ref, scale_ref, l_ref, pay_in_ref, fwd_ref, bwd_ref, old_ref, cols_ref, w0_ref, w_ref, pay_ref):
    nb = v_ref.shape[0]
    nz, nt = scale_ref.shape
    scale = scale_ref[...]
    lane = lane_ids(scale.shape)
    rows = pl.ds(fwd_ref.shape[0] - nb, nb)
    rows_f, rows_b = fwd_ref[rows, :], bwd_ref[rows, :]
    columns = (turned(rows_f)[:nz, :], turned(rows_b)[:nz, :])
    scale_first = jnp.broadcast_to(scale[:, 0:1], scale.shape)
    scale_last = jnp.broadcast_to(scale[:, nt - 1 : nt], scale.shape)
    add_f, add_b = scale_last * columns[0], scale_first * columns[1]
    for b in range(begin):
        w0_ref[b, pl.ds(0, nz), :] = old_ref[b, pl.ds(0, nz), :]
        first = jnp.where(lane == 0, roll_by(add_b, -b, 1), 0.0)
        w0_ref[b, pl.ds(nz, nz), :] = old_ref[b, pl.ds(nz, nz), :] - first
        last = jnp.where(lane == nt - 1, roll_by(add_f, nt - 1 - b, 1), 0.0)
        w0_ref[b, pl.ds(2 * nz, nz), :] = old_ref[b, pl.ds(2 * nz, nz), :] - last
    for b in range(begin, end):
        m = b - begin
        za, tb = (fwd_ref[pl.ds((2 * m + c) * nz, nz), :] for c in range(2))
        uz, ut = (bwd_ref[pl.ds((2 * m + c) * nz, nz), :] for c in range(2))
        works_of(b, (za, tb, uz, ut), l_ref, scale, w_ref, m, columns)
    zero = jnp.zeros((8, nt), jnp.float32)
    ws = [(w0_ref, b) for b in range(begin)] + [(w_ref, b - begin) for b in range(begin, end)]
    pays = add_products(product_pairs(v_ref, ws, begin, end), v_ref.shape[1] // 8, 45, [zero, zero])
    row, col = row_ids((8, nt)), lane_ids((8, nt))
    v_cols, w_cols, scale_cols = cols_ref[0:8, :], cols_ref[8:16, :], cols_ref[16:24, :]
    delta = jnp.where(row < begin, -scale_cols * side_by_side(rows_b, rows_f, nz), 0.0)
    fixed = w_cols + delta
    for b in range(begin):
        proj = jnp.sum(v_cols * row_at(delta, b), axis=1, keepdims=True)
        pays[0] = pays[0] + jnp.where(col == nb * row + b, proj, 0.0)
        pays[1] = pays[1] + jnp.where(col == nb * nb + nb * b + row, proj, 0.0)
        work = jnp.sum(fixed * row_at(fixed, b) - w_cols * row_at(w_cols, b), axis=1, keepdims=True)
        pays[0] = pays[0] + jnp.where(col == nb * nb + nb * row + b, work, 0.0)
    store_pays(pay_ref, pays, pay_in_ref)


def lane_at(x, k):
    return jnp.broadcast_to(x[:, k : k + 1], x.shape)


def row_at(x, k):
    return jnp.broadcast_to(x[k : k + 1, :], x.shape)


def matrix_of(line, offset, nb):
    x = jnp.broadcast_to(line, (8, line.shape[1]))
    row = row_ids(x.shape)
    out = roll_by(x, -offset, 1)
    for i in range(1, nb):
        out = jnp.where(row == i, roll_by(x, -offset - nb * i, 1), out)
    return out


def last_kernel(count, pay_ref, v_ref, *refs):
    w_refs = refs[:-8]
    out_hbm, alpha_hbm, beta_hbm, coef_ref, out_ref, alpha_ref, beta_ref, sems = refs[-8:]
    nb = v_ref.shape[0]
    total = jnp.sum(pay_ref[...], axis=0)
    proj = matrix_of(total[0:1], 0, nb)
    ww = matrix_of(total[0:1], nb * nb, nb)
    vv = matrix_of(total[1:2], 0, nb)
    alpha = proj / count
    alpha_t = matrix_of(total[1:2], nb * nb, nb) / count
    alpha_ref[...] = alpha[:, :nb]
    copies = [pltpu.make_async_copy(alpha_ref, alpha_hbm, sems.at[0])]
    copies[0].start()
    lane = lane_ids(proj.shape)
    row = row_ids(proj.shape)
    cross = jnp.zeros_like(proj)
    half = jnp.zeros_like(proj)
    for j in range(nb):
        coef_ref[j] = lane_at(alpha_t, j)
        cross = cross + lane_at(alpha_t, j) * row_at(proj, j)
        half = half + lane_at(vv, j) * row_at(alpha, j)
    quad = jnp.zeros_like(proj)
    for k in range(nb):
        quad = quad + lane_at(alpha_t, k) * row_at(half, k)
    gram = ((ww - cross) + (quad - cross)) / count
    ws = [(w, i) for w in w_refs for i in range(w.shape[0])]
    blocks = v_ref.shape[1] // 8
    mat = {}
    for i in range(nb):
        line = row_at(gram, i)
        for j in range(i + 1):
            mat[i, j] = lane_at(line, j)
    low, inv = {}, {}
    beta = jnp.zeros_like(proj)
    for k in range(nb):
        root = lax.rsqrt(mat[k, k])
        low[k, k] = mat[k, k] * root
        for i in range(k + 1, nb):
            low[i, k] = mat[i, k] * root
        for i in range(k + 1, nb):
            for j in range(k + 1, i + 1):
                mat[i, j] = mat[i, j] - low[i, k] * low[j, k]
        for i in range(k, nb):
            beta = jnp.where((row == k) & (lane == i), low[i, k], beta)
        inv[k, k] = root
        for j in range(k):
            acc = low[k, j] * inv[j, j]
            for q in range(j + 1, k):
                acc = acc + low[k, q] * inv[q, j]
            inv[k, j] = -(root * acc)
        for j in range(k + 1):
            coef_ref[nb + k * (k + 1) // 2 + j] = inv[k, j]
        for r in range(k * blocks // nb, (k + 1) * blocks // nb):
            rows = pl.ds(8 * r, 8)
            vs = [v_ref[j, rows, :] for j in range(nb)]
            for b, (w_ref, i) in enumerate(ws):
                acc = w_ref[i, rows, :]
                for j in range(nb):
                    acc = acc - coef_ref[j, pl.ds(b, 1), :] * vs[j]
                out_ref[b, rows, :] = acc
    beta_ref[...] = beta[:, :nb]
    copies.append(pltpu.make_async_copy(beta_ref, beta_hbm, sems.at[1]))
    copies[1].start()
    step = 16
    pieces = sems.shape[0] - 2
    length = v_ref.shape[1] // pieces
    for piece in range(pieces):
        base = piece * length

        def body(r, carry):
            rows = pl.ds(pl.multiple_of(base + r * step, step), step)
            xs = [out_ref[j, rows, :] for j in range(nb)]
            for b in range(nb):
                at = nb + b * (b + 1) // 2
                acc = coef_ref[at, pl.ds(0, 1), :] * xs[0]
                for j in range(1, b + 1):
                    acc = acc + coef_ref[at + j, pl.ds(0, 1), :] * xs[j]
                out_ref[b, rows, :] = acc
            return carry

        lax.fori_loop(0, length // step, body, 0)
        part = pl.ds(base, length)
        copy = pltpu.make_async_copy(out_ref.at[:, part, :], out_hbm.at[:, part, :], sems.at[2 + piece])
        copy.start()
        copies.append(copy)
    for copy in copies:
        copy.wait()


def shift(x, loop_by, trans_by):
    if trans_by:
        count = lax.axis_size("trans")
        return lax.ppermute(x, "trans", [(t, t + trans_by) for t in range(count) if 0 <= t + trans_by < count])
    count = lax.axis_size("loop")
    return lax.ppermute(x, "loop", [(i, (i + loop_by) % count) for i in range(count)])


def swap(x):
    return lax.ppermute(x, "loop", [(i, i ^ 1) for i in range(lax.axis_size("loop"))])


def relay(x):
    count = lax.axis_size("loop")
    return lax.ppermute(x, "loop", [(i, (i + (-2 if i % 2 else 2)) % count) for i in range(count)])


def local(block_now, block_prev, coupling_prev, material, permittivity):
    nb, nc, nz, _, nt = block_now.shape
    f32 = jnp.float32
    devices = lax.axis_size("loop") * lax.axis_size("trans")
    count = float(nc * nz * nt * devices)
    v = block_now.reshape(nb, nc * nz, nt)
    q = block_prev.reshape(nb, nc * nz, nt)
    mat = material.reshape(nz, nt)
    vm, sm = pl.BlockSpec(memory_space=VM), pl.BlockSpec(memory_space=SM)
    hbm = pl.BlockSpec(memory_space=pltpu.HBM)
    params = pltpu.CompilerParams(vmem_limit_bytes=32 * 2**20)
    free = pl.CostEstimate(flops=0, bytes_accessed=0, transcendentals=0)
    plane = jax.ShapeDtypeStruct((nz, nt), f32)
    pay_shape = jax.ShapeDtypeStruct((2, nt), f32)
    assert lax.axis_size("loop") % 2 == 0
    cut_a, cut_b, cut_c = (0, nb * 3 // 8), (nb * 3 // 8, nb * 5 // 8), (nb * 5 // 8, nb)

    def planes(n, more=0):
        return jax.ShapeDtypeStruct((n * nz + more, nt), f32)

    def works(n):
        return jax.ShapeDtypeStruct((n, nc * nz, nt), f32)

    size_a, size_b, size_c = (c[1] - c[0] for c in (cut_a, cut_b, cut_c))
    x_a, x_b, scale = pl.pallas_call(
        lambda *refs: first_kernel((cut_a, cut_b), *refs),
        out_shape=(planes(3 * size_a), planes(3 * size_b), plane),
        in_specs=[hbm] * 3,
        out_specs=(vm,) * 3,
        scratch_shapes=[
            VM((cut_b[1], nc * nz, nt), f32),
            VM((nz, nt), jnp.int32),
            SM(permittivity.shape, f32),
            pltpu.SemaphoreType.DMA((2 + cut_b[1],)),
        ],
        compiler_params=params,
        cost_estimate=free,
        name="first",
    )(*(pltpu.with_memory_space_constraint(x, pltpu.HBM) for x in (v, mat, permittivity)))
    x_a, x_b = swap(x_a), swap(x_b)
    right, left = pl.pallas_call(
        edge_kernel,
        out_shape=(plane, plane),
        in_specs=[vm, vm],
        out_specs=(vm, vm),
        compiler_params=params,
        cost_estimate=free,
        name="edges",
    )(v, scale)
    from_left, from_right = shift(right, 0, 1), shift(left, 0, -1)

    def relay_pair(x, size, name, *after):
        return relay(
            pl.pallas_call(
                lambda *refs: relay_kernel(nz, *refs),
                out_shape=planes(2 * size),
                in_specs=[vm] * (1 + len(after)),
                out_specs=vm,
                compiler_params=params,
                cost_estimate=free,
                name=name,
            )(x, *after)
        )

    y_a = relay_pair(x_a, size_a, "relay_a", right, left)
    own_f, own_b = pl.pallas_call(
        lambda *refs: direct_kernel(*cut_c, *refs),
        out_shape=(planes(2 * size_c, nb), planes(2 * size_c, nb)),
        in_specs=[vm] * 4,
        out_specs=(vm, vm),
        compiler_params=params,
        cost_estimate=free,
        name="direct",
    )(v, scale, from_left, from_right)
    fwd_c, bwd_c = shift(own_f, 1, 0), shift(own_b, -1, 0)
    y_b = relay_pair(x_b, size_b, "relay_b", own_f, own_b)
    inner, pay = pl.pallas_call(
        inner_kernel,
        out_shape=(works(nb), pay_shape),
        in_specs=[sm] + [vm] * 5,
        out_specs=(vm, vm),
        compiler_params=params,
        cost_estimate=free,
        name="inner",
    )(coupling_prev, v, scale, q, from_left, from_right)
    w_ab, pay, cols = pl.pallas_call(
        lambda *refs: relayed_kernel((cut_a, cut_b), *refs),
        out_shape=(works(cut_b[1]), pay_shape, jax.ShapeDtypeStruct((24, nt), f32)),
        in_specs=[vm] * 8,
        out_specs=(vm,) * 3,
        compiler_params=params,
        cost_estimate=free,
        name="products",
    )(v, scale, inner, pay, x_a, y_a, x_b, y_b)
    w_ab, w_c, pay = pl.pallas_call(
        lambda *refs: direct_sum_kernel(*cut_c, *refs),
        out_shape=(works(cut_b[1]), works(size_c), pay_shape),
        in_specs=[vm] * 8,
        out_specs=(vm,) * 3,
        compiler_params=params,
        cost_estimate=free,
        name="products_last",
    )(v, scale, inner, pay, fwd_c, bwd_c, w_ab, cols)
    pay = jnp.broadcast_to(pay[None], (devices, 2, nt))
    pay = lax.all_to_all(pay, ("loop", "trans"), 0, 0)
    small = jax.ShapeDtypeStruct((nb, nb), f32)
    out, alpha, beta = pl.pallas_call(
        lambda *refs: last_kernel(count, *refs),
        out_shape=(works(nb), small, small),
        in_specs=[vm] * 4,
        out_specs=(hbm,) * 3,
        scratch_shapes=[
            VM((nb + nb * (nb + 1) // 2, 8, nt), f32),
            VM((nb, nc * nz, nt), f32),
            VM((nb, nb), f32),
            VM((nb, nb), f32),
            pltpu.SemaphoreType.DMA((6,)),
        ],
        compiler_params=params,
        cost_estimate=free,
        name="combine",
    )(pay, v, w_ab, w_c)
    return out.reshape(block_now.shape), alpha, beta


def solution(mesh):
    in_specs = (
        P(None, None, None, "loop", "trans"),
        P(None, None, None, "loop", "trans"),
        P(),
        P(None, "loop", "trans"),
        P(),
    )
    out_specs = (P(None, None, None, "loop", "trans"), P(), P())
    return jax.shard_map(local, mesh=mesh, in_specs=in_specs, out_specs=out_specs, check_vma=False)
```

```python
import jax
import jax.numpy as jnp
from jax import lax
from jax.experimental import pallas as pl
from jax.experimental.pallas import tpu as pltpu
from jax.sharding import PartitionSpec as P

VM = pltpu.VMEM
SM = pltpu.SMEM


def lane_ids(shape):
    return lax.broadcasted_iota(jnp.int32, shape, len(shape) - 1)


def row_ids(shape):
    return lax.broadcasted_iota(jnp.int32, shape, len(shape) - 2)


def roll_by(x, shift, axis):
    return pltpu.roll(x, shift % x.shape[axis], axis)


def cell_scale(mat, eps_ref):
    eps = jnp.full(mat.shape, eps_ref[0], jnp.float32)
    for level in range(1, eps_ref.shape[0]):
        eps = jnp.where(mat == level, eps_ref[level], eps)
    return 1.0 / jnp.sqrt(eps)


def z_next(x):
    n = x.shape[0]
    return jnp.where(row_ids(x.shape) == n - 1, 0.0, roll_by(x, -1, 0))


def z_prev(x):
    return jnp.where(row_ids(x.shape) == 0, 0.0, roll_by(x, 1, 0))


def forward_pair(uz, up, ut):
    lane = lane_ids(up.shape)
    up_next = jnp.where(lane == up.shape[1] - 1, 0.0, roll_by(up, -1, 1))
    return uz + (z_next(up) - up), ut + (up_next - up)


def odd_loop():
    return lax.rem(lax.axis_index("loop"), 2) == 1


def packed(v_ref, b, scale, fwd_ref, bwd_ref, at):
    nz = scale.shape[0]
    uz = v_ref[b, pl.ds(0, nz), :] * scale
    up = v_ref[b, pl.ds(nz, nz), :] * scale
    ut = v_ref[b, pl.ds(2 * nz, nz), :] * scale
    one, two = pl.ds(at * nz, nz), pl.ds((at + 1) * nz, nz)
    bwd_ref[one, :] = uz
    bwd_ref[two, :] = ut
    fwd_ref[one, :], fwd_ref[two, :] = forward_pair(uz, up, ut)


def first_kernel(
    cut_r, cut_a, v_hbm, mat_hbm, eps_hbm, x_ref, fwd_ref, bwd_ref, scale_ref, v_ref, mat_ref, eps_ref, sems
):
    copies = [
        pltpu.make_async_copy(eps_hbm, eps_ref, sems.at[0]),
        pltpu.make_async_copy(mat_hbm, mat_ref, sems.at[1]),
    ]
    for b in range(v_ref.shape[0]):
        copies.append(pltpu.make_async_copy(v_hbm.at[b], v_ref.at[b], sems.at[2 + b]))
    for copy in copies:
        copy.start()
    copies[0].wait()
    copies[1].wait()
    scale = cell_scale(mat_ref[...], eps_ref)
    scale_ref[...] = scale
    nz = scale.shape[0]
    for m, b in enumerate(range(*cut_r)):
        copies[2 + b].wait()
        for c in range(3):
            x_ref[pl.ds((3 * m + c) * nz, nz), :] = v_ref[b, pl.ds(c * nz, nz), :] * scale
    for m, b in enumerate(range(*cut_a)):
        copies[2 + b].wait()
        packed(v_ref, b, scale, fwd_ref, bwd_ref, 2 * m)


def relay_kernel(nz, x_ref, after_f_ref, after_b_ref, y_ref):
    odd = odd_loop()
    count = x_ref.shape[0] // (3 * nz)

    def comps(m):
        return [x_ref[pl.ds((3 * m + c) * nz, nz), :] for c in range(3)]

    def store(m, pair):
        y_ref[pl.ds(2 * m * nz, nz), :] = pair[0]
        y_ref[pl.ds((2 * m + 1) * nz, nz), :] = pair[1]

    @pl.when(odd)
    def _():
        for m in range(count):
            store(m, comps(m)[::2])

    @pl.when(jnp.logical_not(odd))
    def _():
        for m in range(count):
            store(m, forward_pair(*comps(m)))


def edge_kernel(v_ref, scale_ref, right_ref, left_ref):
    scale = scale_ref[...]
    nz = scale.shape[0]
    lane = lane_ids(scale.shape)
    right = jnp.zeros_like(scale)
    left = jnp.zeros_like(scale)
    for b in range(v_ref.shape[0]):
        for c in range(3):
            u = v_ref[b, pl.ds(c * nz, nz), :] * scale
            spot = v_ref.shape[0] * c + b
            right = jnp.where(lane == spot, roll_by(u, spot + 1, 1), right)
            left = jnp.where(lane == spot, roll_by(u, spot, 1), left)
    right_ref[...] = right
    left_ref[...] = left


def turned(x):
    pad = jnp.zeros((x.shape[1] - x.shape[0], x.shape[1]), x.dtype)
    return jnp.concatenate([x, pad], axis=0).T


def corner_kernel(begin, end, v_ref, scale_ref, fr_ref, fl_ref, fwd_ref, bwd_ref):
    scale = scale_ref[...]
    for b in range(begin, end):
        packed(v_ref, b, scale, fwd_ref, bwd_ref, 2 * (b - begin))
    nb = v_ref.shape[0]
    rows = pl.ds(2 * (end - begin) * scale.shape[0], nb)
    fwd_ref[rows, :] = turned(fl_ref[...])[nb : 2 * nb, :]
    bwd_ref[rows, :] = turned(fr_ref[...])[2 * nb : 3 * nb, :]


def more_kernel(begin, end, v_ref, scale_ref, fwd_a_ref, bwd_a_ref, fwd_ref, bwd_ref):
    scale = scale_ref[...]
    for b in range(begin, end):
        packed(v_ref, b, scale, fwd_ref, bwd_ref, 2 * (b - begin))


def merge(a, b, dist):
    low = (row_ids(a.shape) & dist) == 0
    other = jnp.where(low, b, a)
    swapped = roll_by(other, dist, 0)
    if 2 * dist != a.shape[0]:
        swapped = jnp.where(low, roll_by(other, -dist, 0), swapped)
    return jnp.where(low, a, b) + swapped


def add_products(pairs, steps, group, pays, unroll=8):
    shape = pays[0].shape
    lane, row = lane_ids(shape), row_ids(shape)
    zero = jnp.zeros(shape, jnp.float32)
    for first in range(0, len(pairs), group):
        part = pairs[first : first + group]

        def body(r, accs):
            rows = pl.ds(pl.multiple_of(r * 8, 8), 8)
            got = {}
            for left, j, right, b, _ in part:
                for ref, i in ((left, j), (right, b)):
                    if (id(ref), i) not in got:
                        got[(id(ref), i)] = ref[i, rows, :]
            return tuple(
                acc + got[(id(left), j)] * got[(id(right), b)]
                for acc, (left, j, right, b, _) in zip(accs, part)
            )

        accs = list(lax.fori_loop(0, steps, body, tuple(zero for _ in part), unroll=unroll))
        for at in range(0, len(part), 8):
            eight = accs[at : at + 8]
            eight = eight + [zero] * (8 - len(eight))
            four = [merge(eight[i], eight[i + 4], 4) for i in range(4)]
            two = [merge(four[i], four[i + 2], 2) for i in range(2)]
            sums = jnp.sum(merge(two[0], two[1], 1), axis=1, keepdims=True)
            for line in range(len(pays)):
                hit = None
                for i, pair in enumerate(part[at : at + 8]):
                    for spot in sorted(pair[4]):
                        if spot[0] == line:
                            here = (row == i) & (lane == spot[1])
                            hit = here if hit is None else hit | here
                if hit is not None:
                    pays[line] = pays[line] + jnp.where(hit, sums, 0.0)
    return pays


def store_pays(pay_ref, pays, before=None):
    for line, pay in enumerate(pays):
        total = jnp.sum(pay, axis=0, keepdims=True)
        if before is not None:
            total = total + before[line : line + 1, :]
        pay_ref[line : line + 1, :] = total


def inner_kernel(coup_ref, v_ref, scale_ref, q_ref, fr_ref, fl_ref, l_ref, pay_ref):
    nb = v_ref.shape[0]
    nz = scale_ref.shape[0]

    def body(b, carry):
        scale = scale_ref[...]
        lane = lane_ids(scale.shape)
        last = scale.shape[1] - 1
        uz = v_ref[b, pl.ds(0, nz), :] * scale
        up = v_ref[b, pl.ds(nz, nz), :] * scale
        ut = v_ref[b, pl.ds(2 * nz, nz), :] * scale

        def prev(u, c):
            edge = pltpu.roll(fr_ref[...], (last + 1 - (nb * c + b)) % (last + 1), 1)
            return jnp.where(lane == 0, edge, roll_by(u, 1, 1))

        def nxt(u, c):
            edge = pltpu.roll(fl_ref[...], last - (nb * c + b), 1)
            return jnp.where(lane == last, edge, roll_by(u, -1, 1))

        dt_ut = ut - prev(ut, 2)
        up_next = nxt(up, 1)
        uz_next = nxt(uz, 0)
        im_z = (z_next(up) - up) + (z_next(dt_ut) - dt_ut) + 4.0 * uz - uz_next - prev(uz, 0)
        im_p = 4.0 * up - z_next(up) - z_prev(up) - up_next - prev(up, 1) - (uz - z_prev(uz)) - dt_ut
        im_t = (
            (uz_next - z_prev(uz_next)) - (uz - z_prev(uz)) + (up_next - up)
            + 4.0 * ut - z_next(ut) - z_prev(ut)
        )
        for c, im in enumerate((im_z, im_p, im_t)):
            rows = pl.ds(c * nz, nz)
            out = im * scale
            for k in range(nb):
                out = out - coup_ref[b, k] * q_ref[k, rows, :]
            l_ref[b, rows, :] = out
        return carry

    lax.fori_loop(0, nb, body, 0)
    zero = jnp.zeros((8, v_ref.shape[2]), jnp.float32)
    pairs = [(v_ref, j, v_ref, b, {(1, nb * j + b), (1, nb * b + j)}) for b in range(nb) for j in range(b + 1)]
    store_pays(pay_ref, add_products(pairs, v_ref.shape[1] // 8, 36, [zero, zero]))


def sum_kernel(cuts, begin, v_ref, scale_ref, l_ref, pay_in_ref, *refs):
    nb = v_ref.shape[0]
    nz, nt = scale_ref.shape
    end = cuts[-1][1]
    halos = refs[: 2 * len(cuts)]
    corners = refs[2 * len(cuts) : 2 * len(cuts) + 2]
    if begin == 0:
        w_ref, pay_ref, columns_f_ref, columns_b_ref = refs[-4:]
        for corner, columns_ref in zip(corners, (columns_f_ref, columns_b_ref)):
            columns_ref[...] = turned(corner[pl.ds(corner.shape[0] - nb, nb), :])[:nz, :]
    else:
        columns_f_ref, columns_b_ref = corners
        old, w_ref, pay_ref = refs[-3:]
    columns_f, columns_b = columns_f_ref[...], columns_b_ref[...]
    scale = scale_ref[...]
    lane = lane_ids(scale.shape)
    odd = odd_loop()
    for i, (low, high, relayed) in enumerate(cuts):
        fwd_ref, bwd_ref = halos[2 * i : 2 * i + 2]

        for m in range(high - low):
            b = low + m
            one, two = pl.ds(2 * m * nz, nz), pl.ds((2 * m + 1) * nz, nz)
            if relayed:
                xz, xp, xt = (fwd_ref[pl.ds((3 * m + c) * nz, nz), :] for c in range(3))
                y0, y1 = bwd_ref[one, :], bwd_ref[two, :]
                f0, f1 = forward_pair(xz, xp, xt)
                za, tb = jnp.where(odd, f0, y0), jnp.where(odd, f1, y1)
                uz, ut = jnp.where(odd, y0, xz), jnp.where(odd, y1, xt)
            else:
                za, tb = fwd_ref[one, :], fwd_ref[two, :]
                uz, ut = bwd_ref[one, :], bwd_ref[two, :]
            edge_b = roll_by(columns_b, -b, 1)
            edge_f = roll_by(columns_f, nt - 1 - b, 1)
            ut_prev = jnp.where(lane == 0, edge_b, roll_by(ut, 1, 1))
            tb = tb + jnp.where(lane == nt - 1, edge_f, 0.0)
            to = b - begin
            w_ref[to, pl.ds(0, nz), :] = l_ref[b, pl.ds(0, nz), :] - scale * (za + uz)
            div = (uz - z_prev(uz)) + (ut - ut_prev)
            w_ref[to, pl.ds(nz, nz), :] = l_ref[b, pl.ds(nz, nz), :] + scale * div
            w_ref[to, pl.ds(2 * nz, nz), :] = l_ref[b, pl.ds(2 * nz, nz), :] - scale * (tb + ut)

    ws = [(old, b) for b in range(begin)] + [(w_ref, b - begin) for b in range(begin, end)]
    pairs = []
    for b in range(begin, end):
        pairs += [(v_ref, j, *ws[b], {(0, nb * j + b), (1, nb * nb + nb * b + j)}) for j in range(nb)]
        pairs += [(*ws[j], *ws[b], {(0, nb * nb + nb * j + b), (0, nb * nb + nb * b + j)}) for j in range(b + 1)]
    zero = jnp.zeros((8, nt), jnp.float32)
    store_pays(pay_ref, add_products(pairs, v_ref.shape[1] // 8, 42, [zero, zero]), pay_in_ref)


def lane_at(x, k):
    return jnp.broadcast_to(x[:, k : k + 1], x.shape)


def row_at(x, k):
    return jnp.broadcast_to(x[k : k + 1, :], x.shape)


def matrix_of(line, offset, nb):
    x = jnp.broadcast_to(line, (8, line.shape[1]))
    row = row_ids(x.shape)
    out = roll_by(x, -offset, 1)
    for i in range(1, nb):
        out = jnp.where(row == i, roll_by(x, -offset - nb * i, 1), out)
    return out


def last_kernel(count, pay_ref, v_ref, *refs):
    w_refs = refs[:-8]
    out_hbm, alpha_hbm, beta_hbm, coef_ref, out_ref, alpha_ref, beta_ref, sems = refs[-8:]
    nb = v_ref.shape[0]
    total = jnp.sum(pay_ref[...], axis=0)
    proj = matrix_of(total[0:1], 0, nb)
    ww = matrix_of(total[0:1], nb * nb, nb)
    vv = matrix_of(total[1:2], 0, nb)
    alpha = proj / count
    alpha_t = matrix_of(total[1:2], nb * nb, nb) / count
    alpha_ref[...] = alpha[:, :nb]
    copies = [pltpu.make_async_copy(alpha_ref, alpha_hbm, sems.at[0])]
    copies[0].start()
    lane = lane_ids(proj.shape)
    row = row_ids(proj.shape)
    cross = jnp.zeros_like(proj)
    half = jnp.zeros_like(proj)
    for j in range(nb):
        coef_ref[j] = lane_at(alpha_t, j)
        cross = cross + lane_at(alpha_t, j) * row_at(proj, j)
        half = half + lane_at(vv, j) * row_at(alpha, j)
    quad = jnp.zeros_like(proj)
    for k in range(nb):
        quad = quad + lane_at(alpha_t, k) * row_at(half, k)
    gram = ((ww - cross) + (quad - cross)) / count
    ws = [(w, i) for w in w_refs for i in range(w.shape[0])]
    blocks = v_ref.shape[1] // 8
    mat = {}
    for i in range(nb):
        line = row_at(gram, i)
        for j in range(i + 1):
            mat[i, j] = lane_at(line, j)
    low, inv = {}, {}
    beta = jnp.zeros_like(proj)
    for k in range(nb):
        root = lax.rsqrt(mat[k, k])
        low[k, k] = mat[k, k] * root
        for i in range(k + 1, nb):
            low[i, k] = mat[i, k] * root
        for i in range(k + 1, nb):
            for j in range(k + 1, i + 1):
                mat[i, j] = mat[i, j] - low[i, k] * low[j, k]
        for i in range(k, nb):
            beta = jnp.where((row == k) & (lane == i), low[i, k], beta)
        inv[k, k] = root
        for j in range(k):
            acc = low[k, j] * inv[j, j]
            for q in range(j + 1, k):
                acc = acc + low[k, q] * inv[q, j]
            inv[k, j] = -(root * acc)
        for j in range(k + 1):
            coef_ref[nb + k * (k + 1) // 2 + j] = inv[k, j]
        for r in range(k * blocks // nb, (k + 1) * blocks // nb):
            rows = pl.ds(8 * r, 8)
            vs = [v_ref[j, rows, :] for j in range(nb)]
            for b, (w_ref, i) in enumerate(ws):
                acc = w_ref[i, rows, :]
                for j in range(nb):
                    acc = acc - coef_ref[j, pl.ds(b, 1), :] * vs[j]
                out_ref[b, rows, :] = acc
    beta_ref[...] = beta[:, :nb]
    copies.append(pltpu.make_async_copy(beta_ref, beta_hbm, sems.at[1]))
    copies[1].start()
    step = 16
    pieces = sems.shape[0] - 2
    length = v_ref.shape[1] // pieces
    for piece in range(pieces):
        base = piece * length

        def body(r, carry):
            rows = pl.ds(pl.multiple_of(base + r * step, step), step)
            xs = [out_ref[j, rows, :] for j in range(nb)]
            for b in range(nb):
                at = nb + b * (b + 1) // 2
                acc = coef_ref[at, pl.ds(0, 1), :] * xs[0]
                for j in range(1, b + 1):
                    acc = acc + coef_ref[at + j, pl.ds(0, 1), :] * xs[j]
                out_ref[b, rows, :] = acc
            return carry

        lax.fori_loop(0, length // step, body, 0)
        part = pl.ds(base, length)
        copy = pltpu.make_async_copy(out_ref.at[:, part, :], out_hbm.at[:, part, :], sems.at[2 + piece])
        copy.start()
        copies.append(copy)
    for copy in copies:
        copy.wait()


def shift(x, loop_by, trans_by):
    if trans_by:
        count = lax.axis_size("trans")
        return lax.ppermute(x, "trans", [(t, t + trans_by) for t in range(count) if 0 <= t + trans_by < count])
    count = lax.axis_size("loop")
    return lax.ppermute(x, "loop", [(i, (i + loop_by) % count) for i in range(count)])


def swap(x):
    return lax.ppermute(x, "loop", [(i, i ^ 1) for i in range(lax.axis_size("loop"))])


def relay(x):
    count = lax.axis_size("loop")
    return lax.ppermute(x, "loop", [(i, (i + (-2 if i % 2 else 2)) % count) for i in range(count)])


def local(block_now, block_prev, coupling_prev, material, permittivity):
    nb, nc, nz, _, nt = block_now.shape
    f32 = jnp.float32
    devices = lax.axis_size("loop") * lax.axis_size("trans")
    count = float(nc * nz * nt * devices)
    v = block_now.reshape(nb, nc * nz, nt)
    q = block_prev.reshape(nb, nc * nz, nt)
    mat = material.reshape(nz, nt)
    vm, sm = pl.BlockSpec(memory_space=VM), pl.BlockSpec(memory_space=SM)
    hbm = pl.BlockSpec(memory_space=pltpu.HBM)
    params = pltpu.CompilerParams(vmem_limit_bytes=32 * 2**20)
    free = pl.CostEstimate(flops=0, bytes_accessed=0, transcendentals=0)
    plane = jax.ShapeDtypeStruct((nz, nt), f32)
    pay_shape = jax.ShapeDtypeStruct((2, nt), f32)
    assert lax.axis_size("loop") % 2 == 0
    marks = (0, nb * 3 // 8, nb * 5 // 8, nb - 1, nb)
    cut_r, cut_a, cut_b, cut_c = zip(marks[:-1], marks[1:])

    def planes(n, more=0):
        return jax.ShapeDtypeStruct((n * nz + more, nt), f32)

    def works(n):
        return jax.ShapeDtypeStruct((n, nc * nz, nt), f32)

    size_r, size_a, size_b, size_c = (2 * (c[1] - c[0]) for c in (cut_r, cut_a, cut_b, cut_c))
    x_r, fwd_a, bwd_a, scale = pl.pallas_call(
        lambda *refs: first_kernel(cut_r, cut_a, *refs),
        out_shape=(planes(size_r * 3 // 2), planes(size_a), planes(size_a), plane),
        in_specs=[hbm] * 3,
        out_specs=(vm,) * 4,
        scratch_shapes=[
            VM((cut_a[1], nc * nz, nt), f32),
            VM((nz, nt), jnp.int32),
            SM(permittivity.shape, f32),
            pltpu.SemaphoreType.DMA((2 + cut_a[1],)),
        ],
        compiler_params=params,
        cost_estimate=free,
        name="first",
    )(*(pltpu.with_memory_space_constraint(x, pltpu.HBM) for x in (v, mat, permittivity)))
    x_r = swap(x_r)
    fwd_a, bwd_a = shift(fwd_a, 1, 0), shift(bwd_a, -1, 0)
    right, left = pl.pallas_call(
        edge_kernel,
        out_shape=(plane, plane),
        in_specs=[vm, vm],
        out_specs=(vm, vm),
        compiler_params=params,
        cost_estimate=free,
        name="edges",
    )(v, scale)
    from_left, from_right = shift(right, 0, 1), shift(left, 0, -1)
    own_f, own_b = pl.pallas_call(
        lambda *refs: corner_kernel(*cut_b, *refs),
        out_shape=(planes(size_b, nb), planes(size_b, nb)),
        in_specs=[vm] * 4,
        out_specs=(vm, vm),
        compiler_params=params,
        cost_estimate=free,
        name="pack_b",
    )(v, scale, from_left, from_right)
    fwd_b, bwd_b = shift(own_f, 1, 0), shift(own_b, -1, 0)
    y_r = relay(
        pl.pallas_call(
            lambda *refs: relay_kernel(nz, *refs),
            out_shape=planes(size_r),
            in_specs=[vm, hbm, hbm],
            out_specs=vm,
            compiler_params=params,
            cost_estimate=free,
            name="relay",
        )(x_r, own_f, own_b)
    )
    fwd_c, bwd_c = pl.pallas_call(
        lambda *refs: more_kernel(*cut_c, *refs),
        out_shape=(planes(size_c), planes(size_c)),
        in_specs=[vm, vm, hbm, hbm],
        out_specs=(vm, vm),
        compiler_params=params,
        cost_estimate=free,
        name="pack_c",
    )(v, scale, fwd_a, bwd_a)
    fwd_c, bwd_c = shift(fwd_c, 1, 0), shift(bwd_c, -1, 0)
    inner, pay = pl.pallas_call(
        inner_kernel,
        out_shape=(works(nb), pay_shape),
        in_specs=[sm] + [vm] * 5,
        out_specs=(vm, vm),
        compiler_params=params,
        cost_estimate=free,
        name="inner",
    )(coupling_prev, v, scale, q, from_left, from_right)
    w_ab, pay, columns_f, columns_b = pl.pallas_call(
        lambda *refs: sum_kernel(((*cut_r, True), (*cut_a, False), (*cut_b, False)), 0, *refs),
        out_shape=(works(cut_b[1]), pay_shape, plane, plane),
        in_specs=[vm] * 12,
        out_specs=(vm,) * 4,
        compiler_params=params,
        cost_estimate=free,
        name="products",
    )(v, scale, inner, pay, x_r, y_r, fwd_a, bwd_a, fwd_b, bwd_b, fwd_b, bwd_b)
    w_c, pay = pl.pallas_call(
        lambda *refs: sum_kernel(((*cut_c, False),), cut_c[0], *refs),
        out_shape=(works(cut_c[1] - cut_c[0]), pay_shape),
        in_specs=[vm] * 9,
        out_specs=(vm, vm),
        compiler_params=params,
        cost_estimate=free,
        name="products_last",
    )(v, scale, inner, pay, fwd_c, bwd_c, columns_f, columns_b, w_ab)
    pay = jnp.broadcast_to(pay[None], (devices, 2, nt))
    pay = lax.all_to_all(pay, ("loop", "trans"), 0, 0)
    small = jax.ShapeDtypeStruct((nb, nb), f32)
    out, alpha, beta = pl.pallas_call(
        lambda *refs: last_kernel(count, *refs),
        out_shape=(works(nb), small, small),
        in_specs=[vm] * 4,
        out_specs=(hbm,) * 3,
        scratch_shapes=[
            VM((nb + nb * (nb + 1) // 2, 8, nt), f32),
            VM((nb, nc * nz, nt), f32),
            VM((nb, nb), f32),
            VM((nb, nb), f32),
            pltpu.SemaphoreType.DMA((6,)),
        ],
        compiler_params=params,
        cost_estimate=free,
        name="combine",
    )(pay, v, w_ab, w_c)
    return out.reshape(block_now.shape), alpha, beta


def solution(mesh):
    in_specs = (
        P(None, None, None, "loop", "trans"),
        P(None, None, None, "loop", "trans"),
        P(),
        P(None, "loop", "trans"),
        P(),
    )
    out_specs = (P(None, None, None, "loop", "trans"), P(), P())
    return jax.shard_map(local, mesh=mesh, in_specs=in_specs, out_specs=out_specs, check_vma=False)
```

```python
import jax
import jax.numpy as jnp
from jax import lax
from jax.experimental import pallas as pl
from jax.experimental.pallas import tpu as pltpu
from jax.sharding import PartitionSpec as P

VM = pltpu.VMEM
SM = pltpu.SMEM


def lane_ids(shape):
    return lax.broadcasted_iota(jnp.int32, shape, len(shape) - 1)


def row_ids(shape):
    return lax.broadcasted_iota(jnp.int32, shape, len(shape) - 2)


def roll_by(x, shift, axis):
    return pltpu.roll(x, shift % x.shape[axis], axis)


def cell_scale(mat, eps_ref):
    eps = jnp.full(mat.shape, eps_ref[0], jnp.float32)
    for level in range(1, eps_ref.shape[0]):
        eps = jnp.where(mat == level, eps_ref[level], eps)
    return 1.0 / jnp.sqrt(eps)


def z_next(x):
    n = x.shape[0]
    return jnp.where(row_ids(x.shape) == n - 1, 0.0, roll_by(x, -1, 0))


def z_prev(x):
    return jnp.where(row_ids(x.shape) == 0, 0.0, roll_by(x, 1, 0))


def forward_pair(uz, up, ut):
    lane = lane_ids(up.shape)
    up_next = jnp.where(lane == up.shape[1] - 1, 0.0, roll_by(up, -1, 1))
    return uz + (z_next(up) - up), ut + (up_next - up)


def even_trans():
    return lax.rem(lax.axis_index("trans"), 2) == 0


def odd_loop():
    return lax.rem(lax.axis_index("loop"), 2) == 1


def packed(v_ref, b, scale, fwd_ref, bwd_ref, at):
    nz = scale.shape[0]
    uz = v_ref[b, pl.ds(0, nz), :] * scale
    up = v_ref[b, pl.ds(nz, nz), :] * scale
    ut = v_ref[b, pl.ds(2 * nz, nz), :] * scale
    one, two = pl.ds(at * nz, nz), pl.ds((at + 1) * nz, nz)
    bwd_ref[one, :] = uz
    bwd_ref[two, :] = ut
    fwd_ref[one, :], fwd_ref[two, :] = forward_pair(uz, up, ut)


def first_kernel(
    cut_r, cut_a, v_hbm, mat_hbm, eps_hbm, x_ref, fwd_ref, bwd_ref, scale_ref, v_ref, mat_ref, eps_ref, sems
):
    copies = [
        pltpu.make_async_copy(eps_hbm, eps_ref, sems.at[0]),
        pltpu.make_async_copy(mat_hbm, mat_ref, sems.at[1]),
    ]
    for b in range(v_ref.shape[0]):
        copies.append(pltpu.make_async_copy(v_hbm.at[b], v_ref.at[b], sems.at[2 + b]))
    for copy in copies:
        copy.start()
    copies[0].wait()
    copies[1].wait()
    scale = cell_scale(mat_ref[...], eps_ref)
    scale_ref[...] = scale
    nz = scale.shape[0]
    for m, b in enumerate(range(*cut_r)):
        copies[2 + b].wait()
        for c in range(3):
            x_ref[pl.ds((3 * m + c) * nz, nz), :] = v_ref[b, pl.ds(c * nz, nz), :] * scale
    for m, b in enumerate(range(*cut_a)):
        copies[2 + b].wait()
        packed(v_ref, b, scale, fwd_ref, bwd_ref, 2 * m)


def relay_kernel(nz, x_ref, after_f_ref, after_b_ref, y_ref):
    odd = odd_loop()
    count = x_ref.shape[0] // (3 * nz)

    def comps(m):
        return [x_ref[pl.ds((3 * m + c) * nz, nz), :] for c in range(3)]

    def store(m, pair):
        y_ref[pl.ds(2 * m * nz, nz), :] = pair[0]
        y_ref[pl.ds((2 * m + 1) * nz, nz), :] = pair[1]

    @pl.when(odd)
    def _():
        for m in range(count):
            store(m, comps(m)[::2])

    @pl.when(jnp.logical_not(odd))
    def _():
        for m in range(count):
            store(m, forward_pair(*comps(m)))


def edge_kernel(v_ref, scale_ref, near_ref, far_ref):
    scale = scale_ref[...]
    nz = scale.shape[0]
    lane = lane_ids(scale.shape)
    right = jnp.zeros_like(scale)
    left = jnp.zeros_like(scale)
    for b in range(v_ref.shape[0]):
        for c in range(3):
            u = v_ref[b, pl.ds(c * nz, nz), :] * scale
            spot = v_ref.shape[0] * c + b
            right = jnp.where(lane == spot, roll_by(u, spot + 1, 1), right)
            left = jnp.where(lane == spot, roll_by(u, spot, 1), left)
    even = even_trans()
    near_ref[...] = jnp.where(even, right, left)
    far_ref[...] = jnp.where(even, left, right)


def turned(x):
    pad = jnp.zeros((x.shape[1] - x.shape[0], x.shape[1]), x.dtype)
    return jnp.concatenate([x, pad], axis=0).T


def corner_kernel(begin, end, v_ref, scale_ref, near_ref, far_ref, fwd_ref, bwd_ref, fr_ref, fl_ref):
    scale = scale_ref[...]
    for b in range(begin, end):
        packed(v_ref, b, scale, fwd_ref, bwd_ref, 2 * (b - begin))
    nb = v_ref.shape[0]
    even = even_trans()
    near, far = near_ref[...], far_ref[...]
    from_left, from_right = jnp.where(even, far, near), jnp.where(even, near, far)
    fr_ref[...] = from_left
    fl_ref[...] = from_right
    rows = pl.ds(2 * (end - begin) * scale.shape[0], nb)
    fwd_ref[rows, :] = turned(from_right)[nb : 2 * nb, :]
    bwd_ref[rows, :] = turned(from_left)[2 * nb : 3 * nb, :]


def more_kernel(begin, end, v_ref, scale_ref, fwd_a_ref, bwd_a_ref, fwd_ref, bwd_ref):
    scale = scale_ref[...]
    for b in range(begin, end):
        packed(v_ref, b, scale, fwd_ref, bwd_ref, 2 * (b - begin))


def merge(a, b, dist):
    low = (row_ids(a.shape) & dist) == 0
    other = jnp.where(low, b, a)
    swapped = roll_by(other, dist, 0)
    if 2 * dist != a.shape[0]:
        swapped = jnp.where(low, roll_by(other, -dist, 0), swapped)
    return jnp.where(low, a, b) + swapped


def add_products(pairs, steps, group, pays, unroll=8):
    shape = pays[0].shape
    lane, row = lane_ids(shape), row_ids(shape)
    zero = jnp.zeros(shape, jnp.float32)
    for first in range(0, len(pairs), group):
        part = pairs[first : first + group]

        def body(r, accs):
            rows = pl.ds(pl.multiple_of(r * 8, 8), 8)
            got = {}
            for left, j, right, b, _ in part:
                for ref, i in ((left, j), (right, b)):
                    if (id(ref), i) not in got:
                        got[(id(ref), i)] = ref[i, rows, :]
            return tuple(
                acc + got[(id(left), j)] * got[(id(right), b)]
                for acc, (left, j, right, b, _) in zip(accs, part)
            )

        accs = list(lax.fori_loop(0, steps, body, tuple(zero for _ in part), unroll=unroll))
        for at in range(0, len(part), 8):
            eight = accs[at : at + 8]
            eight = eight + [zero] * (8 - len(eight))
            four = [merge(eight[i], eight[i + 4], 4) for i in range(4)]
            two = [merge(four[i], four[i + 2], 2) for i in range(2)]
            sums = jnp.sum(merge(two[0], two[1], 1), axis=1, keepdims=True)
            for line in range(len(pays)):
                hit = None
                for i, pair in enumerate(part[at : at + 8]):
                    for spot in sorted(pair[4]):
                        if spot[0] == line:
                            here = (row == i) & (lane == spot[1])
                            hit = here if hit is None else hit | here
                if hit is not None:
                    pays[line] = pays[line] + jnp.where(hit, sums, 0.0)
    return pays


def store_pays(pay_ref, pays, before=None):
    for line, pay in enumerate(pays):
        total = jnp.sum(pay, axis=0, keepdims=True)
        if before is not None:
            total = total + before[line : line + 1, :]
        pay_ref[line : line + 1, :] = total


def inner_kernel(coup_ref, v_ref, scale_ref, q_ref, fr_ref, fl_ref, l_ref, pay_ref):
    nb = v_ref.shape[0]
    nz = scale_ref.shape[0]

    def body(b, carry):
        scale = scale_ref[...]
        lane = lane_ids(scale.shape)
        last = scale.shape[1] - 1
        uz = v_ref[b, pl.ds(0, nz), :] * scale
        up = v_ref[b, pl.ds(nz, nz), :] * scale
        ut = v_ref[b, pl.ds(2 * nz, nz), :] * scale

        def prev(u, c):
            edge = pltpu.roll(fr_ref[...], (last + 1 - (nb * c + b)) % (last + 1), 1)
            return jnp.where(lane == 0, edge, roll_by(u, 1, 1))

        def nxt(u, c):
            edge = pltpu.roll(fl_ref[...], last - (nb * c + b), 1)
            return jnp.where(lane == last, edge, roll_by(u, -1, 1))

        dt_ut = ut - prev(ut, 2)
        up_next = nxt(up, 1)
        uz_next = nxt(uz, 0)
        im_z = (z_next(up) - up) + (z_next(dt_ut) - dt_ut) + 4.0 * uz - uz_next - prev(uz, 0)
        im_p = 4.0 * up - z_next(up) - z_prev(up) - up_next - prev(up, 1) - (uz - z_prev(uz)) - dt_ut
        im_t = (
            (uz_next - z_prev(uz_next)) - (uz - z_prev(uz)) + (up_next - up)
            + 4.0 * ut - z_next(ut) - z_prev(ut)
        )
        for c, im in enumerate((im_z, im_p, im_t)):
            rows = pl.ds(c * nz, nz)
            out = im * scale
            for k in range(nb):
                out = out - coup_ref[b, k] * q_ref[k, rows, :]
            l_ref[b, rows, :] = out
        return carry

    lax.fori_loop(0, nb, body, 0)
    zero = jnp.zeros((8, v_ref.shape[2]), jnp.float32)
    pairs = [(v_ref, j, v_ref, b, {(1, nb * j + b), (1, nb * b + j)}) for b in range(nb) for j in range(b + 1)]
    store_pays(pay_ref, add_products(pairs, v_ref.shape[1] // 8, 36, [zero, zero]))


def sum_kernel(cuts, begin, v_ref, scale_ref, l_ref, pay_in_ref, *refs):
    nb = v_ref.shape[0]
    nz, nt = scale_ref.shape
    end = cuts[-1][1]
    halos = refs[: 2 * len(cuts)]
    corners = refs[2 * len(cuts) : 2 * len(cuts) + 2]
    if begin == 0:
        w_ref, pay_ref, columns_f_ref, columns_b_ref = refs[-4:]
        for corner, columns_ref in zip(corners, (columns_f_ref, columns_b_ref)):
            columns_ref[...] = turned(corner[pl.ds(corner.shape[0] - nb, nb), :])[:nz, :]
    else:
        columns_f_ref, columns_b_ref = corners
        old, w_ref, pay_ref = refs[-3:]
    columns_f, columns_b = columns_f_ref[...], columns_b_ref[...]
    scale = scale_ref[...]
    lane = lane_ids(scale.shape)
    odd = odd_loop()
    for i, (low, high, relayed) in enumerate(cuts):
        fwd_ref, bwd_ref = halos[2 * i : 2 * i + 2]

        for m in range(high - low):
            b = low + m
            one, two = pl.ds(2 * m * nz, nz), pl.ds((2 * m + 1) * nz, nz)
            if relayed:
                xz, xp, xt = (fwd_ref[pl.ds((3 * m + c) * nz, nz), :] for c in range(3))
                y0, y1 = bwd_ref[one, :], bwd_ref[two, :]
                f0, f1 = forward_pair(xz, xp, xt)
                za, tb = jnp.where(odd, f0, y0), jnp.where(odd, f1, y1)
                uz, ut = jnp.where(odd, y0, xz), jnp.where(odd, y1, xt)
            else:
                za, tb = fwd_ref[one, :], fwd_ref[two, :]
                uz, ut = bwd_ref[one, :], bwd_ref[two, :]
            edge_b = roll_by(columns_b, -b, 1)
            edge_f = roll_by(columns_f, nt - 1 - b, 1)
            ut_prev = jnp.where(lane == 0, edge_b, roll_by(ut, 1, 1))
            tb = tb + jnp.where(lane == nt - 1, edge_f, 0.0)
            to = b - begin
            w_ref[to, pl.ds(0, nz), :] = l_ref[b, pl.ds(0, nz), :] - scale * (za + uz)
            div = (uz - z_prev(uz)) + (ut - ut_prev)
            w_ref[to, pl.ds(nz, nz), :] = l_ref[b, pl.ds(nz, nz), :] + scale * div
            w_ref[to, pl.ds(2 * nz, nz), :] = l_ref[b, pl.ds(2 * nz, nz), :] - scale * (tb + ut)

    ws = [(old, b) for b in range(begin)] + [(w_ref, b - begin) for b in range(begin, end)]
    pairs = []
    for b in range(begin, end):
        pairs += [(v_ref, j, *ws[b], {(0, nb * j + b), (1, nb * nb + nb * b + j)}) for j in range(nb)]
        pairs += [(*ws[j], *ws[b], {(0, nb * nb + nb * j + b), (0, nb * nb + nb * b + j)}) for j in range(b + 1)]
    zero = jnp.zeros((8, nt), jnp.float32)
    store_pays(pay_ref, add_products(pairs, v_ref.shape[1] // 8, 42, [zero, zero]), pay_in_ref)


def lane_at(x, k):
    return jnp.broadcast_to(x[:, k : k + 1], x.shape)


def row_at(x, k):
    return jnp.broadcast_to(x[k : k + 1, :], x.shape)


def matrix_of(line, offset, nb):
    x = jnp.broadcast_to(line, (8, line.shape[1]))
    row = row_ids(x.shape)
    out = roll_by(x, -offset, 1)
    for i in range(1, nb):
        out = jnp.where(row == i, roll_by(x, -offset - nb * i, 1), out)
    return out


def last_kernel(count, pay_ref, v_ref, *refs):
    w_refs = refs[:-8]
    out_hbm, alpha_hbm, beta_hbm, coef_ref, out_ref, alpha_ref, beta_ref, sems = refs[-8:]
    nb = v_ref.shape[0]
    total = jnp.sum(pay_ref[...], axis=0)
    proj = matrix_of(total[0:1], 0, nb)
    ww = matrix_of(total[0:1], nb * nb, nb)
    vv = matrix_of(total[1:2], 0, nb)
    alpha = proj / count
    alpha_t = matrix_of(total[1:2], nb * nb, nb) / count
    alpha_ref[...] = alpha[:, :nb]
    copies = [pltpu.make_async_copy(alpha_ref, alpha_hbm, sems.at[0])]
    copies[0].start()
    lane = lane_ids(proj.shape)
    row = row_ids(proj.shape)
    cross = jnp.zeros_like(proj)
    half = jnp.zeros_like(proj)
    for j in range(nb):
        coef_ref[j] = lane_at(alpha_t, j)
        cross = cross + lane_at(alpha_t, j) * row_at(proj, j)
        half = half + lane_at(vv, j) * row_at(alpha, j)
    quad = jnp.zeros_like(proj)
    for k in range(nb):
        quad = quad + lane_at(alpha_t, k) * row_at(half, k)
    gram = ((ww - cross) + (quad - cross)) / count
    ws = [(w, i) for w in w_refs for i in range(w.shape[0])]
    blocks = v_ref.shape[1] // 8
    mat = {}
    for i in range(nb):
        line = row_at(gram, i)
        for j in range(i + 1):
            mat[i, j] = lane_at(line, j)
    low, inv = {}, {}
    beta = jnp.zeros_like(proj)
    for k in range(nb):
        root = lax.rsqrt(mat[k, k])
        low[k, k] = mat[k, k] * root
        for i in range(k + 1, nb):
            low[i, k] = mat[i, k] * root
        for i in range(k + 1, nb):
            for j in range(k + 1, i + 1):
                mat[i, j] = mat[i, j] - low[i, k] * low[j, k]
        for i in range(k, nb):
            beta = jnp.where((row == k) & (lane == i), low[i, k], beta)
        inv[k, k] = root
        for j in range(k):
            acc = low[k, j] * inv[j, j]
            for q in range(j + 1, k):
                acc = acc + low[k, q] * inv[q, j]
            inv[k, j] = -(root * acc)
        for j in range(k + 1):
            coef_ref[nb + k * (k + 1) // 2 + j] = inv[k, j]
        for r in range(k * blocks // nb, (k + 1) * blocks // nb):
            rows = pl.ds(8 * r, 8)
            vs = [v_ref[j, rows, :] for j in range(nb)]
            for b, (w_ref, i) in enumerate(ws):
                acc = w_ref[i, rows, :]
                for j in range(nb):
                    acc = acc - coef_ref[j, pl.ds(b, 1), :] * vs[j]
                out_ref[b, rows, :] = acc
    beta_ref[...] = beta[:, :nb]
    copies.append(pltpu.make_async_copy(beta_ref, beta_hbm, sems.at[1]))
    copies[1].start()
    step = 16
    pieces = sems.shape[0] - 2
    length = v_ref.shape[1] // pieces
    for piece in range(pieces):
        base = piece * length

        def body(r, carry):
            rows = pl.ds(pl.multiple_of(base + r * step, step), step)
            xs = [out_ref[j, rows, :] for j in range(nb)]
            for b in range(nb):
                at = nb + b * (b + 1) // 2
                acc = coef_ref[at, pl.ds(0, 1), :] * xs[0]
                for j in range(1, b + 1):
                    acc = acc + coef_ref[at + j, pl.ds(0, 1), :] * xs[j]
                out_ref[b, rows, :] = acc
            return carry

        lax.fori_loop(0, length // step, body, 0)
        part = pl.ds(base, length)
        copy = pltpu.make_async_copy(out_ref.at[:, part, :], out_hbm.at[:, part, :], sems.at[2 + piece])
        copy.start()
        copies.append(copy)
    for copy in copies:
        copy.wait()


def shift(x, loop_by):
    count = lax.axis_size("loop")
    return lax.ppermute(x, "loop", [(i, (i + loop_by) % count) for i in range(count)])


def trans_swaps(near, far):
    count = lax.axis_size("trans")
    pairs = [(t, t + (-1 if t % 2 == 0 else 1)) for t in range(1, count - 1)]
    return lax.ppermute(near, "trans", [(t, t ^ 1) for t in range(count)]), lax.ppermute(far, "trans", pairs)


def swap(x):
    return lax.ppermute(x, "loop", [(i, i ^ 1) for i in range(lax.axis_size("loop"))])


def relay(x):
    count = lax.axis_size("loop")
    return lax.ppermute(x, "loop", [(i, (i + (-2 if i % 2 else 2)) % count) for i in range(count)])


def local(block_now, block_prev, coupling_prev, material, permittivity):
    nb, nc, nz, _, nt = block_now.shape
    f32 = jnp.float32
    devices = lax.axis_size("loop") * lax.axis_size("trans")
    count = float(nc * nz * nt * devices)
    v = block_now.reshape(nb, nc * nz, nt)
    q = block_prev.reshape(nb, nc * nz, nt)
    mat = material.reshape(nz, nt)
    vm, sm = pl.BlockSpec(memory_space=VM), pl.BlockSpec(memory_space=SM)
    hbm = pl.BlockSpec(memory_space=pltpu.HBM)
    params = pltpu.CompilerParams(vmem_limit_bytes=32 * 2**20)
    free = pl.CostEstimate(flops=0, bytes_accessed=0, transcendentals=0)
    plane = jax.ShapeDtypeStruct((nz, nt), f32)
    pay_shape = jax.ShapeDtypeStruct((2, nt), f32)
    assert lax.axis_size("loop") % 2 == 0 and lax.axis_size("trans") % 2 == 0
    marks = (0, nb * 3 // 8, nb * 5 // 8, nb - 1, nb)
    cut_r, cut_a, cut_b, cut_c = zip(marks[:-1], marks[1:])

    def planes(n, more=0):
        return jax.ShapeDtypeStruct((n * nz + more, nt), f32)

    def works(n):
        return jax.ShapeDtypeStruct((n, nc * nz, nt), f32)

    size_r, size_a, size_b, size_c = (2 * (c[1] - c[0]) for c in (cut_r, cut_a, cut_b, cut_c))
    x_r, fwd_a, bwd_a, scale = pl.pallas_call(
        lambda *refs: first_kernel(cut_r, cut_a, *refs),
        out_shape=(planes(size_r * 3 // 2), planes(size_a), planes(size_a), plane),
        in_specs=[hbm] * 3,
        out_specs=(vm,) * 4,
        scratch_shapes=[
            VM((cut_a[1], nc * nz, nt), f32),
            VM((nz, nt), jnp.int32),
            SM(permittivity.shape, f32),
            pltpu.SemaphoreType.DMA((2 + cut_a[1],)),
        ],
        compiler_params=params,
        cost_estimate=free,
        name="first",
    )(*(pltpu.with_memory_space_constraint(x, pltpu.HBM) for x in (v, mat, permittivity)))
    x_r = swap(x_r)
    fwd_a, bwd_a = shift(fwd_a, 1), shift(bwd_a, -1)
    near, far = pl.pallas_call(
        edge_kernel,
        out_shape=(plane, plane),
        in_specs=[vm, vm],
        out_specs=(vm, vm),
        compiler_params=params,
        cost_estimate=free,
        name="edges",
    )(v, scale)
    near, far = trans_swaps(near, far)
    own_f, own_b, from_left, from_right = pl.pallas_call(
        lambda *refs: corner_kernel(*cut_b, *refs),
        out_shape=(planes(size_b, nb), planes(size_b, nb), plane, plane),
        in_specs=[vm] * 4,
        out_specs=(vm,) * 4,
        compiler_params=params,
        cost_estimate=free,
        name="pack_b",
    )(v, scale, near, far)
    fwd_b, bwd_b = shift(own_f, 1), shift(own_b, -1)
    y_r = relay(
        pl.pallas_call(
            lambda *refs: relay_kernel(nz, *refs),
            out_shape=planes(size_r),
            in_specs=[vm, hbm, hbm],
            out_specs=vm,
            compiler_params=params,
            cost_estimate=free,
            name="relay",
        )(x_r, own_f, own_b)
    )
    fwd_c, bwd_c = pl.pallas_call(
        lambda *refs: more_kernel(*cut_c, *refs),
        out_shape=(planes(size_c), planes(size_c)),
        in_specs=[vm, vm, hbm, hbm],
        out_specs=(vm, vm),
        compiler_params=params,
        cost_estimate=free,
        name="pack_c",
    )(v, scale, fwd_a, bwd_a)
    fwd_c, bwd_c = shift(fwd_c, 1), shift(bwd_c, -1)
    inner, pay = pl.pallas_call(
        inner_kernel,
        out_shape=(works(nb), pay_shape),
        in_specs=[sm] + [vm] * 5,
        out_specs=(vm, vm),
        compiler_params=params,
        cost_estimate=free,
        name="inner",
    )(coupling_prev, v, scale, q, from_left, from_right)
    w_ab, pay, columns_f, columns_b = pl.pallas_call(
        lambda *refs: sum_kernel(((*cut_r, True), (*cut_a, False), (*cut_b, False)), 0, *refs),
        out_shape=(works(cut_b[1]), pay_shape, plane, plane),
        in_specs=[vm] * 12,
        out_specs=(vm,) * 4,
        compiler_params=params,
        cost_estimate=free,
        name="products",
    )(v, scale, inner, pay, x_r, y_r, fwd_a, bwd_a, fwd_b, bwd_b, fwd_b, bwd_b)
    w_c, pay = pl.pallas_call(
        lambda *refs: sum_kernel(((*cut_c, False),), cut_c[0], *refs),
        out_shape=(works(cut_c[1] - cut_c[0]), pay_shape),
        in_specs=[vm] * 9,
        out_specs=(vm, vm),
        compiler_params=params,
        cost_estimate=free,
        name="products_last",
    )(v, scale, inner, pay, fwd_c, bwd_c, columns_f, columns_b, w_ab)
    pay = jnp.broadcast_to(pay[None], (devices, 2, nt))
    pay = lax.all_to_all(pay, ("loop", "trans"), 0, 0)
    small = jax.ShapeDtypeStruct((nb, nb), f32)
    out, alpha, beta = pl.pallas_call(
        lambda *refs: last_kernel(count, *refs),
        out_shape=(works(nb), small, small),
        in_specs=[vm] * 4,
        out_specs=(hbm,) * 3,
        scratch_shapes=[
            VM((nb + nb * (nb + 1) // 2, 8, nt), f32),
            VM((nb, nc * nz, nt), f32),
            VM((nb, nb), f32),
            VM((nb, nb), f32),
            pltpu.SemaphoreType.DMA((6,)),
        ],
        compiler_params=params,
        cost_estimate=free,
        name="combine",
    )(pay, v, w_ab, w_c)
    return out.reshape(block_now.shape), alpha, beta


def solution(mesh):
    in_specs = (
        P(None, None, None, "loop", "trans"),
        P(None, None, None, "loop", "trans"),
        P(),
        P(None, "loop", "trans"),
        P(),
    )
    out_specs = (P(None, None, None, "loop", "trans"), P(), P())
    return jax.shard_map(local, mesh=mesh, in_specs=in_specs, out_specs=out_specs, check_vma=False)
```

```python
import jax
import jax.numpy as jnp
from jax import lax
from jax.experimental import pallas as pl
from jax.experimental.pallas import tpu as pltpu
from jax.sharding import PartitionSpec as P

VM = pltpu.VMEM
SM = pltpu.SMEM


def lane_ids(shape):
    return lax.broadcasted_iota(jnp.int32, shape, len(shape) - 1)


def row_ids(shape):
    return lax.broadcasted_iota(jnp.int32, shape, len(shape) - 2)


def roll_by(x, shift, axis):
    return pltpu.roll(x, shift % x.shape[axis], axis)


def cell_scale(mat, eps_ref):
    eps = jnp.full(mat.shape, eps_ref[0], jnp.float32)
    for level in range(1, eps_ref.shape[0]):
        eps = jnp.where(mat == level, eps_ref[level], eps)
    return 1.0 / jnp.sqrt(eps)


def z_next(x):
    n = x.shape[0]
    return jnp.where(row_ids(x.shape) == n - 1, 0.0, roll_by(x, -1, 0))


def z_prev(x):
    return jnp.where(row_ids(x.shape) == 0, 0.0, roll_by(x, 1, 0))


def forward_pair(uz, up, ut):
    lane = lane_ids(up.shape)
    up_next = jnp.where(lane == up.shape[1] - 1, 0.0, roll_by(up, -1, 1))
    return uz + (z_next(up) - up), ut + (up_next - up)


def even_trans():
    return lax.rem(lax.axis_index("trans"), 2) == 0


def odd_loop():
    return lax.rem(lax.axis_index("loop"), 2) == 1


def packed(v_ref, b, scale, fwd_ref, bwd_ref, at):
    nz = scale.shape[0]
    uz = v_ref[b, pl.ds(0, nz), :] * scale
    up = v_ref[b, pl.ds(nz, nz), :] * scale
    ut = v_ref[b, pl.ds(2 * nz, nz), :] * scale
    one, two = pl.ds(at * nz, nz), pl.ds((at + 1) * nz, nz)
    bwd_ref[one, :] = uz
    bwd_ref[two, :] = ut
    fwd_ref[one, :], fwd_ref[two, :] = forward_pair(uz, up, ut)


def raw(v_ref, b, scale, out_ref, at):
    nz = scale.shape[0]
    for c in range(3):
        out_ref[pl.ds((at + c) * nz, nz), :] = v_ref[b, pl.ds(c * nz, nz), :] * scale


def first_kernel(cuts, v_hbm, mat_hbm, eps_hbm, *refs):
    outs, (scale_ref, v_ref, mat_ref, eps_ref, sems) = refs[: len(cuts)], refs[len(cuts) :]
    copies = [
        pltpu.make_async_copy(eps_hbm, eps_ref, sems.at[0]),
        pltpu.make_async_copy(mat_hbm, mat_ref, sems.at[1]),
    ]
    for b in range(v_ref.shape[0]):
        copies.append(pltpu.make_async_copy(v_hbm.at[b], v_ref.at[b], sems.at[2 + b]))
    for copy in copies:
        copy.start()
    copies[0].wait()
    copies[1].wait()
    scale = cell_scale(mat_ref[...], eps_ref)
    scale_ref[...] = scale
    for cut, out_ref in zip(cuts, outs):
        for m, b in enumerate(range(*cut)):
            copies[2 + b].wait()
            raw(v_ref, b, scale, out_ref, 3 * m)


def relay_kernel(nz, nb, x_ref, *refs):
    y_ref = refs[-1]
    odd = odd_loop()
    count = x_ref.shape[0] // (3 * nz)
    with_rows = x_ref.shape[0] > 3 * nz * count

    def comps(m):
        return [x_ref[pl.ds((3 * m + c) * nz, nz), :] for c in range(3)]

    def store(pairs, side):
        for m, pair in enumerate(pairs):
            y_ref[pl.ds(2 * m * nz, nz), :] = pair[0]
            y_ref[pl.ds((2 * m + 1) * nz, nz), :] = pair[1]
        if with_rows:
            y_ref[pl.ds(2 * count * nz, nb), :] = x_ref[pl.ds(3 * count * nz + side * nb, nb), :]

    @pl.when(odd)
    def _():
        store((comps(m)[::2] for m in range(count)), 1)

    @pl.when(jnp.logical_not(odd))
    def _():
        store((forward_pair(*comps(m)) for m in range(count)), 0)


def edge_kernel(v_ref, scale_ref, near_ref, far_ref):
    scale = scale_ref[...]
    nz = scale.shape[0]
    lane = lane_ids(scale.shape)
    right = jnp.zeros_like(scale)
    left = jnp.zeros_like(scale)
    for b in range(v_ref.shape[0]):
        for c in range(3):
            u = v_ref[b, pl.ds(c * nz, nz), :] * scale
            spot = v_ref.shape[0] * c + b
            right = jnp.where(lane == spot, roll_by(u, spot + 1, 1), right)
            left = jnp.where(lane == spot, roll_by(u, spot, 1), left)
    even = even_trans()
    near_ref[...] = jnp.where(even, right, left)
    far_ref[...] = jnp.where(even, left, right)


def turned(x):
    pad = jnp.zeros((x.shape[1] - x.shape[0], x.shape[1]), x.dtype)
    return jnp.concatenate([x, pad], axis=0).T


def corner_kernel(begin, end, v_ref, scale_ref, near_ref, far_ref, x_ref, fr_ref, fl_ref):
    scale = scale_ref[...]
    nb = v_ref.shape[0]
    for m, b in enumerate(range(begin, end)):
        raw(v_ref, b, scale, x_ref, 3 * m)
    even = even_trans()
    near, far = near_ref[...], far_ref[...]
    from_left, from_right = jnp.where(even, far, near), jnp.where(even, near, far)
    fr_ref[...] = from_left
    fl_ref[...] = from_right
    at = 3 * (end - begin) * scale.shape[0]
    x_ref[pl.ds(at, nb), :] = turned(from_right)[nb : 2 * nb, :]
    x_ref[pl.ds(at + nb, nb), :] = turned(from_left)[2 * nb : 3 * nb, :]


def direct_kernel(begin, end, v_ref, scale_ref, after_ref, fwd_ref, bwd_ref):
    scale = scale_ref[...]
    for b in range(begin, end):
        packed(v_ref, b, scale, fwd_ref, bwd_ref, 2 * (b - begin))


def merge(a, b, dist):
    low = (row_ids(a.shape) & dist) == 0
    other = jnp.where(low, b, a)
    swapped = roll_by(other, dist, 0)
    if 2 * dist != a.shape[0]:
        swapped = jnp.where(low, roll_by(other, -dist, 0), swapped)
    return jnp.where(low, a, b) + swapped


def add_products(pairs, steps, group, pays, unroll=8):
    shape = pays[0].shape
    lane, row = lane_ids(shape), row_ids(shape)
    zero = jnp.zeros(shape, jnp.float32)
    for first in range(0, len(pairs), group):
        part = pairs[first : first + group]

        def body(r, accs):
            rows = pl.ds(pl.multiple_of(r * 8, 8), 8)
            got = {}
            for left, j, right, b, _ in part:
                for ref, i in ((left, j), (right, b)):
                    if (id(ref), i) not in got:
                        got[(id(ref), i)] = ref[i, rows, :]
            return tuple(
                acc + got[(id(left), j)] * got[(id(right), b)]
                for acc, (left, j, right, b, _) in zip(accs, part)
            )

        accs = list(lax.fori_loop(0, steps, body, tuple(zero for _ in part), unroll=unroll))
        for at in range(0, len(part), 8):
            eight = accs[at : at + 8]
            eight = eight + [zero] * (8 - len(eight))
            four = [merge(eight[i], eight[i + 4], 4) for i in range(4)]
            two = [merge(four[i], four[i + 2], 2) for i in range(2)]
            sums = jnp.sum(merge(two[0], two[1], 1), axis=1, keepdims=True)
            for line in range(len(pays)):
                hit = None
                for i, pair in enumerate(part[at : at + 8]):
                    for spot in sorted(pair[4]):
                        if spot[0] == line:
                            here = (row == i) & (lane == spot[1])
                            hit = here if hit is None else hit | here
                if hit is not None:
                    pays[line] = pays[line] + jnp.where(hit, sums, 0.0)
    return pays


def store_pays(pay_ref, pays, before=None):
    for line, pay in enumerate(pays):
        total = jnp.sum(pay, axis=0, keepdims=True)
        if before is not None:
            total = total + before[line : line + 1, :]
        pay_ref[line : line + 1, :] = total


def inner_kernel(coup_ref, v_ref, scale_ref, q_ref, fr_ref, fl_ref, l_ref, pay_ref):
    nb = v_ref.shape[0]
    nz = scale_ref.shape[0]

    def body(b, carry):
        scale = scale_ref[...]
        lane = lane_ids(scale.shape)
        last = scale.shape[1] - 1
        uz = v_ref[b, pl.ds(0, nz), :] * scale
        up = v_ref[b, pl.ds(nz, nz), :] * scale
        ut = v_ref[b, pl.ds(2 * nz, nz), :] * scale

        def prev(u, c):
            edge = pltpu.roll(fr_ref[...], (last + 1 - (nb * c + b)) % (last + 1), 1)
            return jnp.where(lane == 0, edge, roll_by(u, 1, 1))

        def nxt(u, c):
            edge = pltpu.roll(fl_ref[...], last - (nb * c + b), 1)
            return jnp.where(lane == last, edge, roll_by(u, -1, 1))

        dt_ut = ut - prev(ut, 2)
        up_next = nxt(up, 1)
        uz_next = nxt(uz, 0)
        im_z = (z_next(up) - up) + (z_next(dt_ut) - dt_ut) + 4.0 * uz - uz_next - prev(uz, 0)
        im_p = 4.0 * up - z_next(up) - z_prev(up) - up_next - prev(up, 1) - (uz - z_prev(uz)) - dt_ut
        im_t = (
            (uz_next - z_prev(uz_next)) - (uz - z_prev(uz)) + (up_next - up)
            + 4.0 * ut - z_next(ut) - z_prev(ut)
        )
        for c, im in enumerate((im_z, im_p, im_t)):
            rows = pl.ds(c * nz, nz)
            out = im * scale
            for k in range(nb):
                out = out - coup_ref[b, k] * q_ref[k, rows, :]
            l_ref[b, rows, :] = out
        return carry

    lax.fori_loop(0, nb, body, 0)
    zero = jnp.zeros((8, v_ref.shape[2]), jnp.float32)
    pairs = [(v_ref, j, v_ref, b, {(1, nb * j + b), (1, nb * b + j)}) for b in range(nb) for j in range(b + 1)]
    store_pays(pay_ref, add_products(pairs, v_ref.shape[1] // 8, 36, [zero, zero]))


def sum_kernel(cuts, begin, v_ref, scale_ref, l_ref, pay_in_ref, *refs):
    nb = v_ref.shape[0]
    nz, nt = scale_ref.shape
    end = cuts[-1][1]
    halos = refs[: 2 * len(cuts)]
    corners = refs[2 * len(cuts) : 2 * len(cuts) + 2]
    odd = odd_loop()
    if begin == 0:
        w_ref, pay_ref, columns_f_ref, columns_b_ref = refs[-4:]
        near, far = (ref[pl.ds(ref.shape[0] - n, n), :] for ref, n in zip(corners, (2 * nb, nb)))
        columns_f_ref[...] = turned(jnp.where(odd, near[:nb], far))[:nz, :]
        columns_b_ref[...] = turned(jnp.where(odd, far, near[nb:]))[:nz, :]
    else:
        columns_f_ref, columns_b_ref = corners
        old, w_ref, pay_ref = refs[-3:]
    columns_f, columns_b = columns_f_ref[...], columns_b_ref[...]
    scale = scale_ref[...]
    lane = lane_ids(scale.shape)
    for i, (low, high, relayed) in enumerate(cuts):
        fwd_ref, bwd_ref = halos[2 * i : 2 * i + 2]

        for m in range(high - low):
            b = low + m
            one, two = pl.ds(2 * m * nz, nz), pl.ds((2 * m + 1) * nz, nz)
            if relayed:
                xz, xp, xt = (fwd_ref[pl.ds((3 * m + c) * nz, nz), :] for c in range(3))
                y0, y1 = bwd_ref[one, :], bwd_ref[two, :]
                f0, f1 = forward_pair(xz, xp, xt)
                za, tb = jnp.where(odd, f0, y0), jnp.where(odd, f1, y1)
                uz, ut = jnp.where(odd, y0, xz), jnp.where(odd, y1, xt)
            else:
                za, tb = fwd_ref[one, :], fwd_ref[two, :]
                uz, ut = bwd_ref[one, :], bwd_ref[two, :]
            edge_b = roll_by(columns_b, -b, 1)
            edge_f = roll_by(columns_f, nt - 1 - b, 1)
            ut_prev = jnp.where(lane == 0, edge_b, roll_by(ut, 1, 1))
            tb = tb + jnp.where(lane == nt - 1, edge_f, 0.0)
            to = b - begin
            w_ref[to, pl.ds(0, nz), :] = l_ref[b, pl.ds(0, nz), :] - scale * (za + uz)
            div = (uz - z_prev(uz)) + (ut - ut_prev)
            w_ref[to, pl.ds(nz, nz), :] = l_ref[b, pl.ds(nz, nz), :] + scale * div
            w_ref[to, pl.ds(2 * nz, nz), :] = l_ref[b, pl.ds(2 * nz, nz), :] - scale * (tb + ut)

    ws = [(old, b) for b in range(begin)] + [(w_ref, b - begin) for b in range(begin, end)]
    pairs = []
    for b in range(begin, end):
        pairs += [(v_ref, j, *ws[b], {(0, nb * j + b), (1, nb * nb + nb * b + j)}) for j in range(nb)]
        pairs += [(*ws[j], *ws[b], {(0, nb * nb + nb * j + b), (0, nb * nb + nb * b + j)}) for j in range(b + 1)]
    zero = jnp.zeros((8, nt), jnp.float32)
    store_pays(pay_ref, add_products(pairs, v_ref.shape[1] // 8, 42, [zero, zero]), pay_in_ref)


def lane_at(x, k):
    return jnp.broadcast_to(x[:, k : k + 1], x.shape)


def row_at(x, k):
    return jnp.broadcast_to(x[k : k + 1, :], x.shape)


def matrix_of(line, offset, nb):
    x = jnp.broadcast_to(line, (8, line.shape[1]))
    row = row_ids(x.shape)
    out = roll_by(x, -offset, 1)
    for i in range(1, nb):
        out = jnp.where(row == i, roll_by(x, -offset - nb * i, 1), out)
    return out


def last_kernel(count, pay_ref, v_ref, *refs):
    w_refs = refs[:-8]
    out_hbm, alpha_hbm, beta_hbm, coef_ref, out_ref, alpha_ref, beta_ref, sems = refs[-8:]
    nb = v_ref.shape[0]
    total = jnp.sum(pay_ref[...], axis=0)
    proj = matrix_of(total[0:1], 0, nb)
    ww = matrix_of(total[0:1], nb * nb, nb)
    vv = matrix_of(total[1:2], 0, nb)
    alpha = proj / count
    alpha_t = matrix_of(total[1:2], nb * nb, nb) / count
    alpha_ref[...] = alpha[:, :nb]
    copies = [pltpu.make_async_copy(alpha_ref, alpha_hbm, sems.at[0])]
    copies[0].start()
    lane = lane_ids(proj.shape)
    row = row_ids(proj.shape)
    cross = jnp.zeros_like(proj)
    half = jnp.zeros_like(proj)
    for j in range(nb):
        coef_ref[j] = lane_at(alpha_t, j)
        cross = cross + lane_at(alpha_t, j) * row_at(proj, j)
        half = half + lane_at(vv, j) * row_at(alpha, j)
    quad = jnp.zeros_like(proj)
    for k in range(nb):
        quad = quad + lane_at(alpha_t, k) * row_at(half, k)
    gram = ((ww - cross) + (quad - cross)) / count
    ws = [(w, i) for w in w_refs for i in range(w.shape[0])]
    blocks = v_ref.shape[1] // 8
    mat = {}
    for i in range(nb):
        line = row_at(gram, i)
        for j in range(i + 1):
            mat[i, j] = lane_at(line, j)
    low, inv = {}, {}
    beta = jnp.zeros_like(proj)
    for k in range(nb):
        root = lax.rsqrt(mat[k, k])
        low[k, k] = mat[k, k] * root
        for i in range(k + 1, nb):
            low[i, k] = mat[i, k] * root
        for i in range(k + 1, nb):
            for j in range(k + 1, i + 1):
                mat[i, j] = mat[i, j] - low[i, k] * low[j, k]
        for i in range(k, nb):
            beta = jnp.where((row == k) & (lane == i), low[i, k], beta)
        inv[k, k] = root
        for j in range(k):
            acc = low[k, j] * inv[j, j]
            for q in range(j + 1, k):
                acc = acc + low[k, q] * inv[q, j]
            inv[k, j] = -(root * acc)
        for j in range(k + 1):
            coef_ref[nb + k * (k + 1) // 2 + j] = inv[k, j]
        for r in range(k * blocks // nb, (k + 1) * blocks // nb):
            rows = pl.ds(8 * r, 8)
            vs = [v_ref[j, rows, :] for j in range(nb)]
            for b, (w_ref, i) in enumerate(ws):
                acc = w_ref[i, rows, :]
                for j in range(nb):
                    acc = acc - coef_ref[j, pl.ds(b, 1), :] * vs[j]
                out_ref[b, rows, :] = acc
    beta_ref[...] = beta[:, :nb]
    copies.append(pltpu.make_async_copy(beta_ref, beta_hbm, sems.at[1]))
    copies[1].start()
    step = 16
    pieces = sems.shape[0] - 2
    length = v_ref.shape[1] // pieces
    for piece in range(pieces):
        base = piece * length

        def body(r, carry):
            rows = pl.ds(pl.multiple_of(base + r * step, step), step)
            xs = [out_ref[j, rows, :] for j in range(nb)]
            for b in range(nb):
                at = nb + b * (b + 1) // 2
                acc = coef_ref[at, pl.ds(0, 1), :] * xs[0]
                for j in range(1, b + 1):
                    acc = acc + coef_ref[at + j, pl.ds(0, 1), :] * xs[j]
                out_ref[b, rows, :] = acc
            return carry

        lax.fori_loop(0, length // step, body, 0)
        part = pl.ds(base, length)
        copy = pltpu.make_async_copy(out_ref.at[:, part, :], out_hbm.at[:, part, :], sems.at[2 + piece])
        copy.start()
        copies.append(copy)
    for copy in copies:
        copy.wait()


def shift(x, loop_by):
    count = lax.axis_size("loop")
    return lax.ppermute(x, "loop", [(i, (i + loop_by) % count) for i in range(count)])


def trans_swaps(near, far):
    count = lax.axis_size("trans")
    pairs = [(t, t + (-1 if t % 2 == 0 else 1)) for t in range(1, count - 1)]
    return lax.ppermute(near, "trans", [(t, t ^ 1) for t in range(count)]), lax.ppermute(far, "trans", pairs)


def swap(x):
    return lax.ppermute(x, "loop", [(i, i ^ 1) for i in range(lax.axis_size("loop"))])


def relay(x):
    count = lax.axis_size("loop")
    return lax.ppermute(x, "loop", [(i, (i + (-2 if i % 2 else 2)) % count) for i in range(count)])


def local(block_now, block_prev, coupling_prev, material, permittivity):
    nb, nc, nz, _, nt = block_now.shape
    f32 = jnp.float32
    devices = lax.axis_size("loop") * lax.axis_size("trans")
    count = float(nc * nz * nt * devices)
    v = block_now.reshape(nb, nc * nz, nt)
    q = block_prev.reshape(nb, nc * nz, nt)
    mat = material.reshape(nz, nt)
    vm, sm = pl.BlockSpec(memory_space=VM), pl.BlockSpec(memory_space=SM)
    hbm = pl.BlockSpec(memory_space=pltpu.HBM)
    params = pltpu.CompilerParams(vmem_limit_bytes=32 * 2**20)
    free = pl.CostEstimate(flops=0, bytes_accessed=0, transcendentals=0)
    plane = jax.ShapeDtypeStruct((nz, nt), f32)
    pay_shape = jax.ShapeDtypeStruct((2, nt), f32)
    assert lax.axis_size("loop") % 2 == 0 and lax.axis_size("trans") % 2 == 0
    marks = (0, nb * 3 // 8, nb * 5 // 8, nb)
    cut_a, cut_c, cut_d = zip(marks[:-1], marks[1:])

    def planes(n, more=0):
        return jax.ShapeDtypeStruct((n * nz + more, nt), f32)

    def works(n):
        return jax.ShapeDtypeStruct((n, nc * nz, nt), f32)

    size_a, size_c, size_d = (c[1] - c[0] for c in (cut_a, cut_c, cut_d))
    x_a, scale = pl.pallas_call(
        lambda *refs: first_kernel((cut_a,), *refs),
        out_shape=(planes(3 * size_a), plane),
        in_specs=[hbm] * 3,
        out_specs=(vm,) * 2,
        scratch_shapes=[
            VM((cut_a[1], nc * nz, nt), f32),
            VM((nz, nt), jnp.int32),
            SM(permittivity.shape, f32),
            pltpu.SemaphoreType.DMA((2 + cut_a[1],)),
        ],
        compiler_params=params,
        cost_estimate=free,
        name="first",
    )(*(pltpu.with_memory_space_constraint(x, pltpu.HBM) for x in (v, mat, permittivity)))
    x_a = swap(x_a)
    near, far = pl.pallas_call(
        edge_kernel,
        out_shape=(plane, plane),
        in_specs=[vm, vm],
        out_specs=(vm, vm),
        compiler_params=params,
        cost_estimate=free,
        name="edges",
    )(v, scale)
    near, far = trans_swaps(near, far)
    own_c, from_left, from_right = pl.pallas_call(
        lambda *refs: corner_kernel(*cut_c, *refs),
        out_shape=(planes(3 * size_c, 2 * nb), plane, plane),
        in_specs=[vm] * 4,
        out_specs=(vm,) * 3,
        compiler_params=params,
        cost_estimate=free,
        name="corners",
    )(v, scale, near, far)
    x_c = swap(own_c)

    def relay_pair(x, size, rows, name, *after):
        return pl.pallas_call(
            lambda *refs: relay_kernel(nz, nb, *refs),
            out_shape=planes(2 * size, rows),
            in_specs=[vm] + [hbm] * len(after),
            out_specs=vm,
            compiler_params=params,
            cost_estimate=free,
            name=name,
        )(x, *after)

    pair_a = relay_pair(x_a, size_a, 0, "relay_a", own_c)
    y_a = relay(pair_a)
    own_f, own_b = pl.pallas_call(
        lambda *refs: direct_kernel(*cut_d, *refs),
        out_shape=(planes(2 * size_d), planes(2 * size_d)),
        in_specs=[vm, vm, hbm],
        out_specs=(vm, vm),
        compiler_params=params,
        cost_estimate=free,
        name="direct",
    )(v, scale, pair_a)
    fwd_d, bwd_d = shift(own_f, 1), shift(own_b, -1)
    y_c = relay(relay_pair(x_c, size_c, nb, "relay_c", own_f, own_b))
    inner, pay = pl.pallas_call(
        inner_kernel,
        out_shape=(works(nb), pay_shape),
        in_specs=[sm] + [vm] * 5,
        out_specs=(vm, vm),
        compiler_params=params,
        cost_estimate=free,
        name="inner",
    )(coupling_prev, v, scale, q, from_left, from_right)
    w_ac, pay, columns_f, columns_b = pl.pallas_call(
        lambda *refs: sum_kernel(((*cut_a, True), (*cut_c, True)), 0, *refs),
        out_shape=(works(cut_c[1]), pay_shape, plane, plane),
        in_specs=[vm] * 10,
        out_specs=(vm,) * 4,
        compiler_params=params,
        cost_estimate=free,
        name="products",
    )(v, scale, inner, pay, x_a, y_a, x_c, y_c, x_c, y_c)
    w_d, pay = pl.pallas_call(
        lambda *refs: sum_kernel(((*cut_d, False),), cut_d[0], *refs),
        out_shape=(works(size_d), pay_shape),
        in_specs=[vm] * 9,
        out_specs=(vm, vm),
        compiler_params=params,
        cost_estimate=free,
        name="products_last",
    )(v, scale, inner, pay, fwd_d, bwd_d, columns_f, columns_b, w_ac)
    pay = jnp.broadcast_to(pay[None], (devices, 2, nt))
    pay = lax.all_to_all(pay, ("loop", "trans"), 0, 0)
    small = jax.ShapeDtypeStruct((nb, nb), f32)
    out, alpha, beta = pl.pallas_call(
        lambda *refs: last_kernel(count, *refs),
        out_shape=(works(nb), small, small),
        in_specs=[vm] * 4,
        out_specs=(hbm,) * 3,
        scratch_shapes=[
            VM((nb + nb * (nb + 1) // 2, 8, nt), f32),
            VM((nb, nc * nz, nt), f32),
            VM((nb, nb), f32),
            VM((nb, nb), f32),
            pltpu.SemaphoreType.DMA((6,)),
        ],
        compiler_params=params,
        cost_estimate=free,
        name="combine",
    )(pay, v, w_ac, w_d)
    return out.reshape(block_now.shape), alpha, beta


def solution(mesh):
    in_specs = (
        P(None, None, None, "loop", "trans"),
        P(None, None, None, "loop", "trans"),
        P(),
        P(None, "loop", "trans"),
        P(),
    )
    out_specs = (P(None, None, None, "loop", "trans"), P(), P())
    return jax.shard_map(local, mesh=mesh, in_specs=in_specs, out_specs=out_specs, check_vma=False)
```

```python
import jax
import jax.numpy as jnp
from jax import lax
from jax.experimental import pallas as pl
from jax.experimental.pallas import tpu as pltpu
from jax.sharding import PartitionSpec as P

VM = pltpu.VMEM
SM = pltpu.SMEM


def lane_ids(shape):
    return lax.broadcasted_iota(jnp.int32, shape, len(shape) - 1)


def row_ids(shape):
    return lax.broadcasted_iota(jnp.int32, shape, len(shape) - 2)


def roll_by(x, shift, axis):
    return pltpu.roll(x, shift % x.shape[axis], axis)


def cell_scale(mat, eps_ref):
    eps = jnp.full(mat.shape, eps_ref[0], jnp.float32)
    for level in range(1, eps_ref.shape[0]):
        eps = jnp.where(mat == level, eps_ref[level], eps)
    return 1.0 / jnp.sqrt(eps)


def z_next(x):
    n = x.shape[0]
    return jnp.where(row_ids(x.shape) == n - 1, 0.0, roll_by(x, -1, 0))


def z_prev(x):
    return jnp.where(row_ids(x.shape) == 0, 0.0, roll_by(x, 1, 0))


def forward_pair(uz, up, ut):
    lane = lane_ids(up.shape)
    up_next = jnp.where(lane == up.shape[1] - 1, 0.0, roll_by(up, -1, 1))
    return uz + (z_next(up) - up), ut + (up_next - up)


def even_trans():
    return lax.rem(lax.axis_index("trans"), 2) == 0


def odd_loop():
    return lax.rem(lax.axis_index("loop"), 2) == 1


def packed(v_ref, b, scale, fwd_ref, bwd_ref, at):
    nz = scale.shape[0]
    uz = v_ref[b, pl.ds(0, nz), :] * scale
    up = v_ref[b, pl.ds(nz, nz), :] * scale
    ut = v_ref[b, pl.ds(2 * nz, nz), :] * scale
    one, two = pl.ds(at * nz, nz), pl.ds((at + 1) * nz, nz)
    bwd_ref[one, :] = uz
    bwd_ref[two, :] = ut
    fwd_ref[one, :], fwd_ref[two, :] = forward_pair(uz, up, ut)


def first_kernel(cut_r, v_hbm, mat_hbm, eps_hbm, x_ref, scale_ref, v_ref, mat_ref, eps_ref, sems):
    copies = [
        pltpu.make_async_copy(eps_hbm, eps_ref, sems.at[0]),
        pltpu.make_async_copy(mat_hbm, mat_ref, sems.at[1]),
    ]
    for b in range(v_ref.shape[0]):
        copies.append(pltpu.make_async_copy(v_hbm.at[b], v_ref.at[b], sems.at[2 + b]))
    for copy in copies:
        copy.start()
    copies[0].wait()
    copies[1].wait()
    scale = cell_scale(mat_ref[...], eps_ref)
    scale_ref[...] = scale
    nz = scale.shape[0]
    for m, b in enumerate(range(*cut_r)):
        copies[2 + b].wait()
        for c in range(3):
            x_ref[pl.ds((3 * m + c) * nz, nz), :] = v_ref[b, pl.ds(c * nz, nz), :] * scale


def relay_kernel(nz, x_ref, after_f_ref, after_b_ref, y_ref):
    odd = odd_loop()
    count = x_ref.shape[0] // (3 * nz)

    def comps(m):
        return [x_ref[pl.ds((3 * m + c) * nz, nz), :] for c in range(3)]

    def store(m, pair):
        y_ref[pl.ds(2 * m * nz, nz), :] = pair[0]
        y_ref[pl.ds((2 * m + 1) * nz, nz), :] = pair[1]

    @pl.when(odd)
    def _():
        for m in range(count):
            store(m, comps(m)[::2])

    @pl.when(jnp.logical_not(odd))
    def _():
        for m in range(count):
            store(m, forward_pair(*comps(m)))


def edge_kernel(cut, v_ref, scale_ref, near_ref, far_ref, fwd_ref, bwd_ref):
    scale = scale_ref[...]
    nz = scale.shape[0]
    lane = lane_ids(scale.shape)
    right = jnp.zeros_like(scale)
    left = jnp.zeros_like(scale)
    for b in range(v_ref.shape[0]):
        for c in range(3):
            u = v_ref[b, pl.ds(c * nz, nz), :] * scale
            spot = v_ref.shape[0] * c + b
            right = jnp.where(lane == spot, roll_by(u, spot + 1, 1), right)
            left = jnp.where(lane == spot, roll_by(u, spot, 1), left)
    even = even_trans()
    near_ref[...] = jnp.where(even, right, left)
    far_ref[...] = jnp.where(even, left, right)
    for m, b in enumerate(range(*cut)):
        packed(v_ref, b, scale, fwd_ref, bwd_ref, 2 * m)


def turned(x):
    pad = jnp.zeros((x.shape[1] - x.shape[0], x.shape[1]), x.dtype)
    return jnp.concatenate([x, pad], axis=0).T


def corner_kernel(begin, end, v_ref, scale_ref, near_ref, far_ref, fwd_ref, bwd_ref, fr_ref, fl_ref):
    scale = scale_ref[...]
    for b in range(begin, end):
        packed(v_ref, b, scale, fwd_ref, bwd_ref, 2 * (b - begin))
    nb = v_ref.shape[0]
    even = even_trans()
    near, far = near_ref[...], far_ref[...]
    from_left, from_right = jnp.where(even, far, near), jnp.where(even, near, far)
    fr_ref[...] = from_left
    fl_ref[...] = from_right
    rows = pl.ds(2 * (end - begin) * scale.shape[0], nb)
    fwd_ref[rows, :] = turned(from_right)[nb : 2 * nb, :]
    bwd_ref[rows, :] = turned(from_left)[2 * nb : 3 * nb, :]


def more_kernel(begin, end, v_ref, scale_ref, fwd_a_ref, bwd_a_ref, fwd_ref, bwd_ref):
    scale = scale_ref[...]
    for b in range(begin, end):
        packed(v_ref, b, scale, fwd_ref, bwd_ref, 2 * (b - begin))


def merge(a, b, dist):
    low = (row_ids(a.shape) & dist) == 0
    other = jnp.where(low, b, a)
    swapped = roll_by(other, dist, 0)
    if 2 * dist != a.shape[0]:
        swapped = jnp.where(low, roll_by(other, -dist, 0), swapped)
    return jnp.where(low, a, b) + swapped


def add_products(pairs, steps, group, pays, unroll=8):
    shape = pays[0].shape
    lane, row = lane_ids(shape), row_ids(shape)
    zero = jnp.zeros(shape, jnp.float32)
    for first in range(0, len(pairs), group):
        part = pairs[first : first + group]

        def body(r, accs):
            rows = pl.ds(pl.multiple_of(r * 8, 8), 8)
            got = {}
            for left, j, right, b, _ in part:
                for ref, i in ((left, j), (right, b)):
                    if (id(ref), i) not in got:
                        got[(id(ref), i)] = ref[i, rows, :]
            return tuple(
                acc + got[(id(left), j)] * got[(id(right), b)]
                for acc, (left, j, right, b, _) in zip(accs, part)
            )

        accs = list(lax.fori_loop(0, steps, body, tuple(zero for _ in part), unroll=unroll))
        for at in range(0, len(part), 8):
            eight = accs[at : at + 8]
            eight = eight + [zero] * (8 - len(eight))
            four = [merge(eight[i], eight[i + 4], 4) for i in range(4)]
            two = [merge(four[i], four[i + 2], 2) for i in range(2)]
            sums = jnp.sum(merge(two[0], two[1], 1), axis=1, keepdims=True)
            for line in range(len(pays)):
                hit = None
                for i, pair in enumerate(part[at : at + 8]):
                    for spot in sorted(pair[4]):
                        if spot[0] == line:
                            here = (row == i) & (lane == spot[1])
                            hit = here if hit is None else hit | here
                if hit is not None:
                    pays[line] = pays[line] + jnp.where(hit, sums, 0.0)
    return pays


def store_pays(pay_ref, pays, before=None):
    for line, pay in enumerate(pays):
        total = jnp.sum(pay, axis=0, keepdims=True)
        if before is not None:
            total = total + before[line : line + 1, :]
        pay_ref[line : line + 1, :] = total


def inner_kernel(coup_ref, v_ref, scale_ref, q_ref, fr_ref, fl_ref, l_ref, pay_ref):
    nb = v_ref.shape[0]
    nz = scale_ref.shape[0]

    def body(b, carry):
        scale = scale_ref[...]
        lane = lane_ids(scale.shape)
        last = scale.shape[1] - 1
        uz = v_ref[b, pl.ds(0, nz), :] * scale
        up = v_ref[b, pl.ds(nz, nz), :] * scale
        ut = v_ref[b, pl.ds(2 * nz, nz), :] * scale

        def prev(u, c):
            edge = pltpu.roll(fr_ref[...], (last + 1 - (nb * c + b)) % (last + 1), 1)
            return jnp.where(lane == 0, edge, roll_by(u, 1, 1))

        def nxt(u, c):
            edge = pltpu.roll(fl_ref[...], last - (nb * c + b), 1)
            return jnp.where(lane == last, edge, roll_by(u, -1, 1))

        dt_ut = ut - prev(ut, 2)
        up_next = nxt(up, 1)
        uz_next = nxt(uz, 0)
        im_z = (z_next(up) - up) + (z_next(dt_ut) - dt_ut) + 4.0 * uz - uz_next - prev(uz, 0)
        im_p = 4.0 * up - z_next(up) - z_prev(up) - up_next - prev(up, 1) - (uz - z_prev(uz)) - dt_ut
        im_t = (
            (uz_next - z_prev(uz_next)) - (uz - z_prev(uz)) + (up_next - up)
            + 4.0 * ut - z_next(ut) - z_prev(ut)
        )
        for c, im in enumerate((im_z, im_p, im_t)):
            rows = pl.ds(c * nz, nz)
            out = im * scale
            for k in range(nb):
                out = out - coup_ref[b, k] * q_ref[k, rows, :]
            l_ref[b, rows, :] = out
        return carry

    lax.fori_loop(0, nb, body, 0)
    zero = jnp.zeros((8, v_ref.shape[2]), jnp.float32)
    pairs = [(v_ref, j, v_ref, b, {(1, nb * j + b), (1, nb * b + j)}) for b in range(nb) for j in range(b + 1)]
    store_pays(pay_ref, add_products(pairs, v_ref.shape[1] // 8, 36, [zero, zero]))


def sum_kernel(cuts, begin, v_ref, scale_ref, l_ref, pay_in_ref, *refs):
    nb = v_ref.shape[0]
    nz, nt = scale_ref.shape
    end = cuts[-1][1]
    halos = refs[: 2 * len(cuts)]
    corners = refs[2 * len(cuts) : 2 * len(cuts) + 2]
    if begin == 0:
        w_ref, pay_ref, columns_f_ref, columns_b_ref = refs[-4:]
        for corner, columns_ref in zip(corners, (columns_f_ref, columns_b_ref)):
            columns_ref[...] = turned(corner[pl.ds(corner.shape[0] - nb, nb), :])[:nz, :]
    else:
        columns_f_ref, columns_b_ref = corners
        old, w_ref, pay_ref = refs[-3:]
    columns_f, columns_b = columns_f_ref[...], columns_b_ref[...]
    scale = scale_ref[...]
    lane = lane_ids(scale.shape)
    odd = odd_loop()
    for i, (low, high, relayed) in enumerate(cuts):
        fwd_ref, bwd_ref = halos[2 * i : 2 * i + 2]

        for m in range(high - low):
            b = low + m
            one, two = pl.ds(2 * m * nz, nz), pl.ds((2 * m + 1) * nz, nz)
            if relayed:
                xz, xp, xt = (fwd_ref[pl.ds((3 * m + c) * nz, nz), :] for c in range(3))
                y0, y1 = bwd_ref[one, :], bwd_ref[two, :]
                f0, f1 = forward_pair(xz, xp, xt)
                za, tb = jnp.where(odd, f0, y0), jnp.where(odd, f1, y1)
                uz, ut = jnp.where(odd, y0, xz), jnp.where(odd, y1, xt)
            else:
                za, tb = fwd_ref[one, :], fwd_ref[two, :]
                uz, ut = bwd_ref[one, :], bwd_ref[two, :]
            edge_b = roll_by(columns_b, -b, 1)
            edge_f = roll_by(columns_f, nt - 1 - b, 1)
            ut_prev = jnp.where(lane == 0, edge_b, roll_by(ut, 1, 1))
            tb = tb + jnp.where(lane == nt - 1, edge_f, 0.0)
            to = b - begin
            w_ref[to, pl.ds(0, nz), :] = l_ref[b, pl.ds(0, nz), :] - scale * (za + uz)
            div = (uz - z_prev(uz)) + (ut - ut_prev)
            w_ref[to, pl.ds(nz, nz), :] = l_ref[b, pl.ds(nz, nz), :] + scale * div
            w_ref[to, pl.ds(2 * nz, nz), :] = l_ref[b, pl.ds(2 * nz, nz), :] - scale * (tb + ut)

    ws = [(old, b) for b in range(begin)] + [(w_ref, b - begin) for b in range(begin, end)]
    pairs = []
    for b in range(begin, end):
        pairs += [(v_ref, j, *ws[b], {(0, nb * j + b), (1, nb * nb + nb * b + j)}) for j in range(nb)]
        pairs += [(*ws[j], *ws[b], {(0, nb * nb + nb * j + b), (0, nb * nb + nb * b + j)}) for j in range(b + 1)]
    zero = jnp.zeros((8, nt), jnp.float32)
    store_pays(pay_ref, add_products(pairs, v_ref.shape[1] // 8, 42, [zero, zero]), pay_in_ref)


def lane_at(x, k):
    return jnp.broadcast_to(x[:, k : k + 1], x.shape)


def row_at(x, k):
    return jnp.broadcast_to(x[k : k + 1, :], x.shape)


def matrix_of(line, offset, nb):
    x = jnp.broadcast_to(line, (8, line.shape[1]))
    row = row_ids(x.shape)
    out = roll_by(x, -offset, 1)
    for i in range(1, nb):
        out = jnp.where(row == i, roll_by(x, -offset - nb * i, 1), out)
    return out


def last_kernel(count, pay_ref, v_ref, *refs):
    w_refs = refs[:-8]
    out_hbm, alpha_hbm, beta_hbm, coef_ref, out_ref, alpha_ref, beta_ref, sems = refs[-8:]
    nb = v_ref.shape[0]
    total = jnp.sum(pay_ref[...], axis=0)
    proj = matrix_of(total[0:1], 0, nb)
    ww = matrix_of(total[0:1], nb * nb, nb)
    vv = matrix_of(total[1:2], 0, nb)
    alpha = proj * (1.0 / count)
    alpha_t = matrix_of(total[1:2], nb * nb, nb) * (1.0 / count)
    alpha_ref[...] = alpha[:, :nb]
    copies = [pltpu.make_async_copy(alpha_ref, alpha_hbm, sems.at[0])]
    copies[0].start()
    lane = lane_ids(proj.shape)
    row = row_ids(proj.shape)
    cross = jnp.zeros_like(proj)
    half = jnp.zeros_like(proj)
    for j in range(nb):
        coef_ref[j] = lane_at(alpha_t, j)
        cross = cross + lane_at(alpha_t, j) * row_at(proj, j)
        half = half + lane_at(vv, j) * row_at(alpha, j)
    quad = jnp.zeros_like(proj)
    for k in range(nb):
        quad = quad + lane_at(alpha_t, k) * row_at(half, k)
    gram = ((ww - cross) + (quad - cross)) * (1.0 / count)
    ws = [(w, i) for w in w_refs for i in range(w.shape[0])]
    blocks = v_ref.shape[1] // 8
    mat = {}
    for i in range(nb):
        line = row_at(gram, i)
        for j in range(i + 1):
            mat[i, j] = lane_at(line, j)
    low, inv = {}, {}
    beta = jnp.zeros_like(proj)
    for k in range(nb):
        root = lax.rsqrt(mat[k, k])
        low[k, k] = mat[k, k] * root
        for i in range(k + 1, nb):
            low[i, k] = mat[i, k] * root
        for i in range(k + 1, nb):
            for j in range(k + 1, i + 1):
                mat[i, j] = mat[i, j] - low[i, k] * low[j, k]
        for i in range(k, nb):
            beta = jnp.where((row == k) & (lane == i), low[i, k], beta)
        inv[k, k] = root
        for j in range(k):
            acc = low[k, j] * inv[j, j]
            for q in range(j + 1, k):
                acc = acc + low[k, q] * inv[q, j]
            inv[k, j] = -(root * acc)
        for j in range(k + 1):
            coef_ref[nb + k * (k + 1) // 2 + j] = inv[k, j]
        for r in range(k * blocks // nb, (k + 1) * blocks // nb):
            rows = pl.ds(8 * r, 8)
            vs = [v_ref[j, rows, :] for j in range(nb)]
            for b, (w_ref, i) in enumerate(ws):
                acc = w_ref[i, rows, :]
                for j in range(nb):
                    acc = acc - coef_ref[j, pl.ds(b, 1), :] * vs[j]
                out_ref[b, rows, :] = acc
    beta_ref[...] = beta[:, :nb]
    copies.append(pltpu.make_async_copy(beta_ref, beta_hbm, sems.at[1]))
    copies[1].start()
    step = 16
    pieces = sems.shape[0] - 2
    length = v_ref.shape[1] // pieces
    for piece in range(pieces):
        base = piece * length

        def body(r, carry):
            rows = pl.ds(pl.multiple_of(base + r * step, step), step)
            xs = [out_ref[j, rows, :] for j in range(nb)]
            for b in range(nb):
                at = nb + b * (b + 1) // 2
                acc = coef_ref[at, pl.ds(0, 1), :] * xs[0]
                for j in range(1, b + 1):
                    acc = acc + coef_ref[at + j, pl.ds(0, 1), :] * xs[j]
                out_ref[b, rows, :] = acc
            return carry

        lax.fori_loop(0, length // step, body, 0, unroll=True)
        part = pl.ds(base, length)
        copy = pltpu.make_async_copy(out_ref.at[:, part, :], out_hbm.at[:, part, :], sems.at[2 + piece])
        copy.start()
        copies.append(copy)
    for copy in copies:
        copy.wait()


def shift(x, loop_by):
    count = lax.axis_size("loop")
    return lax.ppermute(x, "loop", [(i, (i + loop_by) % count) for i in range(count)])


def trans_swaps(near, far):
    count = lax.axis_size("trans")
    pairs = [(t, t + (-1 if t % 2 == 0 else 1)) for t in range(1, count - 1)]
    return lax.ppermute(near, "trans", [(t, t ^ 1) for t in range(count)]), lax.ppermute(far, "trans", pairs)


def swap(x):
    return lax.ppermute(x, "loop", [(i, i ^ 1) for i in range(lax.axis_size("loop"))])


def relay(x):
    count = lax.axis_size("loop")
    return lax.ppermute(x, "loop", [(i, (i + (-2 if i % 2 else 2)) % count) for i in range(count)])


def local(block_now, block_prev, coupling_prev, material, permittivity):
    nb, nc, nz, _, nt = block_now.shape
    f32 = jnp.float32
    devices = lax.axis_size("loop") * lax.axis_size("trans")
    count = float(nc * nz * nt * devices)
    v = block_now.reshape(nb, nc * nz, nt)
    q = block_prev.reshape(nb, nc * nz, nt)
    mat = material.reshape(nz, nt)
    vm, sm = pl.BlockSpec(memory_space=VM), pl.BlockSpec(memory_space=SM)
    hbm = pl.BlockSpec(memory_space=pltpu.HBM)
    params = pltpu.CompilerParams(vmem_limit_bytes=32 * 2**20)
    free = pl.CostEstimate(flops=0, bytes_accessed=0, transcendentals=0)
    plane = jax.ShapeDtypeStruct((nz, nt), f32)
    pay_shape = jax.ShapeDtypeStruct((2, nt), f32)
    assert lax.axis_size("loop") % 2 == 0 and lax.axis_size("trans") % 2 == 0
    marks = (0, nb * 3 // 8, nb * 5 // 8, nb - 1, nb)
    cut_r, cut_a, cut_b, cut_c = zip(marks[:-1], marks[1:])

    def planes(n, more=0):
        return jax.ShapeDtypeStruct((n * nz + more, nt), f32)

    def works(n):
        return jax.ShapeDtypeStruct((n, nc * nz, nt), f32)

    size_r, size_a, size_b, size_c = (2 * (c[1] - c[0]) for c in (cut_r, cut_a, cut_b, cut_c))
    x_r, scale = pl.pallas_call(
        lambda *refs: first_kernel(cut_r, *refs),
        out_shape=(planes(size_r * 3 // 2), plane),
        in_specs=[hbm] * 3,
        out_specs=(vm,) * 2,
        scratch_shapes=[
            VM((cut_r[1], nc * nz, nt), f32),
            VM((nz, nt), jnp.int32),
            SM(permittivity.shape, f32),
            pltpu.SemaphoreType.DMA((2 + cut_r[1],)),
        ],
        compiler_params=params,
        cost_estimate=free,
        name="first",
    )(*(pltpu.with_memory_space_constraint(x, pltpu.HBM) for x in (v, mat, permittivity)))
    x_r = swap(x_r)
    near, far, fwd_a, bwd_a = pl.pallas_call(
        lambda *refs: edge_kernel(cut_a, *refs),
        out_shape=(plane, plane, planes(size_a), planes(size_a)),
        in_specs=[vm, vm],
        out_specs=(vm,) * 4,
        compiler_params=params,
        cost_estimate=free,
        name="edges",
    )(v, scale)
    near, far = trans_swaps(near, far)
    fwd_a, bwd_a = shift(fwd_a, 1), shift(bwd_a, -1)
    own_f, own_b, from_left, from_right = pl.pallas_call(
        lambda *refs: corner_kernel(*cut_b, *refs),
        out_shape=(planes(size_b, nb), planes(size_b, nb), plane, plane),
        in_specs=[vm] * 4,
        out_specs=(vm,) * 4,
        compiler_params=params,
        cost_estimate=free,
        name="pack_b",
    )(v, scale, near, far)
    fwd_b, bwd_b = shift(own_f, 1), shift(own_b, -1)
    y_r = relay(
        pl.pallas_call(
            lambda *refs: relay_kernel(nz, *refs),
            out_shape=planes(size_r),
            in_specs=[vm, hbm, hbm],
            out_specs=vm,
            compiler_params=params,
            cost_estimate=free,
            name="relay",
        )(x_r, own_f, own_b)
    )
    fwd_c, bwd_c = pl.pallas_call(
        lambda *refs: more_kernel(*cut_c, *refs),
        out_shape=(planes(size_c), planes(size_c)),
        in_specs=[vm, vm, hbm, hbm],
        out_specs=(vm, vm),
        compiler_params=params,
        cost_estimate=free,
        name="pack_c",
    )(v, scale, fwd_a, bwd_a)
    fwd_c, bwd_c = shift(fwd_c, 1), shift(bwd_c, -1)
    inner, pay = pl.pallas_call(
        inner_kernel,
        out_shape=(works(nb), pay_shape),
        in_specs=[sm] + [vm] * 5,
        out_specs=(vm, vm),
        compiler_params=params,
        cost_estimate=free,
        name="inner",
    )(coupling_prev, v, scale, q, from_left, from_right)
    w_ab, pay, columns_f, columns_b = pl.pallas_call(
        lambda *refs: sum_kernel(((*cut_r, True), (*cut_a, False), (*cut_b, False)), 0, *refs),
        out_shape=(works(cut_b[1]), pay_shape, plane, plane),
        in_specs=[vm] * 12,
        out_specs=(vm,) * 4,
        compiler_params=params,
        cost_estimate=free,
        name="products",
    )(v, scale, inner, pay, x_r, y_r, fwd_a, bwd_a, fwd_b, bwd_b, fwd_b, bwd_b)
    w_c, pay = pl.pallas_call(
        lambda *refs: sum_kernel(((*cut_c, False),), cut_c[0], *refs),
        out_shape=(works(cut_c[1] - cut_c[0]), pay_shape),
        in_specs=[vm] * 9,
        out_specs=(vm, vm),
        compiler_params=params,
        cost_estimate=free,
        name="products_last",
    )(v, scale, inner, pay, fwd_c, bwd_c, columns_f, columns_b, w_ab)
    pay = jnp.broadcast_to(pay[None], (devices, 2, nt))
    pay = lax.all_to_all(pay, ("loop", "trans"), 0, 0)
    small = jax.ShapeDtypeStruct((nb, nb), f32)
    out, alpha, beta = pl.pallas_call(
        lambda *refs: last_kernel(count, *refs),
        out_shape=(works(nb), small, small),
        in_specs=[vm] * 4,
        out_specs=(hbm,) * 3,
        scratch_shapes=[
            VM((nb + nb * (nb + 1) // 2, 8, nt), f32),
            VM((nb, nc * nz, nt), f32),
            VM((nb, nb), f32),
            VM((nb, nb), f32),
            pltpu.SemaphoreType.DMA((6,)),
        ],
        compiler_params=params,
        cost_estimate=free,
        name="combine",
    )(pay, v, w_ab, w_c)
    return out.reshape(block_now.shape), alpha, beta


def solution(mesh):
    in_specs = (
        P(None, None, None, "loop", "trans"),
        P(None, None, None, "loop", "trans"),
        P(),
        P(None, "loop", "trans"),
        P(),
    )
    out_specs = (P(None, None, None, "loop", "trans"), P(), P())
    return jax.shard_map(local, mesh=mesh, in_specs=in_specs, out_specs=out_specs, check_vma=False)
```

```python
import jax
import jax.numpy as jnp
from jax import lax
from jax.experimental import pallas as pl
from jax.experimental.pallas import tpu as pltpu
from jax.sharding import PartitionSpec as P

VM = pltpu.VMEM
SM = pltpu.SMEM


def lane_ids(shape):
    return lax.broadcasted_iota(jnp.int32, shape, len(shape) - 1)


def row_ids(shape):
    return lax.broadcasted_iota(jnp.int32, shape, len(shape) - 2)


def roll_by(x, shift, axis):
    return pltpu.roll(x, shift % x.shape[axis], axis)


def cell_scale(mat, eps_ref):
    eps = jnp.full(mat.shape, eps_ref[0], jnp.float32)
    for level in range(1, eps_ref.shape[0]):
        eps = jnp.where(mat == level, eps_ref[level], eps)
    return 1.0 / jnp.sqrt(eps)


def z_next(x):
    n = x.shape[0]
    return jnp.where(row_ids(x.shape) == n - 1, 0.0, roll_by(x, -1, 0))


def z_prev(x):
    return jnp.where(row_ids(x.shape) == 0, 0.0, roll_by(x, 1, 0))


def forward_pair(uz, up, ut):
    lane = lane_ids(up.shape)
    up_next = jnp.where(lane == up.shape[1] - 1, 0.0, roll_by(up, -1, 1))
    return uz + (z_next(up) - up), ut + (up_next - up)


def even_trans():
    return lax.rem(lax.axis_index("trans"), 2) == 0


def odd_loop():
    return lax.rem(lax.axis_index("loop"), 2) == 1


def packed(v_ref, b, scale, fwd_ref, bwd_ref, at):
    nz = scale.shape[0]
    uz = v_ref[b, pl.ds(0, nz), :] * scale
    up = v_ref[b, pl.ds(nz, nz), :] * scale
    ut = v_ref[b, pl.ds(2 * nz, nz), :] * scale
    one, two = pl.ds(at * nz, nz), pl.ds((at + 1) * nz, nz)
    bwd_ref[one, :] = uz
    bwd_ref[two, :] = ut
    fwd_ref[one, :], fwd_ref[two, :] = forward_pair(uz, up, ut)


def first_kernel(cut_r, v_hbm, mat_hbm, eps_hbm, x_ref, scale_ref, v_ref, mat_ref, eps_ref, sems):
    copies = [
        pltpu.make_async_copy(eps_hbm, eps_ref, sems.at[0]),
        pltpu.make_async_copy(mat_hbm, mat_ref, sems.at[1]),
    ]
    for b in range(v_ref.shape[0]):
        copies.append(pltpu.make_async_copy(v_hbm.at[b], v_ref.at[b], sems.at[2 + b]))
    for copy in copies:
        copy.start()
    copies[0].wait()
    copies[1].wait()
    scale = cell_scale(mat_ref[...], eps_ref)
    scale_ref[...] = scale
    nz = scale.shape[0]
    for m, b in enumerate(range(*cut_r)):
        copies[2 + b].wait()
        for c in range(3):
            x_ref[pl.ds((3 * m + c) * nz, nz), :] = v_ref[b, pl.ds(c * nz, nz), :] * scale


def relay_kernel(nz, x_ref, *refs):
    y_ref = refs[-1]
    odd = odd_loop()
    count = x_ref.shape[0] // (3 * nz)

    def comps(m):
        return [x_ref[pl.ds((3 * m + c) * nz, nz), :] for c in range(3)]

    def store(m, pair):
        y_ref[pl.ds(2 * m * nz, nz), :] = pair[0]
        y_ref[pl.ds((2 * m + 1) * nz, nz), :] = pair[1]

    @pl.when(odd)
    def _():
        for m in range(count):
            store(m, comps(m)[::2])

    @pl.when(jnp.logical_not(odd))
    def _():
        for m in range(count):
            store(m, forward_pair(*comps(m)))


def edge_kernel(cut, v_ref, scale_ref, near_ref, far_ref, x_ref):
    scale = scale_ref[...]
    nz = scale.shape[0]
    lane = lane_ids(scale.shape)
    right = jnp.zeros_like(scale)
    left = jnp.zeros_like(scale)
    for b in range(v_ref.shape[0]):
        for c in range(3):
            u = v_ref[b, pl.ds(c * nz, nz), :] * scale
            spot = v_ref.shape[0] * c + b
            right = jnp.where(lane == spot, roll_by(u, spot + 1, 1), right)
            left = jnp.where(lane == spot, roll_by(u, spot, 1), left)
    even = even_trans()
    near_ref[...] = jnp.where(even, right, left)
    far_ref[...] = jnp.where(even, left, right)
    for m, b in enumerate(range(*cut)):
        for c in range(3):
            x_ref[pl.ds((3 * m + c) * nz, nz), :] = v_ref[b, pl.ds(c * nz, nz), :] * scale


def turned(x):
    pad = jnp.zeros((x.shape[1] - x.shape[0], x.shape[1]), x.dtype)
    return jnp.concatenate([x, pad], axis=0).T


def corner_kernel(
    begin, end, v_ref, scale_ref, near_ref, far_ref, after_ref, fwd_ref, bwd_ref, fr_ref, fl_ref
):
    scale = scale_ref[...]
    for b in range(begin, end):
        packed(v_ref, b, scale, fwd_ref, bwd_ref, 2 * (b - begin))
    nb = v_ref.shape[0]
    even = even_trans()
    near, far = near_ref[...], far_ref[...]
    from_left, from_right = jnp.where(even, far, near), jnp.where(even, near, far)
    fr_ref[...] = from_left
    fl_ref[...] = from_right
    rows = pl.ds(2 * (end - begin) * scale.shape[0], nb)
    fwd_ref[rows, :] = turned(from_right)[nb : 2 * nb, :]
    bwd_ref[rows, :] = turned(from_left)[2 * nb : 3 * nb, :]


def more_kernel(begin, end, v_ref, scale_ref, after_ref, fwd_ref, bwd_ref):
    scale = scale_ref[...]
    for b in range(begin, end):
        packed(v_ref, b, scale, fwd_ref, bwd_ref, 2 * (b - begin))


def merge(a, b, dist):
    low = (row_ids(a.shape) & dist) == 0
    other = jnp.where(low, b, a)
    swapped = roll_by(other, dist, 0)
    if 2 * dist != a.shape[0]:
        swapped = jnp.where(low, roll_by(other, -dist, 0), swapped)
    return jnp.where(low, a, b) + swapped


def add_products(pairs, steps, group, pays, unroll=8):
    shape = pays[0].shape
    lane, row = lane_ids(shape), row_ids(shape)
    zero = jnp.zeros(shape, jnp.float32)
    for first in range(0, len(pairs), group):
        part = pairs[first : first + group]

        def body(r, accs):
            rows = pl.ds(pl.multiple_of(r * 8, 8), 8)
            got = {}
            for left, j, right, b, _ in part:
                for ref, i in ((left, j), (right, b)):
                    if (id(ref), i) not in got:
                        got[(id(ref), i)] = ref[i, rows, :]
            return tuple(
                acc + got[(id(left), j)] * got[(id(right), b)]
                for acc, (left, j, right, b, _) in zip(accs, part)
            )

        accs = list(lax.fori_loop(0, steps, body, tuple(zero for _ in part), unroll=unroll))
        for at in range(0, len(part), 8):
            eight = accs[at : at + 8]
            eight = eight + [zero] * (8 - len(eight))
            four = [merge(eight[i], eight[i + 4], 4) for i in range(4)]
            two = [merge(four[i], four[i + 2], 2) for i in range(2)]
            sums = jnp.sum(merge(two[0], two[1], 1), axis=1, keepdims=True)
            for line in range(len(pays)):
                hit = None
                for i, pair in enumerate(part[at : at + 8]):
                    for spot in sorted(pair[4]):
                        if spot[0] == line:
                            here = (row == i) & (lane == spot[1])
                            hit = here if hit is None else hit | here
                if hit is not None:
                    pays[line] = pays[line] + jnp.where(hit, sums, 0.0)
    return pays


def store_pays(pay_ref, pays, before=None):
    for line, pay in enumerate(pays):
        total = jnp.sum(pay, axis=0, keepdims=True)
        if before is not None:
            total = total + before[line : line + 1, :]
        pay_ref[line : line + 1, :] = total


def inner_kernel(coup_ref, v_ref, scale_ref, q_ref, fr_ref, fl_ref, l_ref, pay_ref):
    nb = v_ref.shape[0]
    nz = scale_ref.shape[0]

    def body(b, carry):
        scale = scale_ref[...]
        lane = lane_ids(scale.shape)
        last = scale.shape[1] - 1
        uz = v_ref[b, pl.ds(0, nz), :] * scale
        up = v_ref[b, pl.ds(nz, nz), :] * scale
        ut = v_ref[b, pl.ds(2 * nz, nz), :] * scale

        def prev(u, c):
            edge = pltpu.roll(fr_ref[...], (last + 1 - (nb * c + b)) % (last + 1), 1)
            return jnp.where(lane == 0, edge, roll_by(u, 1, 1))

        def nxt(u, c):
            edge = pltpu.roll(fl_ref[...], last - (nb * c + b), 1)
            return jnp.where(lane == last, edge, roll_by(u, -1, 1))

        dt_ut = ut - prev(ut, 2)
        up_next = nxt(up, 1)
        uz_next = nxt(uz, 0)
        im_z = (z_next(up) - up) + (z_next(dt_ut) - dt_ut) + 4.0 * uz - uz_next - prev(uz, 0)
        im_p = 4.0 * up - z_next(up) - z_prev(up) - up_next - prev(up, 1) - (uz - z_prev(uz)) - dt_ut
        im_t = (
            (uz_next - z_prev(uz_next)) - (uz - z_prev(uz)) + (up_next - up)
            + 4.0 * ut - z_next(ut) - z_prev(ut)
        )
        for c, im in enumerate((im_z, im_p, im_t)):
            rows = pl.ds(c * nz, nz)
            out = im * scale
            for k in range(nb):
                out = out - coup_ref[b, k] * q_ref[k, rows, :]
            l_ref[b, rows, :] = out
        return carry

    lax.fori_loop(0, nb, body, 0)
    zero = jnp.zeros((8, v_ref.shape[2]), jnp.float32)
    pairs = [(v_ref, j, v_ref, b, {(1, nb * j + b), (1, nb * b + j)}) for b in range(nb) for j in range(b + 1)]
    store_pays(pay_ref, add_products(pairs, v_ref.shape[1] // 8, 36, [zero, zero]))


def sum_kernel(cuts, begin, v_ref, scale_ref, l_ref, pay_in_ref, *refs):
    nb = v_ref.shape[0]
    nz, nt = scale_ref.shape
    end = cuts[-1][1]
    halos = refs[: 2 * len(cuts)]
    corners = refs[2 * len(cuts) : 2 * len(cuts) + 2]
    if begin == 0:
        w_ref, pay_ref, columns_f_ref, columns_b_ref = refs[-4:]
        for corner, columns_ref in zip(corners, (columns_f_ref, columns_b_ref)):
            columns_ref[...] = turned(corner[pl.ds(corner.shape[0] - nb, nb), :])[:nz, :]
    else:
        columns_f_ref, columns_b_ref = corners
        old, w_ref, pay_ref = refs[-3:]
    columns_f, columns_b = columns_f_ref[...], columns_b_ref[...]
    scale = scale_ref[...]
    lane = lane_ids(scale.shape)
    odd = odd_loop()
    for i, (low, high, relayed) in enumerate(cuts):
        fwd_ref, bwd_ref = halos[2 * i : 2 * i + 2]

        for m in range(high - low):
            b = low + m
            one, two = pl.ds(2 * m * nz, nz), pl.ds((2 * m + 1) * nz, nz)
            if relayed:
                xz, xp, xt = (fwd_ref[pl.ds((3 * m + c) * nz, nz), :] for c in range(3))
                y0, y1 = bwd_ref[one, :], bwd_ref[two, :]
                f0, f1 = forward_pair(xz, xp, xt)
                za, tb = jnp.where(odd, f0, y0), jnp.where(odd, f1, y1)
                uz, ut = jnp.where(odd, y0, xz), jnp.where(odd, y1, xt)
            else:
                za, tb = fwd_ref[one, :], fwd_ref[two, :]
                uz, ut = bwd_ref[one, :], bwd_ref[two, :]
            edge_b = roll_by(columns_b, -b, 1)
            edge_f = roll_by(columns_f, nt - 1 - b, 1)
            ut_prev = jnp.where(lane == 0, edge_b, roll_by(ut, 1, 1))
            tb = tb + jnp.where(lane == nt - 1, edge_f, 0.0)
            to = b - begin
            w_ref[to, pl.ds(0, nz), :] = l_ref[b, pl.ds(0, nz), :] - scale * (za + uz)
            div = (uz - z_prev(uz)) + (ut - ut_prev)
            w_ref[to, pl.ds(nz, nz), :] = l_ref[b, pl.ds(nz, nz), :] + scale * div
            w_ref[to, pl.ds(2 * nz, nz), :] = l_ref[b, pl.ds(2 * nz, nz), :] - scale * (tb + ut)

    ws = [(old, b) for b in range(begin)] + [(w_ref, b - begin) for b in range(begin, end)]
    pairs = []
    for b in range(begin, end):
        pairs += [(v_ref, j, *ws[b], {(0, nb * j + b), (1, nb * nb + nb * b + j)}) for j in range(nb)]
        pairs += [(*ws[j], *ws[b], {(0, nb * nb + nb * j + b), (0, nb * nb + nb * b + j)}) for j in range(b + 1)]
    zero = jnp.zeros((8, nt), jnp.float32)
    store_pays(pay_ref, add_products(pairs, v_ref.shape[1] // 8, 42, [zero, zero]), pay_in_ref)


def lane_at(x, k):
    return jnp.broadcast_to(x[:, k : k + 1], x.shape)


def row_at(x, k):
    return jnp.broadcast_to(x[k : k + 1, :], x.shape)


def matrix_of(line, offset, nb):
    x = jnp.broadcast_to(line, (8, line.shape[1]))
    row = row_ids(x.shape)
    out = roll_by(x, -offset, 1)
    for i in range(1, nb):
        out = jnp.where(row == i, roll_by(x, -offset - nb * i, 1), out)
    return out


def last_kernel(count, pay_ref, v_ref, *refs):
    w_refs = refs[:-8]
    out_hbm, alpha_hbm, beta_hbm, coef_ref, out_ref, alpha_ref, beta_ref, sems = refs[-8:]
    nb = v_ref.shape[0]
    total = jnp.sum(pay_ref[...], axis=0)
    proj = matrix_of(total[0:1], 0, nb)
    ww = matrix_of(total[0:1], nb * nb, nb)
    vv = matrix_of(total[1:2], 0, nb)
    alpha = proj * (1.0 / count)
    alpha_t = matrix_of(total[1:2], nb * nb, nb) * (1.0 / count)
    alpha_ref[...] = alpha[:, :nb]
    copies = [pltpu.make_async_copy(alpha_ref, alpha_hbm, sems.at[0])]
    copies[0].start()
    lane = lane_ids(proj.shape)
    row = row_ids(proj.shape)
    cross = jnp.zeros_like(proj)
    half = jnp.zeros_like(proj)
    for j in range(nb):
        coef_ref[j] = lane_at(alpha_t, j)
        cross = cross + lane_at(alpha_t, j) * row_at(proj, j)
        half = half + lane_at(vv, j) * row_at(alpha, j)
    quad = jnp.zeros_like(proj)
    for k in range(nb):
        quad = quad + lane_at(alpha_t, k) * row_at(half, k)
    gram = ((ww - cross) + (quad - cross)) * (1.0 / count)
    ws = [(w, i) for w in w_refs for i in range(w.shape[0])]
    blocks = v_ref.shape[1] // 8
    mat = {}
    for i in range(nb):
        line = row_at(gram, i)
        for j in range(i + 1):
            mat[i, j] = lane_at(line, j)
    low, inv = {}, {}
    beta = jnp.zeros_like(proj)
    for k in range(nb):
        root = lax.rsqrt(mat[k, k])
        low[k, k] = mat[k, k] * root
        for i in range(k + 1, nb):
            low[i, k] = mat[i, k] * root
        for i in range(k + 1, nb):
            for j in range(k + 1, i + 1):
                mat[i, j] = mat[i, j] - low[i, k] * low[j, k]
        for i in range(k, nb):
            beta = jnp.where((row == k) & (lane == i), low[i, k], beta)
        inv[k, k] = root
        for j in range(k):
            acc = low[k, j] * inv[j, j]
            for q in range(j + 1, k):
                acc = acc + low[k, q] * inv[q, j]
            inv[k, j] = -(root * acc)
        for j in range(k + 1):
            coef_ref[nb + k * (k + 1) // 2 + j] = inv[k, j]
        for r in range(k * blocks // nb, (k + 1) * blocks // nb):
            rows = pl.ds(8 * r, 8)
            vs = [v_ref[j, rows, :] for j in range(nb)]
            for b, (w_ref, i) in enumerate(ws):
                acc = w_ref[i, rows, :]
                for j in range(nb):
                    acc = acc - coef_ref[j, pl.ds(b, 1), :] * vs[j]
                out_ref[b, rows, :] = acc
    beta_ref[...] = beta[:, :nb]
    copies.append(pltpu.make_async_copy(beta_ref, beta_hbm, sems.at[1]))
    copies[1].start()
    step = 16
    pieces = sems.shape[0] - 2
    length = v_ref.shape[1] // pieces
    for piece in range(pieces):
        base = piece * length

        def body(r, carry):
            rows = pl.ds(pl.multiple_of(base + r * step, step), step)
            xs = [out_ref[j, rows, :] for j in range(nb)]
            for b in range(nb):
                at = nb + b * (b + 1) // 2
                acc = coef_ref[at, pl.ds(0, 1), :] * xs[0]
                for j in range(1, b + 1):
                    acc = acc + coef_ref[at + j, pl.ds(0, 1), :] * xs[j]
                out_ref[b, rows, :] = acc
            return carry

        lax.fori_loop(0, length // step, body, 0, unroll=True)
        part = pl.ds(base, length)
        copy = pltpu.make_async_copy(out_ref.at[:, part, :], out_hbm.at[:, part, :], sems.at[2 + piece])
        copy.start()
        copies.append(copy)
    for copy in copies:
        copy.wait()


def shift(x, loop_by):
    count = lax.axis_size("loop")
    return lax.ppermute(x, "loop", [(i, (i + loop_by) % count) for i in range(count)])


def trans_swaps(near, far):
    count = lax.axis_size("trans")
    pairs = [(t, t + (-1 if t % 2 == 0 else 1)) for t in range(1, count - 1)]
    return lax.ppermute(near, "trans", [(t, t ^ 1) for t in range(count)]), lax.ppermute(far, "trans", pairs)


def swap(x):
    return lax.ppermute(x, "loop", [(i, i ^ 1) for i in range(lax.axis_size("loop"))])


def relay(x):
    count = lax.axis_size("loop")
    return lax.ppermute(x, "loop", [(i, (i + (-2 if i % 2 else 2)) % count) for i in range(count)])


def local(block_now, block_prev, coupling_prev, material, permittivity):
    nb, nc, nz, _, nt = block_now.shape
    f32 = jnp.float32
    devices = lax.axis_size("loop") * lax.axis_size("trans")
    count = float(nc * nz * nt * devices)
    v = block_now.reshape(nb, nc * nz, nt)
    q = block_prev.reshape(nb, nc * nz, nt)
    mat = material.reshape(nz, nt)
    vm, sm = pl.BlockSpec(memory_space=VM), pl.BlockSpec(memory_space=SM)
    hbm = pl.BlockSpec(memory_space=pltpu.HBM)
    params = pltpu.CompilerParams(vmem_limit_bytes=32 * 2**20)
    free = pl.CostEstimate(flops=0, bytes_accessed=0, transcendentals=0)
    plane = jax.ShapeDtypeStruct((nz, nt), f32)
    pay_shape = jax.ShapeDtypeStruct((2, nt), f32)
    assert lax.axis_size("loop") % 2 == 0 and lax.axis_size("trans") % 2 == 0
    marks = (0, nb // 4, nb // 2, nb - 1, nb)
    cut_r, cut_a, cut_b, cut_c = zip(marks[:-1], marks[1:])

    def planes(n, more=0):
        return jax.ShapeDtypeStruct((n * nz + more, nt), f32)

    def works(n):
        return jax.ShapeDtypeStruct((n, nc * nz, nt), f32)

    size_r, size_a, size_b, size_c = (2 * (c[1] - c[0]) for c in (cut_r, cut_a, cut_b, cut_c))
    x_r, scale = pl.pallas_call(
        lambda *refs: first_kernel(cut_r, *refs),
        out_shape=(planes(size_r * 3 // 2), plane),
        in_specs=[hbm] * 3,
        out_specs=(vm,) * 2,
        scratch_shapes=[
            VM((cut_r[1], nc * nz, nt), f32),
            VM((nz, nt), jnp.int32),
            SM(permittivity.shape, f32),
            pltpu.SemaphoreType.DMA((2 + cut_r[1],)),
        ],
        compiler_params=params,
        cost_estimate=free,
        name="first",
    )(*(pltpu.with_memory_space_constraint(x, pltpu.HBM) for x in (v, mat, permittivity)))
    x_r = swap(x_r)
    near, far, x_a = pl.pallas_call(
        lambda *refs: edge_kernel(cut_a, *refs),
        out_shape=(plane, plane, planes(size_a * 3 // 2)),
        in_specs=[vm, vm],
        out_specs=(vm,) * 3,
        compiler_params=params,
        cost_estimate=free,
        name="edges",
    )(v, scale)
    near, far = trans_swaps(near, far)
    x_a = swap(x_a)
    def relay_pair(x, size, name, *after):
        return pl.pallas_call(
            lambda *refs: relay_kernel(nz, *refs),
            out_shape=planes(size),
            in_specs=[vm] + [hbm] * len(after),
            out_specs=vm,
            compiler_params=params,
            cost_estimate=free,
            name=name,
        )(x, *after)

    pair_r = relay_pair(x_r, size_r, "relay", near, far)
    y_r = relay(pair_r)
    own_f, own_b, from_left, from_right = pl.pallas_call(
        lambda *refs: corner_kernel(*cut_b, *refs),
        out_shape=(planes(size_b, nb), planes(size_b, nb), plane, plane),
        in_specs=[vm] * 4 + [hbm],
        out_specs=(vm,) * 4,
        compiler_params=params,
        cost_estimate=free,
        name="pack_b",
    )(v, scale, near, far, pair_r)
    fwd_b, bwd_b = shift(own_f, 1), shift(own_b, -1)
    pair_a = relay_pair(x_a, size_a, "relay_a", pair_r)
    y_a = relay(pair_a)
    fwd_c, bwd_c = pl.pallas_call(
        lambda *refs: more_kernel(*cut_c, *refs),
        out_shape=(planes(size_c), planes(size_c)),
        in_specs=[vm, vm, hbm],
        out_specs=(vm, vm),
        compiler_params=params,
        cost_estimate=free,
        name="pack_c",
    )(v, scale, pair_a)
    fwd_c, bwd_c = shift(fwd_c, 1), shift(bwd_c, -1)
    inner, pay = pl.pallas_call(
        inner_kernel,
        out_shape=(works(nb), pay_shape),
        in_specs=[sm] + [vm] * 5,
        out_specs=(vm, vm),
        compiler_params=params,
        cost_estimate=free,
        name="inner",
    )(coupling_prev, v, scale, q, from_left, from_right)
    w_ab, pay, columns_f, columns_b = pl.pallas_call(
        lambda *refs: sum_kernel(((*cut_r, True), (*cut_a, True), (*cut_b, False)), 0, *refs),
        out_shape=(works(cut_b[1]), pay_shape, plane, plane),
        in_specs=[vm] * 12,
        out_specs=(vm,) * 4,
        compiler_params=params,
        cost_estimate=free,
        name="products",
    )(v, scale, inner, pay, x_r, y_r, x_a, y_a, fwd_b, bwd_b, fwd_b, bwd_b)
    w_c, pay = pl.pallas_call(
        lambda *refs: sum_kernel(((*cut_c, False),), cut_c[0], *refs),
        out_shape=(works(cut_c[1] - cut_c[0]), pay_shape),
        in_specs=[vm] * 9,
        out_specs=(vm, vm),
        compiler_params=params,
        cost_estimate=free,
        name="products_last",
    )(v, scale, inner, pay, fwd_c, bwd_c, columns_f, columns_b, w_ab)
    pay = jnp.broadcast_to(pay[None], (devices, 2, nt))
    pay = lax.all_to_all(pay, ("loop", "trans"), 0, 0)
    small = jax.ShapeDtypeStruct((nb, nb), f32)
    out, alpha, beta = pl.pallas_call(
        lambda *refs: last_kernel(count, *refs),
        out_shape=(works(nb), small, small),
        in_specs=[vm] * 4,
        out_specs=(hbm,) * 3,
        scratch_shapes=[
            VM((nb + nb * (nb + 1) // 2, 8, nt), f32),
            VM((nb, nc * nz, nt), f32),
            VM((nb, nb), f32),
            VM((nb, nb), f32),
            pltpu.SemaphoreType.DMA((6,)),
        ],
        compiler_params=params,
        cost_estimate=free,
        name="combine",
    )(pay, v, w_ab, w_c)
    return out.reshape(block_now.shape), alpha, beta


def solution(mesh):
    in_specs = (
        P(None, None, None, "loop", "trans"),
        P(None, None, None, "loop", "trans"),
        P(),
        P(None, "loop", "trans"),
        P(),
    )
    out_specs = (P(None, None, None, "loop", "trans"), P(), P())
    return jax.shard_map(local, mesh=mesh, in_specs=in_specs, out_specs=out_specs, check_vma=False)
```

```python
import jax
import jax.numpy as jnp
from jax import lax
from jax.experimental import pallas as pl
from jax.experimental.pallas import tpu as pltpu
from jax.sharding import PartitionSpec as P

VM = pltpu.VMEM
SM = pltpu.SMEM


def lane_ids(shape):
    return lax.broadcasted_iota(jnp.int32, shape, len(shape) - 1)


def row_ids(shape):
    return lax.broadcasted_iota(jnp.int32, shape, len(shape) - 2)


def roll_by(x, shift, axis):
    return pltpu.roll(x, shift % x.shape[axis], axis)


def cell_scale(mat, eps_ref):
    eps = jnp.full(mat.shape, eps_ref[0], jnp.float32)
    for level in range(1, eps_ref.shape[0]):
        eps = jnp.where(mat == level, eps_ref[level], eps)
    return 1.0 / jnp.sqrt(eps)


def z_next(x):
    n = x.shape[0]
    return jnp.where(row_ids(x.shape) == n - 1, 0.0, roll_by(x, -1, 0))


def z_prev(x):
    return jnp.where(row_ids(x.shape) == 0, 0.0, roll_by(x, 1, 0))


def forward_pair(uz, up, ut):
    lane = lane_ids(up.shape)
    up_next = jnp.where(lane == up.shape[1] - 1, 0.0, roll_by(up, -1, 1))
    return uz + (z_next(up) - up), ut + (up_next - up)


def even_trans():
    return lax.rem(lax.axis_index("trans"), 2) == 0


def odd_loop():
    return lax.rem(lax.axis_index("loop"), 2) == 1


def packed(v_ref, b, scale, fwd_ref, bwd_ref, at):
    nz = scale.shape[0]
    uz = v_ref[b, pl.ds(0, nz), :] * scale
    up = v_ref[b, pl.ds(nz, nz), :] * scale
    ut = v_ref[b, pl.ds(2 * nz, nz), :] * scale
    one, two = pl.ds(at * nz, nz), pl.ds((at + 1) * nz, nz)
    bwd_ref[one, :] = uz
    bwd_ref[two, :] = ut
    fwd_ref[one, :], fwd_ref[two, :] = forward_pair(uz, up, ut)


def first_kernel(cut_r, v_hbm, mat_hbm, eps_hbm, x_ref, scale_ref, v_ref, mat_ref, eps_ref, sems):
    copies = [
        pltpu.make_async_copy(eps_hbm, eps_ref, sems.at[0]),
        pltpu.make_async_copy(mat_hbm, mat_ref, sems.at[1]),
    ]
    for b in range(v_ref.shape[0]):
        copies.append(pltpu.make_async_copy(v_hbm.at[b], v_ref.at[b], sems.at[2 + b]))
    for copy in copies:
        copy.start()
    copies[0].wait()
    copies[1].wait()
    scale = cell_scale(mat_ref[...], eps_ref)
    scale_ref[...] = scale
    nz = scale.shape[0]
    for m, b in enumerate(range(*cut_r)):
        copies[2 + b].wait()
        for c in range(3):
            x_ref[pl.ds((3 * m + c) * nz, nz), :] = v_ref[b, pl.ds(c * nz, nz), :] * scale


def relay_kernel(nz, x_ref, after_f_ref, after_b_ref, y_ref):
    odd = odd_loop()
    count = x_ref.shape[0] // (3 * nz)

    def comps(m):
        return [x_ref[pl.ds((3 * m + c) * nz, nz), :] for c in range(3)]

    def store(m, pair):
        y_ref[pl.ds(2 * m * nz, nz), :] = pair[0]
        y_ref[pl.ds((2 * m + 1) * nz, nz), :] = pair[1]

    @pl.when(odd)
    def _():
        for m in range(count):
            store(m, comps(m)[::2])

    @pl.when(jnp.logical_not(odd))
    def _():
        for m in range(count):
            store(m, forward_pair(*comps(m)))


def edge_kernel(cut, v_ref, scale_ref, near_ref, far_ref, fwd_ref, bwd_ref):
    scale = scale_ref[...]
    nz = scale.shape[0]
    lane = lane_ids(scale.shape)
    right = jnp.zeros_like(scale)
    left = jnp.zeros_like(scale)
    for b in range(v_ref.shape[0]):
        for c in range(3):
            u = v_ref[b, pl.ds(c * nz, nz), :] * scale
            spot = v_ref.shape[0] * c + b
            right = jnp.where(lane == spot, roll_by(u, spot + 1, 1), right)
            left = jnp.where(lane == spot, roll_by(u, spot, 1), left)
    even = even_trans()
    near_ref[...] = jnp.where(even, right, left)
    far_ref[...] = jnp.where(even, left, right)
    for m, b in enumerate(range(*cut)):
        packed(v_ref, b, scale, fwd_ref, bwd_ref, 2 * m)


def turned(x):
    pad = jnp.zeros((x.shape[1] - x.shape[0], x.shape[1]), x.dtype)
    return jnp.concatenate([x, pad], axis=0).T


def corner_kernel(begin, end, v_ref, scale_ref, near_ref, far_ref, fwd_ref, bwd_ref, fr_ref, fl_ref):
    scale = scale_ref[...]
    for b in range(begin, end):
        packed(v_ref, b, scale, fwd_ref, bwd_ref, 2 * (b - begin))
    nb = v_ref.shape[0]
    even = even_trans()
    near, far = near_ref[...], far_ref[...]
    from_left, from_right = jnp.where(even, far, near), jnp.where(even, near, far)
    fr_ref[...] = from_left
    fl_ref[...] = from_right
    rows = pl.ds(2 * (end - begin) * scale.shape[0], nb)
    fwd_ref[rows, :] = turned(from_right)[nb : 2 * nb, :]
    bwd_ref[rows, :] = turned(from_left)[2 * nb : 3 * nb, :]


def more_kernel(begin, end, v_ref, scale_ref, fwd_a_ref, bwd_a_ref, fwd_ref, bwd_ref):
    scale = scale_ref[...]
    for b in range(begin, end):
        packed(v_ref, b, scale, fwd_ref, bwd_ref, 2 * (b - begin))


def merge(a, b, dist):
    low = (row_ids(a.shape) & dist) == 0
    other = jnp.where(low, b, a)
    swapped = roll_by(other, dist, 0)
    if 2 * dist != a.shape[0]:
        swapped = jnp.where(low, roll_by(other, -dist, 0), swapped)
    return jnp.where(low, a, b) + swapped


def add_products(pairs, steps, group, pays, unroll=8):
    shape = pays[0].shape
    lane, row = lane_ids(shape), row_ids(shape)
    zero = jnp.zeros(shape, jnp.float32)
    for first in range(0, len(pairs), group):
        part = pairs[first : first + group]

        def body(r, accs):
            rows = pl.ds(pl.multiple_of(r * 8, 8), 8)
            got = {}
            for left, j, right, b, _ in part:
                for ref, i in ((left, j), (right, b)):
                    if (id(ref), i) not in got:
                        got[(id(ref), i)] = ref[i, rows, :]
            return tuple(
                acc + got[(id(left), j)] * got[(id(right), b)]
                for acc, (left, j, right, b, _) in zip(accs, part)
            )

        accs = list(lax.fori_loop(0, steps, body, tuple(zero for _ in part), unroll=unroll))
        for at in range(0, len(part), 8):
            eight = accs[at : at + 8]
            eight = eight + [zero] * (8 - len(eight))
            four = [merge(eight[i], eight[i + 4], 4) for i in range(4)]
            two = [merge(four[i], four[i + 2], 2) for i in range(2)]
            sums = jnp.sum(merge(two[0], two[1], 1), axis=1, keepdims=True)
            for line in range(len(pays)):
                hit = None
                for i, pair in enumerate(part[at : at + 8]):
                    for spot in sorted(pair[4]):
                        if spot[0] == line:
                            here = (row == i) & (lane == spot[1])
                            hit = here if hit is None else hit | here
                if hit is not None:
                    pays[line] = pays[line] + jnp.where(hit, sums, 0.0)
    return pays


def store_pays(pay_ref, pays, before=None):
    for line, pay in enumerate(pays):
        total = jnp.sum(pay, axis=0, keepdims=True)
        if before is not None:
            total = total + before[line : line + 1, :]
        pay_ref[line : line + 1, :] = total


def inner_kernel(coup_ref, v_ref, scale_ref, q_ref, fr_ref, fl_ref, l_ref, pay_ref):
    nb = v_ref.shape[0]
    nz = scale_ref.shape[0]

    def body(b, carry):
        scale = scale_ref[...]
        lane = lane_ids(scale.shape)
        last = scale.shape[1] - 1
        uz = v_ref[b, pl.ds(0, nz), :] * scale
        up = v_ref[b, pl.ds(nz, nz), :] * scale
        ut = v_ref[b, pl.ds(2 * nz, nz), :] * scale

        def prev(u, c):
            edge = pltpu.roll(fr_ref[...], (last + 1 - (nb * c + b)) % (last + 1), 1)
            return jnp.where(lane == 0, edge, roll_by(u, 1, 1))

        def nxt(u, c):
            edge = pltpu.roll(fl_ref[...], last - (nb * c + b), 1)
            return jnp.where(lane == last, edge, roll_by(u, -1, 1))

        dt_ut = ut - prev(ut, 2)
        up_next = nxt(up, 1)
        uz_next = nxt(uz, 0)
        im_z = (z_next(up) - up) + (z_next(dt_ut) - dt_ut) + 4.0 * uz - uz_next - prev(uz, 0)
        im_p = 4.0 * up - z_next(up) - z_prev(up) - up_next - prev(up, 1) - (uz - z_prev(uz)) - dt_ut
        im_t = (
            (uz_next - z_prev(uz_next)) - (uz - z_prev(uz)) + (up_next - up)
            + 4.0 * ut - z_next(ut) - z_prev(ut)
        )
        for c, im in enumerate((im_z, im_p, im_t)):
            rows = pl.ds(c * nz, nz)
            out = im * scale
            for k in range(nb):
                out = out - coup_ref[b, k] * q_ref[k, rows, :]
            l_ref[b, rows, :] = out
        return carry

    lax.fori_loop(0, nb, body, 0)
    zero = jnp.zeros((8, v_ref.shape[2]), jnp.float32)
    pairs = [(v_ref, j, v_ref, b, {(1, nb * j + b), (1, nb * b + j)}) for b in range(nb) for j in range(b + 1)]
    store_pays(pay_ref, add_products(pairs, v_ref.shape[1] // 8, 36, [zero, zero]))


def sum_kernel(cuts, begin, v_ref, scale_ref, l_ref, pay_in_ref, *refs):
    nb = v_ref.shape[0]
    nz, nt = scale_ref.shape
    end = cuts[-1][1]
    halos = refs[: 2 * len(cuts)]
    corners = refs[2 * len(cuts) : 2 * len(cuts) + 2]
    if begin == 0:
        w_ref, pay_ref, columns_f_ref, columns_b_ref = refs[-4:]
        for corner, columns_ref in zip(corners, (columns_f_ref, columns_b_ref)):
            columns_ref[...] = turned(corner[pl.ds(corner.shape[0] - nb, nb), :])[:nz, :]
    else:
        columns_f_ref, columns_b_ref = corners
        old, w_ref, pay_ref = refs[-3:]
    columns_f, columns_b = columns_f_ref[...], columns_b_ref[...]
    scale = scale_ref[...]
    lane = lane_ids(scale.shape)
    odd = odd_loop()
    for i, (low, high, relayed) in enumerate(cuts):
        fwd_ref, bwd_ref = halos[2 * i : 2 * i + 2]

        for m in range(high - low):
            b = low + m
            one, two = pl.ds(2 * m * nz, nz), pl.ds((2 * m + 1) * nz, nz)
            if relayed:
                xz, xp, xt = (fwd_ref[pl.ds((3 * m + c) * nz, nz), :] for c in range(3))
                y0, y1 = bwd_ref[one, :], bwd_ref[two, :]
                f0, f1 = forward_pair(xz, xp, xt)
                za, tb = jnp.where(odd, f0, y0), jnp.where(odd, f1, y1)
                uz, ut = jnp.where(odd, y0, xz), jnp.where(odd, y1, xt)
            else:
                za, tb = fwd_ref[one, :], fwd_ref[two, :]
                uz, ut = bwd_ref[one, :], bwd_ref[two, :]
            edge_b = roll_by(columns_b, -b, 1)
            edge_f = roll_by(columns_f, nt - 1 - b, 1)
            ut_prev = jnp.where(lane == 0, edge_b, roll_by(ut, 1, 1))
            tb = tb + jnp.where(lane == nt - 1, edge_f, 0.0)
            to = b - begin
            w_ref[to, pl.ds(0, nz), :] = l_ref[b, pl.ds(0, nz), :] - scale * (za + uz)
            div = (uz - z_prev(uz)) + (ut - ut_prev)
            w_ref[to, pl.ds(nz, nz), :] = l_ref[b, pl.ds(nz, nz), :] + scale * div
            w_ref[to, pl.ds(2 * nz, nz), :] = l_ref[b, pl.ds(2 * nz, nz), :] - scale * (tb + ut)

    ws = [(old, b) for b in range(begin)] + [(w_ref, b - begin) for b in range(begin, end)]
    pairs = []
    for b in range(begin, end):
        pairs += [(v_ref, j, *ws[b], {(0, nb * j + b), (1, nb * nb + nb * b + j)}) for j in range(nb)]
        pairs += [(*ws[j], *ws[b], {(0, nb * nb + nb * j + b), (0, nb * nb + nb * b + j)}) for j in range(b + 1)]
    zero = jnp.zeros((8, nt), jnp.float32)
    store_pays(pay_ref, add_products(pairs, v_ref.shape[1] // 8, 42, [zero, zero]), pay_in_ref)


def lane_at(x, k):
    return jnp.broadcast_to(x[:, k : k + 1], x.shape)


def row_at(x, k):
    return jnp.broadcast_to(x[k : k + 1, :], x.shape)


def matrix_of(line, offset, nb):
    x = jnp.broadcast_to(line, (8, line.shape[1]))
    row = row_ids(x.shape)
    out = roll_by(x, -offset, 1)
    for i in range(1, nb):
        out = jnp.where(row == i, roll_by(x, -offset - nb * i, 1), out)
    return out


def last_kernel(count, pay_ref, v_ref, *refs):
    w_refs = refs[:-8]
    out_hbm, alpha_hbm, beta_hbm, coef_ref, out_ref, alpha_ref, beta_ref, sems = refs[-8:]
    nb = v_ref.shape[0]
    total = jnp.sum(pay_ref[...], axis=0)
    proj = matrix_of(total[0:1], 0, nb)
    ww = matrix_of(total[0:1], nb * nb, nb)
    vv = matrix_of(total[1:2], 0, nb)
    alpha = proj * (1.0 / count)
    alpha_t = matrix_of(total[1:2], nb * nb, nb) * (1.0 / count)
    alpha_ref[...] = alpha[:, :nb]
    copies = [pltpu.make_async_copy(alpha_ref, alpha_hbm, sems.at[0])]
    copies[0].start()
    lane = lane_ids(proj.shape)
    row = row_ids(proj.shape)
    cross = jnp.zeros_like(proj)
    half = jnp.zeros_like(proj)
    for j in range(nb):
        coef_ref[j] = lane_at(alpha_t, j)
        cross = cross + lane_at(alpha_t, j) * row_at(proj, j)
        half = half + lane_at(vv, j) * row_at(alpha, j)
    quad = jnp.zeros_like(proj)
    for k in range(nb):
        quad = quad + lane_at(alpha_t, k) * row_at(half, k)
    gram = ((ww - cross) + (quad - cross)) * (1.0 / count)
    ws = [(w, i) for w in w_refs for i in range(w.shape[0])]
    blocks = v_ref.shape[1] // 8
    mat = {}
    for i in range(nb):
        line = row_at(gram, i)
        for j in range(i + 1):
            mat[i, j] = lane_at(line, j)
    low, inv = {}, {}
    beta = jnp.zeros_like(proj)
    for k in range(nb):
        root = lax.rsqrt(mat[k, k])
        low[k, k] = mat[k, k] * root
        for i in range(k + 1, nb):
            low[i, k] = mat[i, k] * root
        for i in range(k + 1, nb):
            for j in range(k + 1, i + 1):
                mat[i, j] = mat[i, j] - low[i, k] * low[j, k]
        for i in range(k, nb):
            beta = jnp.where((row == k) & (lane == i), low[i, k], beta)
        inv[k, k] = root
        for j in range(k):
            acc = low[k, j] * inv[j, j]
            for q in range(j + 1, k):
                acc = acc + low[k, q] * inv[q, j]
            inv[k, j] = -(root * acc)
        for j in range(k + 1):
            coef_ref[nb + k * (k + 1) // 2 + j] = inv[k, j]
        for r in range(k * blocks // nb, (k + 1) * blocks // nb):
            rows = pl.ds(8 * r, 8)
            vs = [v_ref[j, rows, :] for j in range(nb)]
            for b, (w_ref, i) in enumerate(ws):
                acc = w_ref[i, rows, :]
                for j in range(nb):
                    acc = acc - coef_ref[j, pl.ds(b, 1), :] * vs[j]
                out_ref[b, rows, :] = acc
    beta_ref[...] = beta[:, :nb]
    copies.append(pltpu.make_async_copy(beta_ref, beta_hbm, sems.at[1]))
    copies[1].start()
    step = 16
    pieces = sems.shape[0] - 2
    length = v_ref.shape[1] // pieces
    for piece in range(pieces):
        base = piece * length

        def body(r, carry):
            rows = pl.ds(pl.multiple_of(base + r * step, step), step)
            xs = [out_ref[j, rows, :] for j in range(nb)]
            for b in range(nb):
                at = nb + b * (b + 1) // 2
                acc = coef_ref[at, pl.ds(0, 1), :] * xs[0]
                for j in range(1, b + 1):
                    acc = acc + coef_ref[at + j, pl.ds(0, 1), :] * xs[j]
                out_ref[b, rows, :] = acc
            return carry

        lax.fori_loop(0, length // step, body, 0, unroll=True)
        part = pl.ds(base, length)
        copy = pltpu.make_async_copy(out_ref.at[:, part, :], out_hbm.at[:, part, :], sems.at[2 + piece])
        copy.start()
        copies.append(copy)
    for copy in copies:
        copy.wait()


def shift(x, loop_by):
    count = lax.axis_size("loop")
    return lax.ppermute(x, "loop", [(i, (i + loop_by) % count) for i in range(count)])


def trans_swaps(near, far):
    count = lax.axis_size("trans")
    pairs = [(t, t + (-1 if t % 2 == 0 else 1)) for t in range(1, count - 1)]
    return lax.ppermute(near, "trans", [(t, t ^ 1) for t in range(count)]), lax.ppermute(far, "trans", pairs)


def swap(x):
    return lax.ppermute(x, "loop", [(i, i ^ 1) for i in range(lax.axis_size("loop"))])


def relay(x):
    count = lax.axis_size("loop")
    return lax.ppermute(x, "loop", [(i, (i + (-2 if i % 2 else 2)) % count) for i in range(count)])


def local(block_now, block_prev, coupling_prev, material, permittivity):
    nb, nc, nz, _, nt = block_now.shape
    f32 = jnp.float32
    devices = lax.axis_size("loop") * lax.axis_size("trans")
    count = float(nc * nz * nt * devices)
    v = block_now.reshape(nb, nc * nz, nt)
    q = block_prev.reshape(nb, nc * nz, nt)
    mat = material.reshape(nz, nt)
    vm, sm = pl.BlockSpec(memory_space=VM), pl.BlockSpec(memory_space=SM)
    hbm = pl.BlockSpec(memory_space=pltpu.HBM)
    params = pltpu.CompilerParams(vmem_limit_bytes=32 * 2**20)
    free = pl.CostEstimate(flops=0, bytes_accessed=0, transcendentals=0)
    plane = jax.ShapeDtypeStruct((nz, nt), f32)
    pay_shape = jax.ShapeDtypeStruct((2, nt), f32)
    assert lax.axis_size("loop") % 2 == 0 and lax.axis_size("trans") % 2 == 0
    marks = (0, nb // 2, nb * 3 // 4, nb - 1, nb)
    cut_r, cut_a, cut_b, cut_c = zip(marks[:-1], marks[1:])

    def planes(n, more=0):
        return jax.ShapeDtypeStruct((n * nz + more, nt), f32)

    def works(n):
        return jax.ShapeDtypeStruct((n, nc * nz, nt), f32)

    size_r, size_a, size_b, size_c = (2 * (c[1] - c[0]) for c in (cut_r, cut_a, cut_b, cut_c))
    x_r, scale = pl.pallas_call(
        lambda *refs: first_kernel(cut_r, *refs),
        out_shape=(planes(size_r * 3 // 2), plane),
        in_specs=[hbm] * 3,
        out_specs=(vm,) * 2,
        scratch_shapes=[
            VM((cut_r[1], nc * nz, nt), f32),
            VM((nz, nt), jnp.int32),
            SM(permittivity.shape, f32),
            pltpu.SemaphoreType.DMA((2 + cut_r[1],)),
        ],
        compiler_params=params,
        cost_estimate=free,
        name="first",
    )(*(pltpu.with_memory_space_constraint(x, pltpu.HBM) for x in (v, mat, permittivity)))
    x_r = swap(x_r)
    near, far, fwd_a, bwd_a = pl.pallas_call(
        lambda *refs: edge_kernel(cut_a, *refs),
        out_shape=(plane, plane, planes(size_a), planes(size_a)),
        in_specs=[vm, vm],
        out_specs=(vm,) * 4,
        compiler_params=params,
        cost_estimate=free,
        name="edges",
    )(v, scale)
    near, far = trans_swaps(near, far)
    fwd_a, bwd_a = shift(fwd_a, 1), shift(bwd_a, -1)
    own_f, own_b, from_left, from_right = pl.pallas_call(
        lambda *refs: corner_kernel(*cut_b, *refs),
        out_shape=(planes(size_b, nb), planes(size_b, nb), plane, plane),
        in_specs=[vm] * 4,
        out_specs=(vm,) * 4,
        compiler_params=params,
        cost_estimate=free,
        name="pack_b",
    )(v, scale, near, far)
    fwd_b, bwd_b = shift(own_f, 1), shift(own_b, -1)
    y_r = relay(
        pl.pallas_call(
            lambda *refs: relay_kernel(nz, *refs),
            out_shape=planes(size_r),
            in_specs=[vm, hbm, hbm],
            out_specs=vm,
            compiler_params=params,
            cost_estimate=free,
            name="relay",
        )(x_r, own_f, own_b)
    )
    fwd_c, bwd_c = pl.pallas_call(
        lambda *refs: more_kernel(*cut_c, *refs),
        out_shape=(planes(size_c), planes(size_c)),
        in_specs=[vm, vm, hbm, hbm],
        out_specs=(vm, vm),
        compiler_params=params,
        cost_estimate=free,
        name="pack_c",
    )(v, scale, fwd_a, bwd_a)
    fwd_c, bwd_c = shift(fwd_c, 1), shift(bwd_c, -1)
    inner, pay = pl.pallas_call(
        inner_kernel,
        out_shape=(works(nb), pay_shape),
        in_specs=[sm] + [vm] * 5,
        out_specs=(vm, vm),
        compiler_params=params,
        cost_estimate=free,
        name="inner",
    )(coupling_prev, v, scale, q, from_left, from_right)
    w_ab, pay, columns_f, columns_b = pl.pallas_call(
        lambda *refs: sum_kernel(((*cut_r, True), (*cut_a, False), (*cut_b, False)), 0, *refs),
        out_shape=(works(cut_b[1]), pay_shape, plane, plane),
        in_specs=[vm] * 12,
        out_specs=(vm,) * 4,
        compiler_params=params,
        cost_estimate=free,
        name="products",
    )(v, scale, inner, pay, x_r, y_r, fwd_a, bwd_a, fwd_b, bwd_b, fwd_b, bwd_b)
    w_c, pay = pl.pallas_call(
        lambda *refs: sum_kernel(((*cut_c, False),), cut_c[0], *refs),
        out_shape=(works(cut_c[1] - cut_c[0]), pay_shape),
        in_specs=[vm] * 9,
        out_specs=(vm, vm),
        compiler_params=params,
        cost_estimate=free,
        name="products_last",
    )(v, scale, inner, pay, fwd_c, bwd_c, columns_f, columns_b, w_ab)
    pay = jnp.broadcast_to(pay[None], (devices, 2, nt))
    pay = lax.all_to_all(pay, ("loop", "trans"), 0, 0)
    small = jax.ShapeDtypeStruct((nb, nb), f32)
    out, alpha, beta = pl.pallas_call(
        lambda *refs: last_kernel(count, *refs),
        out_shape=(works(nb), small, small),
        in_specs=[vm] * 4,
        out_specs=(hbm,) * 3,
        scratch_shapes=[
            VM((nb + nb * (nb + 1) // 2, 8, nt), f32),
            VM((nb, nc * nz, nt), f32),
            VM((nb, nb), f32),
            VM((nb, nb), f32),
            pltpu.SemaphoreType.DMA((6,)),
        ],
        compiler_params=params,
        cost_estimate=free,
        name="combine",
    )(pay, v, w_ab, w_c)
    return out.reshape(block_now.shape), alpha, beta


def solution(mesh):
    in_specs = (
        P(None, None, None, "loop", "trans"),
        P(None, None, None, "loop", "trans"),
        P(),
        P(None, "loop", "trans"),
        P(),
    )
    out_specs = (P(None, None, None, "loop", "trans"), P(), P())
    return jax.shard_map(local, mesh=mesh, in_specs=in_specs, out_specs=out_specs, check_vma=False)
```

```python
import jax
import jax.numpy as jnp
from jax import lax
from jax.experimental import pallas as pl
from jax.experimental.pallas import tpu as pltpu
from jax.sharding import PartitionSpec as P

VM = pltpu.VMEM
SM = pltpu.SMEM


def lane_ids(shape):
    return lax.broadcasted_iota(jnp.int32, shape, len(shape) - 1)


def row_ids(shape):
    return lax.broadcasted_iota(jnp.int32, shape, len(shape) - 2)


def roll_by(x, shift, axis):
    return pltpu.roll(x, shift % x.shape[axis], axis)


def cell_scale(mat, eps_ref):
    eps = jnp.full(mat.shape, eps_ref[0], jnp.float32)
    for level in range(1, eps_ref.shape[0]):
        eps = jnp.where(mat == level, eps_ref[level], eps)
    return 1.0 / jnp.sqrt(eps)


def z_next(x):
    n = x.shape[0]
    return jnp.where(row_ids(x.shape) == n - 1, 0.0, roll_by(x, -1, 0))


def z_prev(x):
    return jnp.where(row_ids(x.shape) == 0, 0.0, roll_by(x, 1, 0))


def forward_pair(uz, up, ut):
    lane = lane_ids(up.shape)
    up_next = jnp.where(lane == up.shape[1] - 1, 0.0, roll_by(up, -1, 1))
    return uz + (z_next(up) - up), ut + (up_next - up)


def even_trans():
    return lax.rem(lax.axis_index("trans"), 2) == 0


def odd_loop():
    return lax.rem(lax.axis_index("loop"), 2) == 1


def packed(v_ref, b, scale, fwd_ref, bwd_ref, at):
    nz = scale.shape[0]
    uz = v_ref[b, pl.ds(0, nz), :] * scale
    up = v_ref[b, pl.ds(nz, nz), :] * scale
    ut = v_ref[b, pl.ds(2 * nz, nz), :] * scale
    one, two = pl.ds(at * nz, nz), pl.ds((at + 1) * nz, nz)
    bwd_ref[one, :] = uz
    bwd_ref[two, :] = ut
    fwd_ref[one, :], fwd_ref[two, :] = forward_pair(uz, up, ut)


def first_kernel(cut_r, v_hbm, mat_hbm, eps_hbm, x_ref, scale_ref, v_ref, mat_ref, eps_ref, sems):
    copies = [
        pltpu.make_async_copy(eps_hbm, eps_ref, sems.at[0]),
        pltpu.make_async_copy(mat_hbm, mat_ref, sems.at[1]),
    ]
    for b in range(v_ref.shape[0]):
        copies.append(pltpu.make_async_copy(v_hbm.at[b], v_ref.at[b], sems.at[2 + b]))
    for copy in copies:
        copy.start()
    copies[0].wait()
    copies[1].wait()
    scale = cell_scale(mat_ref[...], eps_ref)
    scale_ref[...] = scale
    nz = scale.shape[0]
    for m, b in enumerate(range(*cut_r)):
        copies[2 + b].wait()
        for c in range(3):
            x_ref[pl.ds((3 * m + c) * nz, nz), :] = v_ref[b, pl.ds(c * nz, nz), :] * scale


def relay_kernel(nz, x_ref, after_f_ref, after_b_ref, y_ref):
    odd = odd_loop()
    count = x_ref.shape[0] // (3 * nz)

    def comps(m):
        return [x_ref[pl.ds((3 * m + c) * nz, nz), :] for c in range(3)]

    def store(m, pair):
        y_ref[pl.ds(2 * m * nz, nz), :] = pair[0]
        y_ref[pl.ds((2 * m + 1) * nz, nz), :] = pair[1]

    @pl.when(odd)
    def _():
        for m in range(count):
            store(m, comps(m)[::2])

    @pl.when(jnp.logical_not(odd))
    def _():
        for m in range(count):
            store(m, forward_pair(*comps(m)))


def edge_kernel(cut, v_ref, scale_ref, near_ref, far_ref, fwd_ref, bwd_ref):
    scale = scale_ref[...]
    nz = scale.shape[0]
    lane = lane_ids(scale.shape)
    right = jnp.zeros_like(scale)
    left = jnp.zeros_like(scale)
    for b in range(v_ref.shape[0]):
        for c in range(3):
            u = v_ref[b, pl.ds(c * nz, nz), :] * scale
            spot = v_ref.shape[0] * c + b
            right = jnp.where(lane == spot, roll_by(u, spot + 1, 1), right)
            left = jnp.where(lane == spot, roll_by(u, spot, 1), left)
    even = even_trans()
    near_ref[...] = jnp.where(even, right, left)
    far_ref[...] = jnp.where(even, left, right)
    for m, b in enumerate(range(*cut)):
        packed(v_ref, b, scale, fwd_ref, bwd_ref, 2 * m)


def turned(x):
    pad = jnp.zeros((x.shape[1] - x.shape[0], x.shape[1]), x.dtype)
    return jnp.concatenate([x, pad], axis=0).T


def corner_kernel(begin, end, v_ref, scale_ref, near_ref, far_ref, fwd_ref, bwd_ref, fr_ref, fl_ref):
    scale = scale_ref[...]
    for b in range(begin, end):
        packed(v_ref, b, scale, fwd_ref, bwd_ref, 2 * (b - begin))
    nb = v_ref.shape[0]
    even = even_trans()
    near, far = near_ref[...], far_ref[...]
    from_left, from_right = jnp.where(even, far, near), jnp.where(even, near, far)
    fr_ref[...] = from_left
    fl_ref[...] = from_right
    rows = pl.ds(2 * (end - begin) * scale.shape[0], nb)
    fwd_ref[rows, :] = turned(from_right)[nb : 2 * nb, :]
    bwd_ref[rows, :] = turned(from_left)[2 * nb : 3 * nb, :]


def more_kernel(begin, end, v_ref, scale_ref, fwd_a_ref, bwd_a_ref, fwd_ref, bwd_ref):
    scale = scale_ref[...]
    for b in range(begin, end):
        packed(v_ref, b, scale, fwd_ref, bwd_ref, 2 * (b - begin))


def merge(a, b, dist):
    low = (row_ids(a.shape) & dist) == 0
    other = jnp.where(low, b, a)
    swapped = roll_by(other, dist, 0)
    if 2 * dist != a.shape[0]:
        swapped = jnp.where(low, roll_by(other, -dist, 0), swapped)
    return jnp.where(low, a, b) + swapped


def add_products(pairs, steps, group, pays, unroll=24):
    shape = pays[0].shape
    lane, row = lane_ids(shape), row_ids(shape)
    zero = jnp.zeros(shape, jnp.float32)
    for first in range(0, len(pairs), group):
        part = pairs[first : first + group]

        def body(r, accs):
            rows = pl.ds(pl.multiple_of(r * 8, 8), 8)
            got = {}
            for left, j, right, b, _ in part:
                for ref, i in ((left, j), (right, b)):
                    if (id(ref), i) not in got:
                        got[(id(ref), i)] = ref[i, rows, :]
            return tuple(
                acc + got[(id(left), j)] * got[(id(right), b)]
                for acc, (left, j, right, b, _) in zip(accs, part)
            )

        accs = list(lax.fori_loop(0, steps, body, tuple(zero for _ in part), unroll=unroll))
        for at in range(0, len(part), 8):
            eight = accs[at : at + 8]
            eight = eight + [zero] * (8 - len(eight))
            four = [merge(eight[i], eight[i + 4], 4) for i in range(4)]
            two = [merge(four[i], four[i + 2], 2) for i in range(2)]
            sums = jnp.sum(merge(two[0], two[1], 1), axis=1, keepdims=True)
            for line in range(len(pays)):
                hit = None
                for i, pair in enumerate(part[at : at + 8]):
                    for spot in sorted(pair[4]):
                        if spot[0] == line:
                            here = (row == i) & (lane == spot[1])
                            hit = here if hit is None else hit | here
                if hit is not None:
                    pays[line] = pays[line] + jnp.where(hit, sums, 0.0)
    return pays


def store_pays(pay_ref, pays, before=None):
    for line, pay in enumerate(pays):
        total = jnp.sum(pay, axis=0, keepdims=True)
        if before is not None:
            total = total + before[line : line + 1, :]
        pay_ref[line : line + 1, :] = total


def inner_kernel(coup_ref, v_ref, scale_ref, q_ref, fr_ref, fl_ref, l_ref, pay_ref):
    nb = v_ref.shape[0]
    nz = scale_ref.shape[0]

    def body(b, carry):
        scale = scale_ref[...]
        lane = lane_ids(scale.shape)
        last = scale.shape[1] - 1
        uz = v_ref[b, pl.ds(0, nz), :] * scale
        up = v_ref[b, pl.ds(nz, nz), :] * scale
        ut = v_ref[b, pl.ds(2 * nz, nz), :] * scale

        def prev(u, c):
            edge = pltpu.roll(fr_ref[...], (last + 1 - (nb * c + b)) % (last + 1), 1)
            return jnp.where(lane == 0, edge, roll_by(u, 1, 1))

        def nxt(u, c):
            edge = pltpu.roll(fl_ref[...], last - (nb * c + b), 1)
            return jnp.where(lane == last, edge, roll_by(u, -1, 1))

        dt_ut = ut - prev(ut, 2)
        up_next = nxt(up, 1)
        uz_next = nxt(uz, 0)
        im_z = (z_next(up) - up) + (z_next(dt_ut) - dt_ut) + 4.0 * uz - uz_next - prev(uz, 0)
        im_p = 4.0 * up - z_next(up) - z_prev(up) - up_next - prev(up, 1) - (uz - z_prev(uz)) - dt_ut
        im_t = (
            (uz_next - z_prev(uz_next)) - (uz - z_prev(uz)) + (up_next - up)
            + 4.0 * ut - z_next(ut) - z_prev(ut)
        )
        for c, im in enumerate((im_z, im_p, im_t)):
            rows = pl.ds(c * nz, nz)
            out = im * scale
            for k in range(nb):
                out = out - coup_ref[b, k] * q_ref[k, rows, :]
            l_ref[b, rows, :] = out
        return carry

    lax.fori_loop(0, nb, body, 0)
    zero = jnp.zeros((8, v_ref.shape[2]), jnp.float32)
    pairs = [(v_ref, j, v_ref, b, {(1, nb * j + b), (1, nb * b + j)}) for b in range(nb) for j in range(b + 1)]
    store_pays(pay_ref, add_products(pairs, v_ref.shape[1] // 8, 36, [zero, zero]))


def sum_kernel(cuts, begin, v_ref, scale_ref, l_ref, pay_in_ref, *refs):
    nb = v_ref.shape[0]
    nz, nt = scale_ref.shape
    end = cuts[-1][1]
    halos = refs[: 2 * len(cuts)]
    corners = refs[2 * len(cuts) : 2 * len(cuts) + 2]
    if begin == 0:
        w_ref, pay_ref, columns_f_ref, columns_b_ref = refs[-4:]
        for corner, columns_ref in zip(corners, (columns_f_ref, columns_b_ref)):
            columns_ref[...] = turned(corner[pl.ds(corner.shape[0] - nb, nb), :])[:nz, :]
    else:
        columns_f_ref, columns_b_ref = corners
        old, w_ref, pay_ref = refs[-3:]
    columns_f, columns_b = columns_f_ref[...], columns_b_ref[...]
    scale = scale_ref[...]
    lane = lane_ids(scale.shape)
    odd = odd_loop()
    for i, (low, high, relayed) in enumerate(cuts):
        fwd_ref, bwd_ref = halos[2 * i : 2 * i + 2]

        for m in range(high - low):
            b = low + m
            one, two = pl.ds(2 * m * nz, nz), pl.ds((2 * m + 1) * nz, nz)
            if relayed:
                xz, xp, xt = (fwd_ref[pl.ds((3 * m + c) * nz, nz), :] for c in range(3))
                y0, y1 = bwd_ref[one, :], bwd_ref[two, :]
                f0, f1 = forward_pair(xz, xp, xt)
                za, tb = jnp.where(odd, f0, y0), jnp.where(odd, f1, y1)
                uz, ut = jnp.where(odd, y0, xz), jnp.where(odd, y1, xt)
            else:
                za, tb = fwd_ref[one, :], fwd_ref[two, :]
                uz, ut = bwd_ref[one, :], bwd_ref[two, :]
            edge_b = roll_by(columns_b, -b, 1)
            edge_f = roll_by(columns_f, nt - 1 - b, 1)
            ut_prev = jnp.where(lane == 0, edge_b, roll_by(ut, 1, 1))
            tb = tb + jnp.where(lane == nt - 1, edge_f, 0.0)
            to = b - begin
            w_ref[to, pl.ds(0, nz), :] = l_ref[b, pl.ds(0, nz), :] - scale * (za + uz)
            div = (uz - z_prev(uz)) + (ut - ut_prev)
            w_ref[to, pl.ds(nz, nz), :] = l_ref[b, pl.ds(nz, nz), :] + scale * div
            w_ref[to, pl.ds(2 * nz, nz), :] = l_ref[b, pl.ds(2 * nz, nz), :] - scale * (tb + ut)

    ws = [(old, b) for b in range(begin)] + [(w_ref, b - begin) for b in range(begin, end)]
    pairs = []
    for b in range(begin, end):
        pairs += [(v_ref, j, *ws[b], {(0, nb * j + b), (1, nb * nb + nb * b + j)}) for j in range(nb)]
        pairs += [(*ws[j], *ws[b], {(0, nb * nb + nb * j + b), (0, nb * nb + nb * b + j)}) for j in range(b + 1)]
    zero = jnp.zeros((8, nt), jnp.float32)
    store_pays(pay_ref, add_products(pairs, v_ref.shape[1] // 8, 42, [zero, zero]), pay_in_ref)


def lane_at(x, k):
    return jnp.broadcast_to(x[:, k : k + 1], x.shape)


def row_at(x, k):
    return jnp.broadcast_to(x[k : k + 1, :], x.shape)


def matrix_of(line, offset, nb):
    x = jnp.broadcast_to(line, (8, line.shape[1]))
    row = row_ids(x.shape)
    out = roll_by(x, -offset, 1)
    for i in range(1, nb):
        out = jnp.where(row == i, roll_by(x, -offset - nb * i, 1), out)
    return out


def last_kernel(count, pay_ref, v_ref, *refs):
    w_refs = refs[:-8]
    out_hbm, alpha_hbm, beta_hbm, coef_ref, out_ref, alpha_ref, beta_ref, sems = refs[-8:]
    nb = v_ref.shape[0]
    total = jnp.sum(pay_ref[...], axis=0)
    proj = matrix_of(total[0:1], 0, nb)
    ww = matrix_of(total[0:1], nb * nb, nb)
    vv = matrix_of(total[1:2], 0, nb)
    alpha = proj * (1.0 / count)
    alpha_t = matrix_of(total[1:2], nb * nb, nb) * (1.0 / count)
    alpha_ref[...] = alpha[:, :nb]
    copies = [pltpu.make_async_copy(alpha_ref, alpha_hbm, sems.at[0])]
    copies[0].start()
    lane = lane_ids(proj.shape)
    row = row_ids(proj.shape)
    cross = jnp.zeros_like(proj)
    half = jnp.zeros_like(proj)
    for j in range(nb):
        coef_ref[j] = lane_at(alpha_t, j)
        cross = cross + lane_at(alpha_t, j) * row_at(proj, j)
        half = half + lane_at(vv, j) * row_at(alpha, j)
    quad = jnp.zeros_like(proj)
    for k in range(nb):
        quad = quad + lane_at(alpha_t, k) * row_at(half, k)
    gram = ((ww - cross) + (quad - cross)) * (1.0 / count)
    ws = [(w, i) for w in w_refs for i in range(w.shape[0])]
    blocks = v_ref.shape[1] // 8
    mat = {}
    for i in range(nb):
        line = row_at(gram, i)
        for j in range(i + 1):
            mat[i, j] = lane_at(line, j)
    low, inv = {}, {}
    beta = jnp.zeros_like(proj)
    for k in range(nb):
        root = lax.rsqrt(mat[k, k])
        low[k, k] = mat[k, k] * root
        for i in range(k + 1, nb):
            low[i, k] = mat[i, k] * root
        for i in range(k + 1, nb):
            for j in range(k + 1, i + 1):
                mat[i, j] = mat[i, j] - low[i, k] * low[j, k]
        for i in range(k, nb):
            beta = jnp.where((row == k) & (lane == i), low[i, k], beta)
        inv[k, k] = root
        for j in range(k):
            acc = low[k, j] * inv[j, j]
            for q in range(j + 1, k):
                acc = acc + low[k, q] * inv[q, j]
            inv[k, j] = -(root * acc)
        for j in range(k + 1):
            coef_ref[nb + k * (k + 1) // 2 + j] = inv[k, j]
        for r in range(k * blocks // nb, (k + 1) * blocks // nb):
            rows = pl.ds(8 * r, 8)
            vs = [v_ref[j, rows, :] for j in range(nb)]
            for b, (w_ref, i) in enumerate(ws):
                acc = w_ref[i, rows, :]
                for j in range(nb):
                    acc = acc - coef_ref[j, pl.ds(b, 1), :] * vs[j]
                out_ref[b, rows, :] = acc
    beta_ref[...] = beta[:, :nb]
    copies.append(pltpu.make_async_copy(beta_ref, beta_hbm, sems.at[1]))
    copies[1].start()
    step = 16
    pieces = sems.shape[0] - 2
    length = v_ref.shape[1] // pieces
    for piece in range(pieces):
        base = piece * length

        def body(r, carry):
            rows = pl.ds(pl.multiple_of(base + r * step, step), step)
            xs = [out_ref[j, rows, :] for j in range(nb)]
            for b in range(nb):
                at = nb + b * (b + 1) // 2
                acc = coef_ref[at, pl.ds(0, 1), :] * xs[0]
                for j in range(1, b + 1):
                    acc = acc + coef_ref[at + j, pl.ds(0, 1), :] * xs[j]
                out_ref[b, rows, :] = acc
            return carry

        lax.fori_loop(0, length // step, body, 0, unroll=True)
        part = pl.ds(base, length)
        copy = pltpu.make_async_copy(out_ref.at[:, part, :], out_hbm.at[:, part, :], sems.at[2 + piece])
        copy.start()
        copies.append(copy)
    for copy in copies:
        copy.wait()


def shift(x, loop_by):
    count = lax.axis_size("loop")
    return lax.ppermute(x, "loop", [(i, (i + loop_by) % count) for i in range(count)])


def trans_swaps(near, far):
    count = lax.axis_size("trans")
    pairs = [(t, t + (-1 if t % 2 == 0 else 1)) for t in range(1, count - 1)]
    return lax.ppermute(near, "trans", [(t, t ^ 1) for t in range(count)]), lax.ppermute(far, "trans", pairs)


def swap(x):
    return lax.ppermute(x, "loop", [(i, i ^ 1) for i in range(lax.axis_size("loop"))])


def relay(x):
    count = lax.axis_size("loop")
    return lax.ppermute(x, "loop", [(i, (i + (-2 if i % 2 else 2)) % count) for i in range(count)])


def local(block_now, block_prev, coupling_prev, material, permittivity):
    nb, nc, nz, _, nt = block_now.shape
    f32 = jnp.float32
    devices = lax.axis_size("loop") * lax.axis_size("trans")
    count = float(nc * nz * nt * devices)
    v = block_now.reshape(nb, nc * nz, nt)
    q = block_prev.reshape(nb, nc * nz, nt)
    mat = material.reshape(nz, nt)
    vm, sm = pl.BlockSpec(memory_space=VM), pl.BlockSpec(memory_space=SM)
    hbm = pl.BlockSpec(memory_space=pltpu.HBM)
    params = pltpu.CompilerParams(vmem_limit_bytes=32 * 2**20)
    free = pl.CostEstimate(flops=0, bytes_accessed=0, transcendentals=0)
    plane = jax.ShapeDtypeStruct((nz, nt), f32)
    pay_shape = jax.ShapeDtypeStruct((2, nt), f32)
    assert lax.axis_size("loop") % 2 == 0 and lax.axis_size("trans") % 2 == 0
    marks = (0, nb * 3 // 8, nb * 5 // 8, nb - 1, nb)
    cut_r, cut_a, cut_b, cut_c = zip(marks[:-1], marks[1:])

    def planes(n, more=0):
        return jax.ShapeDtypeStruct((n * nz + more, nt), f32)

    def works(n):
        return jax.ShapeDtypeStruct((n, nc * nz, nt), f32)

    size_r, size_a, size_b, size_c = (2 * (c[1] - c[0]) for c in (cut_r, cut_a, cut_b, cut_c))
    x_r, scale = pl.pallas_call(
        lambda *refs: first_kernel(cut_r, *refs),
        out_shape=(planes(size_r * 3 // 2), plane),
        in_specs=[hbm] * 3,
        out_specs=(vm,) * 2,
        scratch_shapes=[
            VM((cut_r[1], nc * nz, nt), f32),
            VM((nz, nt), jnp.int32),
            SM(permittivity.shape, f32),
            pltpu.SemaphoreType.DMA((2 + cut_r[1],)),
        ],
        compiler_params=params,
        cost_estimate=free,
        name="first",
    )(*(pltpu.with_memory_space_constraint(x, pltpu.HBM) for x in (v, mat, permittivity)))
    x_r = swap(x_r)
    near, far, fwd_a, bwd_a = pl.pallas_call(
        lambda *refs: edge_kernel(cut_a, *refs),
        out_shape=(plane, plane, planes(size_a), planes(size_a)),
        in_specs=[vm, vm],
        out_specs=(vm,) * 4,
        compiler_params=params,
        cost_estimate=free,
        name="edges",
    )(v, scale)
    near, far = trans_swaps(near, far)
    fwd_a, bwd_a = shift(fwd_a, 1), shift(bwd_a, -1)
    own_f, own_b, from_left, from_right = pl.pallas_call(
        lambda *refs: corner_kernel(*cut_b, *refs),
        out_shape=(planes(size_b, nb), planes(size_b, nb), plane, plane),
        in_specs=[vm] * 4,
        out_specs=(vm,) * 4,
        compiler_params=params,
        cost_estimate=free,
        name="pack_b",
    )(v, scale, near, far)
    fwd_b, bwd_b = shift(own_f, 1), shift(own_b, -1)
    y_r = relay(
        pl.pallas_call(
            lambda *refs: relay_kernel(nz, *refs),
            out_shape=planes(size_r),
            in_specs=[vm, hbm, hbm],
            out_specs=vm,
            compiler_params=params,
            cost_estimate=free,
            name="relay",
        )(x_r, own_f, own_b)
    )
    fwd_c, bwd_c = pl.pallas_call(
        lambda *refs: more_kernel(*cut_c, *refs),
        out_shape=(planes(size_c), planes(size_c)),
        in_specs=[vm, vm, hbm, hbm],
        out_specs=(vm, vm),
        compiler_params=params,
        cost_estimate=free,
        name="pack_c",
    )(v, scale, fwd_a, bwd_a)
    fwd_c, bwd_c = shift(fwd_c, 1), shift(bwd_c, -1)
    inner, pay = pl.pallas_call(
        inner_kernel,
        out_shape=(works(nb), pay_shape),
        in_specs=[sm] + [vm] * 5,
        out_specs=(vm, vm),
        compiler_params=params,
        cost_estimate=free,
        name="inner",
    )(coupling_prev, v, scale, q, from_left, from_right)
    w_ab, pay, columns_f, columns_b = pl.pallas_call(
        lambda *refs: sum_kernel(((*cut_r, True), (*cut_a, False), (*cut_b, False)), 0, *refs),
        out_shape=(works(cut_b[1]), pay_shape, plane, plane),
        in_specs=[vm] * 12,
        out_specs=(vm,) * 4,
        compiler_params=params,
        cost_estimate=free,
        name="products",
    )(v, scale, inner, pay, x_r, y_r, fwd_a, bwd_a, fwd_b, bwd_b, fwd_b, bwd_b)
    w_c, pay = pl.pallas_call(
        lambda *refs: sum_kernel(((*cut_c, False),), cut_c[0], *refs),
        out_shape=(works(cut_c[1] - cut_c[0]), pay_shape),
        in_specs=[vm] * 9,
        out_specs=(vm, vm),
        compiler_params=params,
        cost_estimate=free,
        name="products_last",
    )(v, scale, inner, pay, fwd_c, bwd_c, columns_f, columns_b, w_ab)
    pay = jnp.broadcast_to(pay[None], (devices, 2, nt))
    pay = lax.all_to_all(pay, ("loop", "trans"), 0, 0)
    small = jax.ShapeDtypeStruct((nb, nb), f32)
    out, alpha, beta = pl.pallas_call(
        lambda *refs: last_kernel(count, *refs),
        out_shape=(works(nb), small, small),
        in_specs=[vm] * 4,
        out_specs=(hbm,) * 3,
        scratch_shapes=[
            VM((nb + nb * (nb + 1) // 2, 8, nt), f32),
            VM((nb, nc * nz, nt), f32),
            VM((nb, nb), f32),
            VM((nb, nb), f32),
            pltpu.SemaphoreType.DMA((6,)),
        ],
        compiler_params=params,
        cost_estimate=free,
        name="combine",
    )(pay, v, w_ab, w_c)
    return out.reshape(block_now.shape), alpha, beta


def solution(mesh):
    in_specs = (
        P(None, None, None, "loop", "trans"),
        P(None, None, None, "loop", "trans"),
        P(),
        P(None, "loop", "trans"),
        P(),
    )
    out_specs = (P(None, None, None, "loop", "trans"), P(), P())
    return jax.shard_map(local, mesh=mesh, in_specs=in_specs, out_specs=out_specs, check_vma=False)
```
